256 devices in a mesh: dp: 16 (over z_lo, x), col: 16 (over z_hi, y, core).
Axes of the slice: x: 4, y: 4, z: 8 (z_hi: 2, z_lo: 4; z = z_hi * 4 + z_lo), core: 2. Of those that a mesh axis runs over, the one named last changes fastest.
Arguments:
- latent: bfloat16 [32768, 512], P('dp'), may hold values from -6 to 6
- adapter_down_matrix: bfloat16 [64, 512], replicated, may hold values from -0.25 to 0.25
- output_gradient_rows: bfloat16 [32768, 32768], P('dp', 'col'), may hold values from -40 to 40
- output_sketch_factor: bfloat16 [32768, 128], P('col'), may hold values from -0.03125 to 0.03125
- rank_sketch_factor: bfloat16 [64, 64], replicated, may hold values from -0.75 to 0.75
- token_example_index: int32 [32768], P('dp'), may hold values from 0 to 127, as said below
- validation_sketches: float32 [256, 8192], P('dp', 'col'), may hold values from -6 to 6
Outputs:
- scores: float32 [128, 256], P('dp')
The draws below stay inside these ranges and needn't reach their ends.
Inputs may be any that keep to these rules, and one draw needn't show every extreme that they name: `token_example_index`: Nondecreasing. The tokens of index i of dp carry ids from i * 8 - 1 (never below 0) to (i + 1) * 8 - 1, and every id of i's own range starts on index i; an example's tokens lie on its own index and possibly the next one.
All inputs are finite; a program needn't handle non-finite values.
Results may differ from the reference program's by a relative error of at most 0.007.
Values sent between devices are 32-bit elements; how exact they have to be, the bound alone decides.
A program may use at most 64 MiB of HBM per device.

```python
import math
import jax
import jax.numpy as jnp
from jax import lax

LATENT_WIDTH = 512
DOUT = 32768
ADAPTER_RANK = 64
PA = 128
PB = 64
FEAT = 8192
NVAL = 256
EX_DEV = 8
EX_LEN = 256
TOK_DEV = 2048
TOKENS = 32768
N_DP = 16


def draw_output_gradient_rows(key, part):
    key = jax.random.fold_in(key, 5)
    column_scale = 3.0 ** (jnp.arange(DOUT, dtype=jnp.float32) / DOUT)
    values = jnp.clip(jax.random.normal(key, (TOKENS, DOUT), jnp.float32), -6.0, 6.0)
    return (values * column_scale[None, :]).astype(jnp.bfloat16)


def draw_token_example_index(key, part):
    key = jax.random.fold_in(key, 11)
    offsets = jax.random.randint(key, (N_DP, EX_DEV), 1, EX_LEN // 2 + 1)
    first_cell = (jnp.arange(N_DP)[:, None] == 0) & (jnp.arange(EX_DEV)[None, :] == 0)
    offsets = jnp.where(first_cell, 0, offsets)
    starts = jnp.arange(EX_DEV, dtype=jnp.int32)[None, :] * EX_LEN + offsets
    position = jnp.arange(TOK_DEV, dtype=jnp.int32)
    counted = jnp.sum((position[None, :, None] >= starts[:, None, :]).astype(jnp.int32), axis=2)
    result = jnp.arange(N_DP, dtype=jnp.int32)[:, None] * EX_DEV + counted - 1
    return result.reshape(-1).astype(jnp.int32)


def levels(key, shape, cuts, least, largest):
    factor_of = 1.0
    for axis_at, shards_of in cuts:
        draws = jax.random.uniform(jax.random.fold_in(jax.random.fold_in(key, 6), axis_at), (shards_of,), jnp.float32, least / len(cuts), largest / len(cuts))
        factor_of = factor_of * jnp.repeat(jnp.exp(draws), shape[axis_at] // shards_of).reshape((-1,) + (1,) * (len(shape) - 1 - axis_at))
    return factor_of


def normal_values(own_key, extent, scale, limit, cuts=(), kind=jnp.bfloat16):
    values = scale * jax.random.normal(own_key, extent, jnp.float32)
    if cuts:
        values = values * levels(own_key, extent, cuts, -0.22, 0.18)
    return jnp.clip(values, -limit, limit).astype(kind)


def setup_inputs(seed: int = 0) -> dict:
    arg_keys = jax.random.split(jax.random.key(seed), 8)
    latent = normal_values(arg_keys[0], (TOKENS, LATENT_WIDTH), 1.0, 6.0, ((0, 16),))
    adapter_down_matrix = normal_values(arg_keys[1], (ADAPTER_RANK, LATENT_WIDTH), LATENT_WIDTH ** -0.5, 0.25)
    output_gradient_rows = draw_output_gradient_rows(jax.random.fold_in(arg_keys[7], 71), 0)
    output_sketch_factor = normal_values(arg_keys[3], (DOUT, PA), DOUT ** -0.5, 0.03125, ((0, 16),))
    rank_sketch_factor = normal_values(arg_keys[4], (ADAPTER_RANK, PB), ADAPTER_RANK ** -0.5, 0.75)
    token_example_index = draw_token_example_index(jax.random.fold_in(arg_keys[7], 71), 0)
    validation_sketches = normal_values(arg_keys[6], (NVAL, FEAT), 1.0, 6.0, ((0, 16), (1, 16)), jnp.float32)
    return dict(latent=latent, adapter_down_matrix=adapter_down_matrix, output_gradient_rows=output_gradient_rows, output_sketch_factor=output_sketch_factor, rank_sketch_factor=rank_sketch_factor, token_example_index=token_example_index, validation_sketches=validation_sketches)


epsilon = 1e-06

def reference(latent, adapter_down_matrix, output_gradient_rows, output_sketch_factor, rank_sketch_factor, token_example_index, validation_sketches):
    hidden_width = lax.dot_general(latent, adapter_down_matrix, (((1,), (1,)), ((), ())), preferred_element_type=jnp.float32).astype(jnp.bfloat16)
    rank_side = jnp.dot(hidden_width, rank_sketch_factor, preferred_element_type=jnp.float32).astype(jnp.bfloat16)
    grad_blocks = output_gradient_rows.reshape(N_DP, TOK_DEV, DOUT)

    def project(grad_block):
        return jnp.dot(grad_block, output_sketch_factor, preferred_element_type=jnp.float32)
    out_side = lax.map(project, grad_blocks)
    side_blocks = rank_side.reshape(N_DP, TOK_DEV, PB)
    seg_blocks = token_example_index.reshape(N_DP, TOK_DEV)

    def accumulate(running, pieces):
        out_block, side_block, seg_block = pieces
        outers = out_block.astype(jnp.float32)[:, :, None] * side_block.astype(jnp.float32)[:, None, :]
        outers = outers.reshape(TOK_DEV, PA * PB)
        summed = jax.ops.segment_sum(outers, seg_block.astype(jnp.int32), num_segments=EX_DEV * N_DP)
        return (running + summed, None)
    start_total = jnp.zeros((EX_DEV * N_DP, PA * PB), jnp.float32)
    grad_proj, _ = lax.scan(accumulate, start_total, (out_side, side_blocks, seg_blocks))
    dots = lax.dot_general(grad_proj, validation_sketches, (((1,), (1,)), ((), ())), precision=lax.Precision.HIGHEST, preferred_element_type=jnp.float32)
    own_square = lax.optimization_barrier(jnp.sum(grad_proj * grad_proj, axis=1))
    val_square = lax.optimization_barrier(jnp.sum(validation_sketches * validation_sketches, axis=1))
    scale = math.sqrt(PA * PB)
    return scale * dots * lax.rsqrt(own_square + epsilon)[:, None] * lax.rsqrt(val_square + epsilon)[None, :]
```

```python
import functools
import math

import jax
import jax.numpy as jnp
from jax import lax
from jax.experimental import pallas as pl
from jax.experimental.pallas import tpu as pltpu
from jax.sharding import PartitionSpec as P

PA = 128
PB = 64
EX_DEV = 8
MESH = pl.DeviceIdType.MESH

epsilon = 1e-06

BF = jnp.bfloat16
F32 = jnp.float32

CHUNK = 512
OWN = EX_DEV * PB
ROWS = OWN + 2 * PB


def nt(x, y):
    return lax.dot_general(x, y, (((1,), (1,)), ((), ())), preferred_element_type=F32)


def kernel(
    lat_h, down_h, grad_h, sketch_h, rank_h, seg_h, val_h, out_ref,
    lat, down, grad, sketch, rank, seg, masked, gp, gt,
    r0, a0, r1, a1, r2, r3, vg, fin, rz, fb,
    local_sem, lat_sem, grad_sem, vown_sem,
    s0_send, s0_recv, s1_send, s1_recv, s2_send, s2_recv, s3_send, s3_recv,
    vz_send, vz_recv, vx_send, vx_recv, fz_send, fz_recv, fb_send, fb_recv,
):
    steps = grad.shape[0]
    i = lax.axis_index("dp")
    c = lax.axis_index("col")
    zl, x = i // 4, i % 4
    zh, y, core = c // 8, (c // 2) % 4, c % 2
    p = c % 8
    below, above = (i + 15) % 16, (i + 1) % 16

    def at(dp, col):
        return {"dp": dp, "col": col}

    core_peer = at(i, zh * 8 + y * 2 + (1 - core))
    y_peer = [at(i, zh * 8 + ((y + k) % 4) * 2 + core) for k in (1, 2, 3)]
    z_peer = at(i, (1 - zh) * 8 + p)
    p_peer = [at(i, zh * 8 + (p + k) % 8) for k in range(1, 8)]
    vz_peer = [at(((zl + k) % 4) * 4 + x, c) for k in (1, 2, 3)]
    vx_peer = [at(zl * 4 + (x + k) % 4, c) for k in (1, 2, 3)]
    z_col = (1 - zh) * 8 + p

    small = [
        pltpu.make_async_copy(src, dst, local_sem.at[n])
        for n, (src, dst) in enumerate(
            ((down_h, down), (rank_h, rank), (seg_h, seg), (sketch_h, sketch))
        )
    ]
    for cp in small:
        cp.start()

    def lat_copy(n):
        return pltpu.make_async_copy(lat_h.at[pl.ds(n * CHUNK, CHUNK), :], lat.at[n], lat_sem.at[n])

    def grad_copy(n):
        return pltpu.make_async_copy(grad_h.at[pl.ds(n * CHUNK, CHUNK), :], grad.at[n], grad_sem.at[n])

    for n in range(steps):
        lat_copy(n).start()
    for n in range(steps):
        grad_copy(n).start()
    vown = pltpu.make_async_copy(val_h, vg.at[zl, x], vown_sem)
    vown.start()

    barrier = pltpu.get_barrier_semaphore()
    signals = p_peer + [z_peer] + vz_peer + vx_peer + [at(above, c), at(above, z_col)]
    for peer in signals:
        pl.semaphore_signal(barrier, inc=1, device_id=peer, device_id_type=MESH)
    pl.semaphore_wait(barrier, len(signals))

    def remote(src, dst, send, recv, peer):
        return pltpu.make_async_remote_copy(
            src_ref=src, dst_ref=dst, send_sem=send, recv_sem=recv,
            device_id=peer, device_id_type=MESH,
        )

    vz = [remote(val_h, vg.at[zl, x], vz_send.at[k], vz_recv.at[k], vz_peer[k]) for k in range(3)]
    for cp in vz:
        cp.start()

    for cp in small[:3]:
        cp.wait()
    first = i * EX_DEV - 1

    def rank_step(n, carry):
        lat_copy(n).wait()
        hidden = nt(down[...], lat[n]).astype(BF)
        side = lax.dot_general(
            rank[...], hidden, (((0,), (0,)), ((), ())), preferred_element_type=F32
        ).astype(BF).astype(F32)
        ids = seg[n] - first
        for e in range(1, EX_DEV + 1):
            masked[n, (e - 1) * PB : e * PB, :] = jnp.where(ids == e, side, 0.0).astype(BF)
        masked[n, OWN : OWN + PB, :] = jnp.where(ids == 0, side, 0.0).astype(BF)
        return carry

    lax.fori_loop(0, steps, rank_step, 0)

    gp[...] = jnp.zeros_like(gp)
    small[3].wait()

    def grad_step(n, carry):
        grad_copy(n).wait()
        side = jnp.dot(grad[n], sketch[...], preferred_element_type=F32).astype(BF)
        part = jnp.dot(masked[n], side, preferred_element_type=F32)
        gp[0:OWN, :] += part[0:OWN]
        gp[OWN + PB : ROWS, :] += part[OWN:]
        return carry

    lax.fori_loop(0, steps, grad_step, 0)

    vown.wait()
    for cp in vz:
        cp.wait()
    vx = [
        remote(vg.at[:, x], vg.at[:, x], vx_send.at[k], vx_recv.at[k], vx_peer[k])
        for k in range(3)
    ]

    for t in range(ROWS // 128):
        piece = gp[t * 128 : (t + 1) * 128, :].T
        gt[:, :, :, :, t * 128 : (t + 1) * 128] = piece.reshape(2, 4, 2, 8, 128)

    c0 = remote(gt.at[:, :, 1 - core], r0, s0_send, s0_recv, core_peer)
    c0.start()
    for cp in vx:
        cp.start()
    c0.wait()
    a0[...] = gt[:, :, core] + r0[...]
    c1 = [
        remote(a0.at[:, (y + k) % 4], r1.at[k - 1], s1_send.at[k - 1], s1_recv.at[k - 1], y_peer[k - 1])
        for k in (1, 2, 3)
    ]
    for cp in c1:
        cp.start()
    for cp in c1:
        cp.wait()
    a1[...] = (a0[:, y] + r1[0]) + (r1[1] + r1[2])
    c2 = remote(a1.at[1 - zh, :, 0:OWN], r2, s2_send, s2_recv, z_peer)
    c3 = [
        remote(a1.at[zh, :, OWN:ROWS], r3.at[0], s3_send.at[0], s3_recv.at[0], at(below, c)),
        remote(a1.at[1 - zh, :, OWN:ROWS], r3.at[1], s3_send.at[1], s3_recv.at[1], at(below, z_col)),
    ]
    c2.start()
    for cp in c3:
        cp.start()

    for cp in vx:
        cp.wait()
    val = vg[...].reshape(256, 512)
    val_hi = val.astype(BF)
    val_lo = (val - val_hi.astype(F32)).astype(BF)
    square = val * val
    sq_hi = square.astype(BF)
    sq_lo = (square - sq_hi.astype(F32)).astype(BF)
    ones = jnp.ones((16, 512), BF)
    vsum = nt(ones, sq_hi) + nt(ones, sq_lo)

    c2.wait()
    for cp in c3:
        cp.wait()
    own = a1[zh, :, 0:OWN] + r2[...]
    spill = r3[0] + r3[1]
    own = jnp.concatenate([own[:, : OWN - 128], own[:, OWN - 128 :] + spill], axis=1)

    stack = jnp.concatenate([own[:, e * PB : (e + 1) * PB] for e in range(EX_DEV)], axis=0)
    wide = jnp.concatenate([stack, stack], axis=1)
    wide = jnp.concatenate([wide, wide, wide, wide], axis=1)
    row_a = lax.broadcasted_iota(jnp.int32, (EX_DEV * 8, 512), 0) % 8
    lane_a = lax.broadcasted_iota(jnp.int32, (EX_DEV * 8, 512), 1) // PB
    wide = jnp.where(row_a == lane_a, wide, 0.0)
    hi = wide.astype(BF)
    lo = (wide - hi.astype(F32)).astype(BF)
    dots = nt(hi, val_hi) + (nt(lo, val_hi) + nt(hi, val_lo))
    dots = jnp.sum(dots.reshape(EX_DEV, 8, 256), axis=1)
    own_sq = jnp.sum(jnp.sum(wide * wide, axis=1, keepdims=True).reshape(EX_DEV, 8, 1), axis=1)
    fin[:, 0:256] = dots
    fin[:, 256:384] = jnp.broadcast_to(own_sq, (EX_DEV, 128))
    fin[:, 384:512] = jnp.zeros((EX_DEV, 128), F32)
    fin[0:1, 384:512] = vsum[0:1, 0:128]
    fin[1:2, 384:512] = vsum[0:1, 128:256]

    cz = remote(fin, rz, fz_send, fz_recv, z_peer)
    cz.start()
    cz.wait()
    fb[p] = fin[...] + rz[...]
    cb = [
        remote(fb.at[p], fb.at[p], fb_send.at[k], fb_recv.at[k], p_peer[k]) for k in range(7)
    ]
    for cp in cb:
        cp.start()
    for cp in cb:
        cp.wait()
    total = ((fb[0] + fb[1]) + (fb[2] + fb[3])) + ((fb[4] + fb[5]) + (fb[6] + fb[7]))
    own_scale = math.sqrt(PA * PB) * lax.rsqrt(total[:, 256:257] + epsilon)
    val_scale = lax.rsqrt(total[0:2, 384:512] + epsilon)
    out_ref[:, 0:128] = total[:, 0:128] * own_scale * val_scale[0:1]
    out_ref[:, 128:256] = total[:, 128:256] * own_scale * val_scale[1:2]


def on_device(
    latent,
    adapter_down_matrix,
    output_gradient_rows,
    output_sketch_factor,
    rank_sketch_factor,
    token_example_index,
    validation_sketches,
):
    tokens, columns = output_gradient_rows.shape
    width = latent.shape[1]
    steps = tokens // CHUNK
    dma = pltpu.SemaphoreType.DMA
    vm = pltpu.VMEM
    return pl.pallas_call(
        kernel,
        out_shape=jax.ShapeDtypeStruct((EX_DEV, 256), F32),
        in_specs=[pl.BlockSpec(memory_space=pl.ANY)] * 7,
        out_specs=pl.BlockSpec(memory_space=pltpu.VMEM),
        scratch_shapes=[
            vm((steps, CHUNK, width), BF),
            vm((PB, width), BF),
            vm((steps, CHUNK, columns), BF),
            vm((columns, PA), BF),
            vm((PB, PB), BF),
            vm((steps, 1, CHUNK), jnp.int32),
            vm((steps, OWN + PB, CHUNK), BF),
            vm((ROWS, PA), F32),
            vm((2, 4, 2, 8, ROWS), F32),
            vm((2, 4, 8, ROWS), F32),
            vm((2, 4, 8, ROWS), F32),
            vm((3, 2, 8, ROWS), F32),
            vm((2, 8, ROWS), F32),
            vm((8, OWN), F32),
            vm((2, 8, 128), F32),
            vm((4, 4, 16, 512), F32),
            vm((8, 512), F32),
            vm((8, 512), F32),
            vm((8, 8, 512), F32),
            dma((4,)), dma((steps,)), dma((steps,)), dma,
            dma, dma, dma((3,)), dma((3,)), dma, dma, dma((2,)), dma((2,)),
            dma((3,)), dma((3,)), dma((3,)), dma((3,)), dma, dma, dma((7,)), dma((7,)),
        ],
        compiler_params=pltpu.CompilerParams(
            collective_id=0, has_side_effects=True, vmem_limit_bytes=60 * 1024 * 1024
        ),
    )(
        latent,
        adapter_down_matrix,
        output_gradient_rows,
        output_sketch_factor,
        rank_sketch_factor,
        token_example_index.reshape(steps, 1, CHUNK),
        validation_sketches,
    )


def solution(mesh):
    in_specs = (P("dp", None), P(), P("dp", "col"), P("col", None), P(), P("dp"), P("dp", "col"))
    out_specs = P("dp", None)
    return jax.shard_map(
        on_device, mesh=mesh, in_specs=in_specs, out_specs=out_specs, check_vma=False
    )
```

```python
import functools
import math

import jax
import jax.numpy as jnp
from jax import lax
from jax.experimental import pallas as pl
from jax.experimental.pallas import tpu as pltpu
from jax.sharding import PartitionSpec as P

PA = 128
PB = 64
EX_DEV = 8
MESH = pl.DeviceIdType.MESH

epsilon = 1e-06

BF = jnp.bfloat16
F32 = jnp.float32

CHUNK = 512
OWN = EX_DEV * PB
ROWS = OWN + 2 * PB


def nt(x, y):
    return lax.dot_general(x, y, (((1,), (1,)), ((), ())), preferred_element_type=F32)


def kernel(
    lat_h, down_h, grad_h, sketch_h, rank_h, seg_h, val_h, out_ref,
    lat, down, grad, sketch, rank, seg, masked, gp, gt,
    r0, a0, r1, a1, r2, r3, vg, fin, rz, fb,
    local_sem, lat_sem, grad_sem, vown_sem,
    s0_send, s0_recv, s1_send, s1_recv, s2_send, s2_recv, s3_send, s3_recv,
    vz_send, vz_recv, vx_send, vx_recv, vf_send, vf_recv, fz_send, fz_recv, fb_send, fb_recv,
):
    steps = grad.shape[0]
    i = lax.axis_index("dp")
    c = lax.axis_index("col")
    zl, x = i // 4, i % 4
    zh, y, core = c // 8, (c // 2) % 4, c % 2
    p = c % 8
    below, above = (i + 15) % 16, (i + 1) % 16

    def at(dp, col):
        return {"dp": dp, "col": col}

    core_peer = at(i, zh * 8 + y * 2 + (1 - core))
    y_peer = [at(i, zh * 8 + ((y + k) % 4) * 2 + core) for k in (1, 2, 3)]
    z_peer = at(i, (1 - zh) * 8 + p)
    p_peer = [at(i, zh * 8 + (p + k) % 8) for k in range(1, 8)]
    vz_peer = [at(((zl + k) % 4) * 4 + x, c) for k in (1, 2, 3)]
    vx_peer = [at(zl * 4 + (x + k) % 4, c) for k in (1, 3)]
    z_col = (1 - zh) * 8 + p

    small = [
        pltpu.make_async_copy(src, dst, local_sem.at[n])
        for n, (src, dst) in enumerate(
            ((down_h, down), (rank_h, rank), (seg_h, seg), (sketch_h, sketch))
        )
    ]
    for cp in small:
        cp.start()

    def lat_copy(n):
        return pltpu.make_async_copy(lat_h.at[pl.ds(n * CHUNK, CHUNK), :], lat.at[n], lat_sem.at[n])

    def grad_copy(n):
        return pltpu.make_async_copy(grad_h.at[pl.ds(n * CHUNK, CHUNK), :], grad.at[n], grad_sem.at[n])

    for n in range(steps):
        lat_copy(n).start()
    for n in range(steps):
        grad_copy(n).start()
    vown = pltpu.make_async_copy(val_h, vg.at[zl, x], vown_sem)
    vown.start()

    barrier = pltpu.get_barrier_semaphore()
    signals = p_peer + [z_peer] + vz_peer + vx_peer + [at(above, c), at(above, z_col)]
    for peer in signals:
        pl.semaphore_signal(barrier, inc=1, device_id=peer, device_id_type=MESH)
    pl.semaphore_wait(barrier, len(signals))

    def remote(src, dst, send, recv, peer):
        return pltpu.make_async_remote_copy(
            src_ref=src, dst_ref=dst, send_sem=send, recv_sem=recv,
            device_id=peer, device_id_type=MESH,
        )

    vz = [remote(val_h, vg.at[zl, x], vz_send.at[k], vz_recv.at[k], vz_peer[k]) for k in range(3)]
    for cp in vz:
        cp.start()

    for cp in small[:3]:
        cp.wait()
    first = i * EX_DEV - 1

    def rank_step(n, carry):
        lat_copy(n).wait()
        hidden = nt(down[...], lat[n]).astype(BF)
        side = lax.dot_general(
            rank[...], hidden, (((0,), (0,)), ((), ())), preferred_element_type=F32
        ).astype(BF).astype(F32)
        ids = seg[n] - first
        for e in range(1, EX_DEV + 1):
            masked[n, (e - 1) * PB : e * PB, :] = jnp.where(ids == e, side, 0.0).astype(BF)
        masked[n, OWN : OWN + PB, :] = jnp.where(ids == 0, side, 0.0).astype(BF)
        return carry

    lax.fori_loop(0, steps, rank_step, 0)

    sends = list(vz)

    vown.wait()
    for cp in vz:
        cp.wait_recv()
    vx = [remote(vg.at[:, x], vg.at[:, x], vx_send.at[k], vx_recv.at[k], vx_peer[k]) for k in (0, 1)]
    for cp in vx:
        cp.start()
    sends += vx

    gp[...] = jnp.zeros_like(gp)
    small[3].wait()

    def grad_step(n, carry):
        grad_copy(n).wait()
        side = jnp.dot(grad[n], sketch[...], preferred_element_type=F32).astype(BF)
        part = jnp.dot(masked[n], side, preferred_element_type=F32)
        gp[0:OWN, :] += part[0:OWN]
        gp[OWN + PB : ROWS, :] += part[OWN:]
        return carry

    lax.fori_loop(0, steps, grad_step, 0)

    for t in range(ROWS // 128):
        piece = gp[t * 128 : (t + 1) * 128, :].T
        gt[:, :, :, :, t * 128 : (t + 1) * 128] = piece.reshape(2, 4, 2, 8, 128)

    c0 = remote(gt.at[:, :, 1 - core], r0, s0_send, s0_recv, core_peer)
    c0.start()

    for cp in vx:
        cp.wait_recv()
    left, right = (x + 3) % 4, (x + 1) % 4
    vf = [
        remote(vg.at[0:2, left], vg.at[0:2, left], vf_send.at[0], vf_recv.at[0], vx_peer[0]),
        remote(vg.at[2:4, right], vg.at[2:4, right], vf_send.at[1], vf_recv.at[1], vx_peer[1]),
    ]
    for cp in vf:
        cp.start()

    c0.wait_recv()
    a0[...] = gt[:, :, core] + r0[...]
    c1 = [
        remote(a0.at[:, (y + k) % 4], r1.at[k - 1], s1_send.at[k - 1], s1_recv.at[k - 1], y_peer[k - 1])
        for k in (1, 2, 3)
    ]
    for cp in c1:
        cp.start()
    for cp in c1:
        cp.wait_recv()
    a1[...] = (a0[:, y] + r1[0]) + (r1[1] + r1[2])
    c2 = remote(a1.at[1 - zh, :, 0:OWN], r2, s2_send, s2_recv, z_peer)
    c3 = [
        remote(a1.at[zh, :, OWN:ROWS], r3.at[0], s3_send.at[0], s3_recv.at[0], at(below, c)),
        remote(a1.at[1 - zh, :, OWN:ROWS], r3.at[1], s3_send.at[1], s3_recv.at[1], at(below, z_col)),
    ]
    c2.start()
    for cp in c3:
        cp.start()
    sends += vf + [c0] + c1 + [c2] + c3

    for cp in vf:
        cp.wait_recv()
    val = vg[...].reshape(256, 512)
    val_hi = val.astype(BF)
    val_lo = (val - val_hi.astype(F32)).astype(BF)
    square = val * val
    sq_hi = square.astype(BF)
    sq_lo = (square - sq_hi.astype(F32)).astype(BF)
    ones = jnp.ones((16, 512), BF)
    vsum = nt(ones, sq_hi) + nt(ones, sq_lo)

    c2.wait_recv()
    for cp in c3:
        cp.wait_recv()
    own = a1[zh, :, 0:OWN] + r2[...]
    spill = r3[0] + r3[1]
    own = jnp.concatenate([own[:, : OWN - 128], own[:, OWN - 128 :] + spill], axis=1)

    stack = jnp.concatenate([own[:, e * PB : (e + 1) * PB] for e in range(EX_DEV)], axis=0)
    wide = jnp.concatenate([stack, stack], axis=1)
    wide = jnp.concatenate([wide, wide, wide, wide], axis=1)
    row_a = lax.broadcasted_iota(jnp.int32, (EX_DEV * 8, 512), 0) % 8
    lane_a = lax.broadcasted_iota(jnp.int32, (EX_DEV * 8, 512), 1) // PB
    wide = jnp.where(row_a == lane_a, wide, 0.0)
    hi = wide.astype(BF)
    lo = (wide - hi.astype(F32)).astype(BF)
    dots = nt(hi, val_hi) + (nt(lo, val_hi) + nt(hi, val_lo))
    dots = jnp.sum(dots.reshape(EX_DEV, 8, 256), axis=1)
    own_sq = jnp.sum(jnp.sum(wide * wide, axis=1, keepdims=True).reshape(EX_DEV, 8, 1), axis=1)
    fin[:, 0:256] = dots
    fin[:, 256:384] = jnp.broadcast_to(own_sq, (EX_DEV, 128))
    fin[:, 384:512] = jnp.zeros((EX_DEV, 128), F32)
    fin[0:1, 384:512] = vsum[0:1, 0:128]
    fin[1:2, 384:512] = vsum[0:1, 128:256]

    cz = remote(fin, rz, fz_send, fz_recv, z_peer)
    cz.start()
    cz.wait_recv()
    fb[p] = fin[...] + rz[...]
    cb = [
        remote(fb.at[p], fb.at[p], fb_send.at[k], fb_recv.at[k], p_peer[k]) for k in range(7)
    ]
    for cp in cb:
        cp.start()
    for cp in cb:
        cp.wait_recv()
    total = ((fb[0] + fb[1]) + (fb[2] + fb[3])) + ((fb[4] + fb[5]) + (fb[6] + fb[7]))
    own_scale = math.sqrt(PA * PB) * lax.rsqrt(total[:, 256:257] + epsilon)
    val_scale = lax.rsqrt(total[0:2, 384:512] + epsilon)
    out_ref[:, 0:128] = total[:, 0:128] * own_scale * val_scale[0:1]
    out_ref[:, 128:256] = total[:, 128:256] * own_scale * val_scale[1:2]
    for cp in sends + [cz] + cb:
        cp.wait_send()


def on_device(
    latent,
    adapter_down_matrix,
    output_gradient_rows,
    output_sketch_factor,
    rank_sketch_factor,
    token_example_index,
    validation_sketches,
):
    tokens, columns = output_gradient_rows.shape
    width = latent.shape[1]
    steps = tokens // CHUNK
    dma = pltpu.SemaphoreType.DMA
    vm = pltpu.VMEM
    return pl.pallas_call(
        kernel,
        out_shape=pltpu.VMEM((EX_DEV, 256), F32),
        in_specs=[pl.BlockSpec(memory_space=pl.ANY)] * 7,
        out_specs=pl.BlockSpec(memory_space=pltpu.VMEM),
        scratch_shapes=[
            vm((steps, CHUNK, width), BF),
            vm((PB, width), BF),
            vm((steps, CHUNK, columns), BF),
            vm((columns, PA), BF),
            vm((PB, PB), BF),
            vm((steps, 1, CHUNK), jnp.int32),
            vm((steps, OWN + PB, CHUNK), BF),
            vm((ROWS, PA), F32),
            vm((2, 4, 2, 8, ROWS), F32),
            vm((2, 4, 8, ROWS), F32),
            vm((2, 4, 8, ROWS), F32),
            vm((3, 2, 8, ROWS), F32),
            vm((2, 8, ROWS), F32),
            vm((8, OWN), F32),
            vm((2, 8, 128), F32),
            vm((4, 4, 16, 512), F32),
            vm((8, 512), F32),
            vm((8, 512), F32),
            vm((8, 8, 512), F32),
            dma((4,)), dma((steps,)), dma((steps,)), dma,
            dma, dma, dma((3,)), dma((3,)), dma, dma, dma((2,)), dma((2,)),
            dma((3,)), dma((3,)), dma((2,)), dma((2,)), dma((2,)), dma((2,)), dma, dma, dma((7,)), dma((7,)),
        ],
        compiler_params=pltpu.CompilerParams(
            collective_id=0, has_side_effects=True, vmem_limit_bytes=60 * 1024 * 1024
        ),
    )(
        latent,
        adapter_down_matrix,
        output_gradient_rows,
        output_sketch_factor,
        rank_sketch_factor,
        token_example_index.reshape(steps, 1, CHUNK),
        validation_sketches,
    )


def solution(mesh):
    in_specs = (P("dp", None), P(), P("dp", "col"), P("col", None), P(), P("dp"), P("dp", "col"))
    out_specs = P("dp", None)
    return jax.shard_map(
        on_device, mesh=mesh, in_specs=in_specs, out_specs=out_specs, check_vma=False
    )
```

```python
import functools
import math

import jax
import jax.numpy as jnp
from jax import lax
from jax.experimental import pallas as pl
from jax.experimental.pallas import tpu as pltpu
from jax.sharding import PartitionSpec as P

PA = 128
PB = 64
EX_DEV = 8
MESH = pl.DeviceIdType.MESH

epsilon = 1e-06

BF = jnp.bfloat16
F32 = jnp.float32

CHUNK = 512
OWN = EX_DEV * PB
ROWS = OWN + 2 * PB


def nt(x, y):
    return lax.dot_general(x, y, (((1,), (1,)), ((), ())), preferred_element_type=F32)


def local_kernel(
    lat_h, down_h, grad_h, sketch_h, rank_h, seg_h, gt,
    lat, down, grad, sketch, rank, seg, masked, gp, local_sem, lat_sem, grad_sem,
):
    steps = grad.shape[0]
    first = lax.axis_index("dp") * EX_DEV - 1

    small = [
        pltpu.make_async_copy(src, dst, local_sem.at[n])
        for n, (src, dst) in enumerate(
            ((down_h, down), (rank_h, rank), (seg_h, seg), (sketch_h, sketch))
        )
    ]
    for cp in small:
        cp.start()

    def lat_copy(n):
        return pltpu.make_async_copy(lat_h.at[pl.ds(n * CHUNK, CHUNK), :], lat.at[n], lat_sem.at[n])

    def grad_copy(n):
        return pltpu.make_async_copy(grad_h.at[pl.ds(n * CHUNK, CHUNK), :], grad.at[n], grad_sem.at[n])

    for n in range(steps):
        lat_copy(n).start()
    for n in range(steps):
        grad_copy(n).start()
    for cp in small[:3]:
        cp.wait()

    def rank_step(n, carry):
        lat_copy(n).wait()
        hidden = nt(down[...], lat[n]).astype(BF)
        side = lax.dot_general(
            rank[...], hidden, (((0,), (0,)), ((), ())), preferred_element_type=F32
        ).astype(BF).astype(F32)
        ids = seg[n] - first
        for e in range(1, EX_DEV + 1):
            masked[n, (e - 1) * PB : e * PB, :] = jnp.where(ids == e, side, 0.0).astype(BF)
        masked[n, OWN : OWN + PB, :] = jnp.where(ids == 0, side, 0.0).astype(BF)
        return carry

    lax.fori_loop(0, steps, rank_step, 0)

    gp[...] = jnp.zeros_like(gp)
    small[3].wait()

    def grad_step(n, carry):
        grad_copy(n).wait()
        side = jnp.dot(grad[n], sketch[...], preferred_element_type=F32).astype(BF)
        part = jnp.dot(masked[n], side, preferred_element_type=F32)
        gp[0:OWN, :] += part[0:OWN]
        gp[OWN + PB : ROWS, :] += part[OWN:]
        return carry

    lax.fori_loop(0, steps, grad_step, 0)

    for t in range(ROWS // 128):
        piece = gp[t * 128 : (t + 1) * 128, :].T
        gt[:, :, :, :, t * 128 : (t + 1) * 128] = piece.reshape(2, 4, 2, 8, 128)


def comm_kernel(
    gt, val_h, out_ref,
    r0, a0, r1, a1, r2, r3, vg, fin, rz, fb, vown_sem,
    s0_send, s0_recv, s1_send, s1_recv, s2_send, s2_recv, s3_send, s3_recv,
    vz_send, vz_recv, vx_send, vx_recv, fz_send, fz_recv, fb_send, fb_recv,
):
    i = lax.axis_index("dp")
    c = lax.axis_index("col")
    zl, x = i // 4, i % 4
    zh, y, core = c // 8, (c // 2) % 4, c % 2
    p = c % 8
    below, above = (i + 15) % 16, (i + 1) % 16

    def at(dp, col):
        return {"dp": dp, "col": col}

    core_peer = at(i, zh * 8 + y * 2 + (1 - core))
    y_peer = [at(i, zh * 8 + ((y + k) % 4) * 2 + core) for k in (1, 2, 3)]
    z_peer = at(i, (1 - zh) * 8 + p)
    p_peer = [at(i, zh * 8 + (p + k) % 8) for k in range(1, 8)]
    vz_peer = [at(((zl + k) % 4) * 4 + x, c) for k in (1, 2, 3)]
    vx_peer = [at(zl * 4 + (x + k) % 4, c) for k in (1, 2, 3)]
    z_col = (1 - zh) * 8 + p

    vown = pltpu.make_async_copy(val_h, vg.at[zl, x], vown_sem)
    vown.start()

    barrier = pltpu.get_barrier_semaphore()
    signals = p_peer + [z_peer] + vz_peer + vx_peer + [at(above, c), at(above, z_col)]
    for peer in signals:
        pl.semaphore_signal(barrier, inc=1, device_id=peer, device_id_type=MESH)
    pl.semaphore_wait(barrier, len(signals))

    def remote(src, dst, send, recv, peer):
        return pltpu.make_async_remote_copy(
            src_ref=src, dst_ref=dst, send_sem=send, recv_sem=recv,
            device_id=peer, device_id_type=MESH,
        )

    c0 = remote(gt.at[:, :, 1 - core], r0, s0_send, s0_recv, core_peer)
    c0.start()
    vz = [remote(val_h, vg.at[zl, x], vz_send.at[k], vz_recv.at[k], vz_peer[k]) for k in range(3)]
    for cp in vz:
        cp.start()
    sends = [c0] + vz

    c0.wait_recv()
    a0[...] = gt[:, :, core] + r0[...]
    c1 = [
        remote(a0.at[:, (y + k) % 4], r1.at[k - 1], s1_send.at[k - 1], s1_recv.at[k - 1], y_peer[k - 1])
        for k in (1, 2, 3)
    ]
    for cp in c1:
        cp.start()

    vown.wait()
    for cp in vz:
        cp.wait_recv()
    vx = [
        remote(vg.at[:, x], vg.at[:, x], vx_send.at[k], vx_recv.at[k], vx_peer[k])
        for k in range(3)
    ]
    for cp in vx:
        cp.start()

    for cp in c1:
        cp.wait_recv()
    a1[...] = (a0[:, y] + r1[0]) + (r1[1] + r1[2])
    c2 = remote(a1.at[1 - zh, :, 0:OWN], r2, s2_send, s2_recv, z_peer)
    c3 = [
        remote(a1.at[zh, :, OWN:ROWS], r3.at[0], s3_send.at[0], s3_recv.at[0], at(below, c)),
        remote(a1.at[1 - zh, :, OWN:ROWS], r3.at[1], s3_send.at[1], s3_recv.at[1], at(below, z_col)),
    ]
    c2.start()
    for cp in c3:
        cp.start()
    sends += c1 + vx + [c2] + c3

    for cp in vx:
        cp.wait_recv()
    val = vg[...].reshape(256, 512)
    val_hi = val.astype(BF)
    val_lo = (val - val_hi.astype(F32)).astype(BF)
    square = val * val
    sq_hi = square.astype(BF)
    sq_lo = (square - sq_hi.astype(F32)).astype(BF)
    ones = jnp.ones((16, 512), BF)
    vsum = nt(ones, sq_hi) + nt(ones, sq_lo)

    c2.wait_recv()
    for cp in c3:
        cp.wait_recv()
    own = a1[zh, :, 0:OWN] + r2[...]
    spill = r3[0] + r3[1]
    own = jnp.concatenate([own[:, : OWN - 128], own[:, OWN - 128 :] + spill], axis=1)

    stack = jnp.concatenate([own[:, e * PB : (e + 1) * PB] for e in range(EX_DEV)], axis=0)
    wide = jnp.concatenate([stack, stack], axis=1)
    wide = jnp.concatenate([wide, wide, wide, wide], axis=1)
    row_a = lax.broadcasted_iota(jnp.int32, (EX_DEV * 8, 512), 0) % 8
    lane_a = lax.broadcasted_iota(jnp.int32, (EX_DEV * 8, 512), 1) // PB
    wide = jnp.where(row_a == lane_a, wide, 0.0)
    hi = wide.astype(BF)
    lo = (wide - hi.astype(F32)).astype(BF)
    dots = nt(hi, val_hi) + (nt(lo, val_hi) + nt(hi, val_lo))
    dots = jnp.sum(dots.reshape(EX_DEV, 8, 256), axis=1)
    own_sq = jnp.sum(jnp.sum(wide * wide, axis=1, keepdims=True).reshape(EX_DEV, 8, 1), axis=1)
    fin[:, 0:256] = dots
    fin[:, 256:384] = jnp.broadcast_to(own_sq, (EX_DEV, 128))
    fin[:, 384:512] = jnp.zeros((EX_DEV, 128), F32)
    fin[0:1, 384:512] = vsum[0:1, 0:128]
    fin[1:2, 384:512] = vsum[0:1, 128:256]

    cz = remote(fin, rz, fz_send, fz_recv, z_peer)
    cz.start()
    cz.wait_recv()
    fb[p] = fin[...] + rz[...]
    cb = [
        remote(fb.at[p], fb.at[p], fb_send.at[k], fb_recv.at[k], p_peer[k]) for k in range(7)
    ]
    for cp in cb:
        cp.start()
    for cp in cb:
        cp.wait_recv()
    total = ((fb[0] + fb[1]) + (fb[2] + fb[3])) + ((fb[4] + fb[5]) + (fb[6] + fb[7]))
    own_scale = math.sqrt(PA * PB) * lax.rsqrt(total[:, 256:257] + epsilon)
    val_scale = lax.rsqrt(total[0:2, 384:512] + epsilon)
    out_ref[:, 0:128] = total[:, 0:128] * own_scale * val_scale[0:1]
    out_ref[:, 128:256] = total[:, 128:256] * own_scale * val_scale[1:2]
    for cp in sends + [cz] + cb:
        cp.wait_send()


def on_device(
    latent,
    adapter_down_matrix,
    output_gradient_rows,
    output_sketch_factor,
    rank_sketch_factor,
    token_example_index,
    validation_sketches,
):
    tokens, columns = output_gradient_rows.shape
    width = latent.shape[1]
    steps = tokens // CHUNK
    dma = pltpu.SemaphoreType.DMA
    vm = pltpu.VMEM
    any_spec = pl.BlockSpec(memory_space=pl.ANY)
    vmem_spec = pl.BlockSpec(memory_space=pltpu.VMEM)
    partial_features = pl.pallas_call(
        local_kernel,
        out_shape=vm((2, 4, 2, 8, ROWS), F32),
        in_specs=[any_spec] * 6,
        out_specs=vmem_spec,
        scratch_shapes=[
            vm((steps, CHUNK, width), BF),
            vm((PB, width), BF),
            vm((steps, CHUNK, columns), BF),
            vm((columns, PA), BF),
            vm((PB, PB), BF),
            vm((steps, 1, CHUNK), jnp.int32),
            vm((steps, OWN + PB, CHUNK), BF),
            vm((ROWS, PA), F32),
            dma((4,)), dma((steps,)), dma((steps,)),
        ],
        compiler_params=pltpu.CompilerParams(vmem_limit_bytes=60 * 1024 * 1024),
    )(
        latent,
        adapter_down_matrix,
        output_gradient_rows,
        output_sketch_factor,
        rank_sketch_factor,
        token_example_index.reshape(steps, 1, CHUNK),
    )
    return pl.pallas_call(
        comm_kernel,
        out_shape=vm((EX_DEV, 256), F32),
        in_specs=[vmem_spec, any_spec],
        out_specs=vmem_spec,
        scratch_shapes=[
            vm((2, 4, 8, ROWS), F32),
            vm((2, 4, 8, ROWS), F32),
            vm((3, 2, 8, ROWS), F32),
            vm((2, 8, ROWS), F32),
            vm((8, OWN), F32),
            vm((2, 8, 128), F32),
            vm((4, 4, 16, 512), F32),
            vm((8, 512), F32),
            vm((8, 512), F32),
            vm((8, 8, 512), F32),
            dma, dma, dma, dma((3,)), dma((3,)), dma, dma, dma((2,)), dma((2,)),
            dma((3,)), dma((3,)), dma((3,)), dma((3,)), dma, dma, dma((7,)), dma((7,)),
        ],
        compiler_params=pltpu.CompilerParams(
            collective_id=0, has_side_effects=True, vmem_limit_bytes=16 * 1024 * 1024
        ),
    )(partial_features, validation_sketches)


def solution(mesh):
    in_specs = (P("dp", None), P(), P("dp", "col"), P("col", None), P(), P("dp"), P("dp", "col"))
    out_specs = P("dp", None)
    return jax.shard_map(
        on_device, mesh=mesh, in_specs=in_specs, out_specs=out_specs, check_vma=False
    )
```

```python
import functools
import math

import jax
import jax.numpy as jnp
from jax import lax
from jax.experimental import pallas as pl
from jax.experimental.pallas import tpu as pltpu
from jax.sharding import PartitionSpec as P

PA = 128
PB = 64
EX_DEV = 8
MESH = pl.DeviceIdType.MESH

epsilon = 1e-06

BF = jnp.bfloat16
F32 = jnp.float32

LAT_ROWS = 1024
GRAD_ROWS = 256
STEP = 512
OWN = EX_DEV * PB
ROWS = OWN + 2 * PB


def nt(x, y):
    return lax.dot_general(x, y, (((1,), (1,)), ((), ())), preferred_element_type=F32)


def local_kernel(
    lat_h, down_h, grad_h, sketch_h, rank_h, seg_h, gt,
    lat, down, grad, sketch, rank, seg, masked, side, gp, local_sem, lat_sem, grad_sem,
):
    tokens = grad.shape[0]
    first = lax.axis_index("dp") * EX_DEV - 1

    def rows(src, dst, sem, n, size):
        at = pl.ds(n * size, size)
        return pltpu.make_async_copy(src.at[at, :], dst.at[at, :], sem.at[n])

    small = [
        pltpu.make_async_copy(src, dst, local_sem.at[n])
        for n, (src, dst) in enumerate(
            ((down_h, down), (rank_h, rank), (seg_h, seg), (sketch_h, sketch))
        )
    ]
    lats = [rows(lat_h, lat, lat_sem, n, LAT_ROWS) for n in range(tokens // LAT_ROWS)]
    grads = [rows(grad_h, grad, grad_sem, n, GRAD_ROWS) for n in range(tokens // GRAD_ROWS)]
    order = iter(grads)

    def more(count):
        for cp in [cp for _, cp in zip(range(count), order)]:
            cp.start()

    for cp in small[:3]:
        cp.start()
    lats[0].start()
    lats[1].start()
    small[3].start()
    more(2)
    for cp in small[:3]:
        cp.wait()

    for n, cp in enumerate(lats):
        cp.wait()
        more(1)
        at = slice(n * LAT_ROWS, (n + 1) * LAT_ROWS)
        hidden = nt(down[...], lat[at, :]).astype(BF)
        rank_side = lax.dot_general(
            rank[...], hidden, (((0,), (0,)), ((), ())), preferred_element_type=F32
        ).astype(BF).astype(F32)
        ids = seg[:, at] - first
        for e in range(1, EX_DEV + 1):
            masked[(e - 1) * PB : e * PB, at] = jnp.where(ids == e, rank_side, 0.0).astype(BF)
        masked[OWN : OWN + PB, at] = jnp.where(ids == 0, rank_side, 0.0).astype(BF)

    small[3].wait()
    gp[OWN : OWN + PB, :] = jnp.zeros((PB, PA), F32)

    def project(n):
        at = slice(n * STEP, (n + 1) * STEP)
        part = jnp.dot(masked[:, at], side[at, :], preferred_element_type=F32)
        if n == 0:
            gp[0:OWN, :] = part[0:OWN]
            gp[OWN + PB : ROWS, :] = part[OWN:]
        else:
            gp[0:OWN, :] += part[0:OWN]
            gp[OWN + PB : ROWS, :] += part[OWN:]

    per = STEP // GRAD_ROWS
    for n in range(tokens // STEP):
        for cp in grads[n * per : (n + 1) * per]:
            cp.wait()
        more(per)
        at = slice(n * STEP, (n + 1) * STEP)
        side[at, :] = jnp.dot(grad[at, :], sketch[...], preferred_element_type=F32).astype(BF)
        if n:
            project(n - 1)
    project(tokens // STEP - 1)

    for t in range(ROWS // 128):
        piece = gp[t * 128 : (t + 1) * 128, :].T
        gt[:, :, :, :, t * 128 : (t + 1) * 128] = piece.reshape(2, 4, 2, 8, 128)


def comm_kernel(
    gt, val_h, out_ref,
    r0, a0, r1, a1, r2, r3, vg, vs, fin, rz, fb, vown_sem,
    s0_send, s0_recv, s1_send, s1_recv, s2_send, s2_recv, s3_send, s3_recv,
    vz_send, vz_recv, vx_send, vx_recv, vs_send, vs_recv, fz_send, fz_recv, fb_send, fb_recv,
):
    i = lax.axis_index("dp")
    c = lax.axis_index("col")
    zl, x = i // 4, i % 4
    zh, y, core = c // 8, (c // 2) % 4, c % 2
    p = c % 8
    below, above = (i + 15) % 16, (i + 1) % 16

    def at(dp, col):
        return {"dp": dp, "col": col}

    core_peer = at(i, zh * 8 + y * 2 + (1 - core))
    y_peer = [at(i, zh * 8 + ((y + k) % 4) * 2 + core) for k in (1, 2, 3)]
    z_peer = at(i, (1 - zh) * 8 + p)
    p_peer = [at(i, zh * 8 + (p + k) % 8) for k in range(1, 8)]
    c_peer = [at(i, (c + k) % 16) for k in range(1, 16)]
    vz_peer = [at(((zl + k) % 4) * 4 + x, c) for k in (1, 2, 3)]
    vx_peer = [at(zl * 4 + (x + k) % 4, c) for k in (1, 2, 3)]
    z_col = (1 - zh) * 8 + p

    vown = pltpu.make_async_copy(val_h, vg.at[zl, x], vown_sem)
    vown.start()

    barrier = pltpu.get_barrier_semaphore()
    signals = c_peer + vz_peer + vx_peer + [at(above, c), at(above, z_col)]
    for peer in signals:
        pl.semaphore_signal(barrier, inc=1, device_id=peer, device_id_type=MESH)
    pl.semaphore_wait(barrier, len(signals))

    def remote(src, dst, send, recv, peer):
        return pltpu.make_async_remote_copy(
            src_ref=src, dst_ref=dst, send_sem=send, recv_sem=recv,
            device_id=peer, device_id_type=MESH,
        )

    c0 = remote(gt.at[:, :, 1 - core], r0, s0_send, s0_recv, core_peer)
    c0.start()
    vz = [remote(val_h, vg.at[zl, x], vz_send.at[k], vz_recv.at[k], vz_peer[k]) for k in range(3)]
    for cp in vz:
        cp.start()
    sends = [c0] + vz

    c0.wait_recv()
    a0[...] = gt[:, :, core] + r0[...]
    c1 = [
        remote(a0.at[:, (y + k) % 4], r1.at[k - 1], s1_send.at[k - 1], s1_recv.at[k - 1], y_peer[k - 1])
        for k in (1, 2, 3)
    ]
    for cp in c1:
        cp.start()

    vown.wait()
    for cp in vz:
        cp.wait_recv()
    vx = [
        remote(vg.at[:, x], vg.at[:, x], vx_send.at[k], vx_recv.at[k], vx_peer[k])
        for k in range(3)
    ]
    for cp in vx:
        cp.start()

    for cp in c1:
        cp.wait_recv()
    a1[...] = (a0[:, y] + r1[0]) + (r1[1] + r1[2])
    c2 = remote(a1.at[1 - zh, :, 0:OWN], r2, s2_send, s2_recv, z_peer)
    c3 = [
        remote(a1.at[zh, :, OWN:ROWS], r3.at[0], s3_send.at[0], s3_recv.at[0], at(below, c)),
        remote(a1.at[1 - zh, :, OWN:ROWS], r3.at[1], s3_send.at[1], s3_recv.at[1], at(below, z_col)),
    ]
    c2.start()
    for cp in c3:
        cp.start()
    sends += c1 + vx + [c2] + c3

    for cp in vx:
        cp.wait_recv()
    val = vg[...].reshape(256, 512)
    val_hi = val.astype(BF)
    val_lo = (val - val_hi.astype(F32)).astype(BF)
    square = val * val
    sq_hi = square.astype(BF)
    sq_lo = (square - sq_hi.astype(F32)).astype(BF)
    ones = jnp.ones((16, 512), BF)
    vs[c] = nt(ones, sq_hi)[0:1] + nt(ones, sq_lo)[0:1]
    cv = [
        remote(vs.at[c], vs.at[c], vs_send.at[k], vs_recv.at[k], c_peer[k])
        for k in range(15)
    ]
    for cp in cv:
        cp.start()

    c2.wait_recv()
    for cp in c3:
        cp.wait_recv()
    own = a1[zh, :, 0:OWN] + r2[...]
    spill = r3[0] + r3[1]
    own = jnp.concatenate([own[:, : OWN - 128], own[:, OWN - 128 :] + spill], axis=1)

    stack = jnp.concatenate([own[:, e * PB : (e + 1) * PB] for e in range(EX_DEV)], axis=0)
    wide = jnp.concatenate([stack, stack], axis=1)
    wide = jnp.concatenate([wide, wide, wide, wide], axis=1)
    row_a = lax.broadcasted_iota(jnp.int32, (EX_DEV * 8, 512), 0) % 8
    lane_a = lax.broadcasted_iota(jnp.int32, (EX_DEV * 8, 512), 1) // PB
    wide = jnp.where(row_a == lane_a, wide, 0.0)
    hi = wide.astype(BF)
    lo = (wide - hi.astype(F32)).astype(BF)
    dots = nt(hi, val_hi) + (nt(lo, val_hi) + nt(hi, val_lo))
    dots = jnp.sum(dots.reshape(EX_DEV, 8, 256), axis=1)
    own_sq = jnp.sum(jnp.sum(wide * wide, axis=1, keepdims=True).reshape(EX_DEV, 8, 1), axis=1)
    fin[:, 0:256] = dots
    fin[:, 256:384] = jnp.broadcast_to(own_sq, (EX_DEV, 128))

    cz = remote(fin, rz, fz_send, fz_recv, z_peer)
    cz.start()
    cz.wait_recv()
    fb[p] = fin[...] + rz[...]
    for cp in cv:
        cp.wait_recv()
    val_scale = lax.rsqrt(jnp.sum(vs[...], axis=0) + epsilon)
    cb = [
        remote(fb.at[p], fb.at[p], fb_send.at[k], fb_recv.at[k], p_peer[k]) for k in range(7)
    ]
    for cp in cb:
        cp.start()
    for cp in cb:
        cp.wait_recv()
    total = ((fb[0] + fb[1]) + (fb[2] + fb[3])) + ((fb[4] + fb[5]) + (fb[6] + fb[7]))
    own_scale = math.sqrt(PA * PB) * lax.rsqrt(total[:, 256:257] + epsilon)
    out_ref[...] = total[:, 0:256] * own_scale * val_scale
    for cp in sends + cv + [cz] + cb:
        cp.wait_send()


def on_device(
    latent,
    adapter_down_matrix,
    output_gradient_rows,
    output_sketch_factor,
    rank_sketch_factor,
    token_example_index,
    validation_sketches,
):
    tokens, columns = output_gradient_rows.shape
    width = latent.shape[1]
    dma = pltpu.SemaphoreType.DMA
    vm = pltpu.VMEM
    any_spec = pl.BlockSpec(memory_space=pl.ANY)
    vmem_spec = pl.BlockSpec(memory_space=pltpu.VMEM)
    partial_features = pl.pallas_call(
        local_kernel,
        out_shape=vm((2, 4, 2, 8, ROWS), F32),
        in_specs=[any_spec] * 6,
        out_specs=vmem_spec,
        scratch_shapes=[
            vm((tokens, width), BF),
            vm((PB, width), BF),
            vm((tokens, columns), BF),
            vm((columns, PA), BF),
            vm((PB, PB), BF),
            vm((1, tokens), jnp.int32),
            vm((OWN + PB, tokens), BF),
            vm((tokens, PA), BF),
            vm((ROWS, PA), F32),
            dma((4,)), dma((tokens // LAT_ROWS,)), dma((tokens // GRAD_ROWS,)),
        ],
        compiler_params=pltpu.CompilerParams(vmem_limit_bytes=60 * 1024 * 1024),
    )(
        latent,
        adapter_down_matrix,
        output_gradient_rows,
        output_sketch_factor,
        rank_sketch_factor,
        token_example_index.reshape(1, tokens),
    )
    return pl.pallas_call(
        comm_kernel,
        out_shape=vm((EX_DEV, 256), F32),
        in_specs=[vmem_spec, any_spec],
        out_specs=vmem_spec,
        scratch_shapes=[
            vm((2, 4, 8, ROWS), F32),
            vm((2, 4, 8, ROWS), F32),
            vm((3, 2, 8, ROWS), F32),
            vm((2, 8, ROWS), F32),
            vm((8, OWN), F32),
            vm((2, 8, 128), F32),
            vm((4, 4, 16, 512), F32),
            vm((16, 1, 256), F32),
            vm((8, 384), F32),
            vm((8, 384), F32),
            vm((8, 8, 384), F32),
            dma, dma, dma, dma((3,)), dma((3,)), dma, dma, dma((2,)), dma((2,)),
            dma((3,)), dma((3,)), dma((3,)), dma((3,)), dma((15,)), dma((15,)), dma, dma, dma((7,)), dma((7,)),
        ],
        compiler_params=pltpu.CompilerParams(
            collective_id=0, has_side_effects=True, vmem_limit_bytes=16 * 1024 * 1024
        ),
    )(partial_features, validation_sketches)


def solution(mesh):
    in_specs = (P("dp", None), P(), P("dp", "col"), P("col", None), P(), P("dp"), P("dp", "col"))
    out_specs = P("dp", None)
    return jax.shard_map(
        on_device, mesh=mesh, in_specs=in_specs, out_specs=out_specs, check_vma=False
    )
```

```python
import functools
import math

import jax
import jax.numpy as jnp
from jax import lax
from jax.experimental import pallas as pl
from jax.experimental.pallas import tpu as pltpu
from jax.sharding import PartitionSpec as P

PA = 128
PB = 64
EX_DEV = 8
MESH = pl.DeviceIdType.MESH

epsilon = 1e-06

BF = jnp.bfloat16
F32 = jnp.float32

STEP = 512
OWN = EX_DEV * PB
ROWS = OWN + 2 * PB


def nt(x, y):
    return lax.dot_general(x, y, (((1,), (1,)), ((), ())), preferred_element_type=F32)


def local_kernel(
    lat_h, down_h, grad_h, sketch_h, rank_h, seg_h, gt,
    lat, down, grad, sketch, rank, seg, masked, side, local_sem, grad_sem,
):
    steps = grad.shape[0]
    first = lax.axis_index("dp") * EX_DEV - 1

    small = [
        pltpu.make_async_copy(src, dst, local_sem.at[n])
        for n, (src, dst) in enumerate(
            ((down_h, down), (rank_h, rank), (seg_h, seg), (lat_h, lat), (sketch_h, sketch))
        )
    ]
    for cp in small:
        cp.start()

    def grad_copy(n):
        return pltpu.make_async_copy(grad_h.at[pl.ds(n * STEP, STEP), :], grad.at[n], grad_sem.at[n])

    for n in range(steps):
        grad_copy(n).start()
    gt[...] = jnp.zeros_like(gt)
    for cp in small[:4]:
        cp.wait()

    def rank_step(n, carry):
        rows = pl.ds(pl.multiple_of(n * STEP, STEP), STEP)
        hidden = nt(down[...], lat[rows, :]).astype(BF)
        rank_side = lax.dot_general(
            rank[...], hidden, (((0,), (0,)), ((), ())), preferred_element_type=F32
        ).astype(BF).astype(F32)
        ids = seg[n] - first
        for e in range(1, EX_DEV + 1):
            masked[n, (e - 1) * PB : e * PB, :] = jnp.where(ids == e, rank_side, 0.0).astype(BF)
        masked[n, OWN : OWN + PB, :] = jnp.zeros((PB, STEP), BF)
        masked[n, OWN + PB : ROWS, :] = jnp.where(ids == 0, rank_side, 0.0).astype(BF)
        return carry

    lax.fori_loop(0, steps, rank_step, 0)
    side[steps - 1] = jnp.zeros((PA, STEP), BF)
    small[4].wait()

    def project(n):
        gt[...] += nt(side[n], masked[n]).reshape(2, 4, 2, 8, ROWS)

    def grad_step(n, carry):
        grad_copy(n).wait()
        project(lax.rem(n + steps - 1, steps))
        out_side = jnp.dot(grad[n], sketch[...], preferred_element_type=F32)
        side[n] = out_side.T.astype(BF)
        return carry

    lax.fori_loop(0, steps, grad_step, 0)
    project(steps - 1)


def comm_kernel(
    gt, val_h, out_ref,
    r0, a0, r1, a1, r2, r3, vg, fin, rz, fb, vown_sem,
    s0_send, s0_recv, s1_send, s1_recv, s2_send, s2_recv, s3_send, s3_recv,
    vz_send, vz_recv, vx_send, vx_recv, fz_send, fz_recv, fb_send, fb_recv,
):
    i = lax.axis_index("dp")
    c = lax.axis_index("col")
    zl, x = i // 4, i % 4
    zh, y, core = c // 8, (c // 2) % 4, c % 2
    p = c % 8
    below, above = (i + 15) % 16, (i + 1) % 16

    def at(dp, col):
        return {"dp": dp, "col": col}

    core_peer = at(i, zh * 8 + y * 2 + (1 - core))
    y_peer = [at(i, zh * 8 + ((y + k) % 4) * 2 + core) for k in (1, 2, 3)]
    z_peer = at(i, (1 - zh) * 8 + p)
    p_peer = [at(i, zh * 8 + (p + k) % 8) for k in range(1, 8)]
    vz_peer = [at(((zl + k) % 4) * 4 + x, c) for k in (1, 2, 3)]
    vx_peer = [at(zl * 4 + (x + k) % 4, c) for k in (1, 2, 3)]
    z_col = (1 - zh) * 8 + p

    vown = pltpu.make_async_copy(val_h, vg.at[zl, x], vown_sem)
    vown.start()

    barrier = pltpu.get_barrier_semaphore()
    signals = p_peer + [z_peer] + vz_peer + vx_peer + [at(above, c), at(above, z_col)]
    for peer in signals:
        pl.semaphore_signal(barrier, inc=1, device_id=peer, device_id_type=MESH)
    pl.semaphore_wait(barrier, len(signals))

    def remote(src, dst, send, recv, peer):
        return pltpu.make_async_remote_copy(
            src_ref=src, dst_ref=dst, send_sem=send, recv_sem=recv,
            device_id=peer, device_id_type=MESH,
        )

    def drain(ref, sem):
        pltpu.make_async_copy(ref, ref, sem).wait()

    c0 = remote(gt.at[:, :, 1 - core], r0, s0_send, s0_recv, core_peer)
    c0.start()
    vz = [remote(val_h, vg.at[zl, x], vz_send, vz_recv, vz_peer[k]) for k in range(3)]
    for cp in vz:
        cp.start()

    c0.wait_recv()
    a0[...] = gt[:, :, core] + r0[...]
    c1 = [
        remote(a0.at[:, (y + k) % 4], r1.at[k - 1], s1_send, s1_recv, y_peer[k - 1])
        for k in (1, 2, 3)
    ]
    for cp in c1:
        cp.start()

    vown.wait()
    drain(vg.at[0, 0:3], vz_recv)
    vx = [
        remote(vg.at[:, x], vg.at[:, x], vx_send, vx_recv, vx_peer[k])
        for k in range(3)
    ]
    for cp in vx:
        cp.start()

    drain(r1, s1_recv)
    a1[...] = (a0[:, y] + r1[0]) + (r1[1] + r1[2])
    c2 = remote(a1.at[1 - zh, :, 0:OWN], r2, s2_send, s2_recv, z_peer)
    c3 = [
        remote(a1.at[zh, :, OWN:ROWS], r3.at[0], s3_send, s3_recv, at(below, c)),
        remote(a1.at[1 - zh, :, OWN:ROWS], r3.at[1], s3_send, s3_recv, at(below, z_col)),
    ]
    c2.start()
    for cp in c3:
        cp.start()

    drain(vg.at[0:3], vx_recv)
    val = vg[...].reshape(256, 512)
    val_hi = val.astype(BF)
    val_lo = (val - val_hi.astype(F32)).astype(BF)
    square = val * val
    sq_hi = square.astype(BF)
    sq_lo = (square - sq_hi.astype(F32)).astype(BF)
    ones = jnp.ones((16, 512), BF)
    vsum = nt(ones, sq_hi) + nt(ones, sq_lo)

    c2.wait_recv()
    drain(r3, s3_recv)
    own = a1[zh, :, 0:OWN] + r2[...]
    spill = r3[0] + r3[1]
    own = jnp.concatenate([own[:, : OWN - 128], own[:, OWN - 128 :] + spill], axis=1)

    stack = jnp.concatenate([own[:, e * PB : (e + 1) * PB] for e in range(EX_DEV)], axis=0)
    wide = jnp.concatenate([stack, stack], axis=1)
    wide = jnp.concatenate([wide, wide, wide, wide], axis=1)
    row_a = lax.broadcasted_iota(jnp.int32, (EX_DEV * 8, 512), 0) % 8
    lane_a = lax.broadcasted_iota(jnp.int32, (EX_DEV * 8, 512), 1) // PB
    wide = jnp.where(row_a == lane_a, wide, 0.0)
    hi = wide.astype(BF)
    lo = (wide - hi.astype(F32)).astype(BF)
    dots = nt(hi, val_hi) + (nt(lo, val_hi) + nt(hi, val_lo))
    dots = jnp.sum(dots.reshape(EX_DEV, 8, 256), axis=1)
    own_sq = jnp.sum(jnp.sum(wide * wide, axis=1, keepdims=True).reshape(EX_DEV, 8, 1), axis=1)
    fin[:, 0:256] = dots
    fin[:, 256:384] = jnp.broadcast_to(own_sq, (EX_DEV, 128))
    fin[:, 384:512] = jnp.zeros((EX_DEV, 128), F32)
    fin[0:1, 384:512] = vsum[0:1, 0:128]
    fin[1:2, 384:512] = vsum[0:1, 128:256]

    cz = remote(fin, rz, fz_send, fz_recv, z_peer)
    cz.start()
    cz.wait_recv()
    fb[p] = fin[...] + rz[...]
    cb = [
        remote(fb.at[p], fb.at[p], fb_send, fb_recv, p_peer[k]) for k in range(7)
    ]
    for cp in cb:
        cp.start()
    drain(fb.at[0:7], fb_recv)
    total = ((fb[0] + fb[1]) + (fb[2] + fb[3])) + ((fb[4] + fb[5]) + (fb[6] + fb[7]))
    own_scale = math.sqrt(PA * PB) * lax.rsqrt(total[:, 256:257] + epsilon)
    val_scale = lax.rsqrt(total[0:2, 384:512] + epsilon)
    out_ref[:, 0:128] = total[:, 0:128] * own_scale * val_scale[0:1]
    out_ref[:, 128:256] = total[:, 128:256] * own_scale * val_scale[1:2]
    for ref, sem in (
        (r0, s0_send), (r1, s1_send), (r2, s2_send), (r3, s3_send), (rz, fz_send),
        (vg.at[0, 0:3], vz_send), (vg.at[0:3], vx_send), (fb.at[0:7], fb_send),
    ):
        drain(ref, sem)


def on_device(
    latent,
    adapter_down_matrix,
    output_gradient_rows,
    output_sketch_factor,
    rank_sketch_factor,
    token_example_index,
    validation_sketches,
):
    tokens, columns = output_gradient_rows.shape
    width = latent.shape[1]
    steps = tokens // STEP
    dma = pltpu.SemaphoreType.DMA
    vm = pltpu.VMEM
    any_spec = pl.BlockSpec(memory_space=pl.ANY)
    vmem_spec = pl.BlockSpec(memory_space=pltpu.VMEM)
    partial_features = pl.pallas_call(
        local_kernel,
        out_shape=vm((2, 4, 2, 8, ROWS), F32),
        in_specs=[any_spec] * 6,
        out_specs=vmem_spec,
        scratch_shapes=[
            vm((tokens, width), BF),
            vm((PB, width), BF),
            vm((steps, STEP, columns), BF),
            vm((columns, PA), BF),
            vm((PB, PB), BF),
            vm((steps, 1, STEP), jnp.int32),
            vm((steps, ROWS, STEP), BF),
            vm((steps, PA, STEP), BF),
            dma((5,)), dma((steps,)),
        ],
        compiler_params=pltpu.CompilerParams(vmem_limit_bytes=60 * 1024 * 1024),
    )(
        latent,
        adapter_down_matrix,
        output_gradient_rows,
        output_sketch_factor,
        rank_sketch_factor,
        token_example_index.reshape(steps, 1, STEP),
    )
    return pl.pallas_call(
        comm_kernel,
        out_shape=vm((EX_DEV, 256), F32),
        in_specs=[vmem_spec, any_spec],
        out_specs=vmem_spec,
        scratch_shapes=[
            vm((2, 4, 8, ROWS), F32),
            vm((2, 4, 8, ROWS), F32),
            vm((3, 2, 8, ROWS), F32),
            vm((2, 8, ROWS), F32),
            vm((8, OWN), F32),
            vm((2, 8, 128), F32),
            vm((4, 4, 16, 512), F32),
            vm((8, 512), F32),
            vm((8, 512), F32),
            vm((8, 8, 512), F32),
        ] + [dma] * 17,
        compiler_params=pltpu.CompilerParams(
            collective_id=0, has_side_effects=True, vmem_limit_bytes=16 * 1024 * 1024
        ),
    )(partial_features, validation_sketches)


def solution(mesh):
    in_specs = (P("dp", None), P(), P("dp", "col"), P("col", None), P(), P("dp"), P("dp", "col"))
    out_specs = P("dp", None)
    return jax.shard_map(
        on_device, mesh=mesh, in_specs=in_specs, out_specs=out_specs, check_vma=False
    )
```

```python
import functools
import math

import jax
import jax.numpy as jnp
from jax import lax
from jax.experimental import pallas as pl
from jax.experimental.pallas import tpu as pltpu
from jax.sharding import PartitionSpec as P

PA = 128
PB = 64
EX_DEV = 8
MESH = pl.DeviceIdType.MESH

epsilon = 1e-06

BF = jnp.bfloat16
F32 = jnp.float32

STEP = 512
HALF = 1024
WIDE = 512
OWN = EX_DEV * PB
ROWS = OWN + 2 * PB


def nt(x, y):
    return lax.dot_general(x, y, (((1,), (1,)), ((), ())), preferred_element_type=F32)


def local_kernel(
    lat_h, down_h, grad_h, sketch_h, rank_h, seg_h, gt,
    lat, down, grad, sketch, rank, seg, masked, side, gp, local_sem, grad_sem,
):
    halves, chunks = grad.shape[:2]
    half = grad.shape[2]
    tokens = halves * half
    first = lax.axis_index("dp") * EX_DEV - 1

    small = [
        pltpu.make_async_copy(src, dst, local_sem.at[n])
        for n, (src, dst) in enumerate(
            ((down_h, down), (rank_h, rank), (seg_h, seg), (lat_h, lat), (sketch_h, sketch))
        )
    ]
    for cp in small:
        cp.start()

    def grad_copy(h, n):
        return pltpu.make_async_copy(
            grad_h.at[pl.ds(h * half, half), pl.ds(n * WIDE, WIDE)], grad.at[h, n], grad_sem.at[h, n]
        )

    for h in range(halves):
        for n in range(chunks):
            grad_copy(h, n).start()
    for cp in small[:4]:
        cp.wait()

    hidden = nt(lat[...], down[...]).astype(BF)
    twice = jnp.concatenate([rank[...], rank[...]], axis=1)
    rank_side = jnp.dot(hidden, twice, preferred_element_type=F32).astype(BF).astype(F32)
    for n in range(tokens // STEP):
        at = slice(n * STEP, (n + 1) * STEP)
        turned = rank_side[at].T[0:PB]
        ids = seg[:, at] - first
        for e in range(1, EX_DEV + 1):
            masked[(e - 1) * PB : e * PB, at] = jnp.where(ids == e, turned, 0.0).astype(BF)
        masked[OWN : OWN + PB, at] = jnp.where(ids == 0, turned, 0.0).astype(BF)
    gp[OWN : OWN + PB, :] = jnp.zeros((PB, PA), F32)
    small[4].wait()

    def project(h):
        at = slice(h * half, (h + 1) * half)
        part = jnp.dot(masked[:, at], side[h].astype(BF), preferred_element_type=F32)
        if h == 0:
            gp[0:OWN, :] = part[0:OWN]
            gp[OWN + PB : ROWS, :] = part[OWN:]
        else:
            gp[0:OWN, :] += part[0:OWN]
            gp[OWN + PB : ROWS, :] += part[OWN:]

    for h in range(halves):
        for n in range(chunks):
            grad_copy(h, n).wait()
            if h and n == 1:
                project(h - 1)
            part = jnp.dot(
                grad[h, n], sketch[n * WIDE : (n + 1) * WIDE, :], preferred_element_type=F32
            )
            if n == 0:
                side[h] = part
            else:
                side[h] += part
    project(halves - 1)

    for t in range(ROWS // 128):
        piece = gp[t * 128 : (t + 1) * 128, :].T
        gt[:, :, :, :, t * 128 : (t + 1) * 128] = piece.reshape(2, 4, 2, 8, 128)


def comm_kernel(
    gt, val_h, out_ref,
    r0, a0, r1, a1, r2, r3, vg, fin, rz, fb, vown_sem,
    s0_send, s0_recv, s1_send, s1_recv, s2_send, s2_recv, s3_send, s3_recv,
    vz_send, vz_recv, vx_send, vx_recv, fz_send, fz_recv, fb_send, fb_recv,
):
    i = lax.axis_index("dp")
    c = lax.axis_index("col")
    zl, x = i // 4, i % 4
    zh, y, core = c // 8, (c // 2) % 4, c % 2
    p = c % 8
    below, above = (i + 15) % 16, (i + 1) % 16

    def at(dp, col):
        return {"dp": dp, "col": col}

    core_peer = at(i, zh * 8 + y * 2 + (1 - core))
    y_peer = [at(i, zh * 8 + ((y + k) % 4) * 2 + core) for k in (1, 2, 3)]
    z_peer = at(i, (1 - zh) * 8 + p)
    p_peer = [at(i, zh * 8 + (p + k) % 8) for k in range(1, 8)]
    vz_peer = [at(((zl + k) % 4) * 4 + x, c) for k in (1, 2, 3)]
    vx_peer = [at(zl * 4 + (x + k) % 4, c) for k in (1, 2, 3)]
    z_col = (1 - zh) * 8 + p

    vown = pltpu.make_async_copy(val_h, vg.at[zl, x], vown_sem)
    vown.start()

    barrier = pltpu.get_barrier_semaphore()
    signals = p_peer + [z_peer] + vz_peer + vx_peer + [at(above, c), at(above, z_col)]
    for peer in signals:
        pl.semaphore_signal(barrier, inc=1, device_id=peer, device_id_type=MESH)
    pl.semaphore_wait(barrier, len(signals))

    def remote(src, dst, send, recv, peer):
        return pltpu.make_async_remote_copy(
            src_ref=src, dst_ref=dst, send_sem=send, recv_sem=recv,
            device_id=peer, device_id_type=MESH,
        )

    def drain(ref, sem):
        pltpu.make_async_copy(ref, ref, sem).wait()

    c0 = remote(gt.at[:, :, 1 - core], r0, s0_send, s0_recv, core_peer)
    c0.start()
    vz = [remote(val_h, vg.at[zl, x], vz_send, vz_recv, vz_peer[k]) for k in range(3)]
    for cp in vz:
        cp.start()

    c0.wait_recv()
    a0[...] = gt[:, :, core] + r0[...]
    c1 = [
        remote(a0.at[:, (y + k) % 4], r1.at[k - 1], s1_send, s1_recv, y_peer[k - 1])
        for k in (1, 2, 3)
    ]
    for cp in c1:
        cp.start()

    vown.wait()
    drain(vg.at[0, 0:3], vz_recv)
    vx = [
        remote(vg.at[:, x], vg.at[:, x], vx_send, vx_recv, vx_peer[k])
        for k in range(3)
    ]
    for cp in vx:
        cp.start()

    drain(r1, s1_recv)
    a1[...] = (a0[:, y] + r1[0]) + (r1[1] + r1[2])
    c2 = remote(a1.at[1 - zh, :, 0:OWN], r2, s2_send, s2_recv, z_peer)
    c3 = [
        remote(a1.at[zh, :, OWN:ROWS], r3.at[0], s3_send, s3_recv, at(below, c)),
        remote(a1.at[1 - zh, :, OWN:ROWS], r3.at[1], s3_send, s3_recv, at(below, z_col)),
    ]
    c2.start()
    for cp in c3:
        cp.start()

    drain(vg.at[0:3], vx_recv)
    val = vg[...].reshape(256, 512)
    val_hi = val.astype(BF)
    vsum = nt(jnp.ones((16, 512), BF), (val * val).astype(BF))

    c2.wait_recv()
    drain(r3, s3_recv)
    own = a1[zh, :, 0:OWN] + r2[...]
    spill = r3[0] + r3[1]
    own = jnp.concatenate([own[:, : OWN - 128], own[:, OWN - 128 :] + spill], axis=1)

    stack = jnp.concatenate([own[:, e * PB : (e + 1) * PB] for e in range(EX_DEV)], axis=0)
    wide = jnp.concatenate([stack, stack], axis=1)
    wide = jnp.concatenate([wide, wide, wide, wide], axis=1)
    row_a = lax.broadcasted_iota(jnp.int32, (EX_DEV * 8, 512), 0) % 8
    lane_a = lax.broadcasted_iota(jnp.int32, (EX_DEV * 8, 512), 1) // PB
    wide = jnp.where(row_a == lane_a, wide, 0.0)
    hi = wide.astype(BF)
    lo = (wide - hi.astype(F32)).astype(BF)
    dots = nt(jnp.concatenate([hi, lo], axis=0), val_hi)
    dots = dots[0 : EX_DEV * 8] + dots[EX_DEV * 8 :]
    dots = jnp.sum(dots.reshape(EX_DEV, 8, 256), axis=1)
    own_sq = jnp.sum(jnp.sum(wide * wide, axis=1, keepdims=True).reshape(EX_DEV, 8, 1), axis=1)
    fin[:, 0:256] = dots
    fin[:, 256:384] = jnp.broadcast_to(own_sq, (EX_DEV, 128))
    fin[:, 384:512] = jnp.zeros((EX_DEV, 128), F32)
    fin[0:1, 384:512] = vsum[0:1, 0:128]
    fin[1:2, 384:512] = vsum[0:1, 128:256]

    cz = remote(fin, rz, fz_send, fz_recv, z_peer)
    cz.start()
    cz.wait_recv()
    fb[p] = fin[...] + rz[...]
    cb = [
        remote(fb.at[p], fb.at[p], fb_send, fb_recv, p_peer[k]) for k in range(7)
    ]
    for cp in cb:
        cp.start()
    drain(fb.at[0:7], fb_recv)
    total = ((fb[0] + fb[1]) + (fb[2] + fb[3])) + ((fb[4] + fb[5]) + (fb[6] + fb[7]))
    own_scale = math.sqrt(PA * PB) * lax.rsqrt(total[:, 256:257] + epsilon)
    val_scale = lax.rsqrt(total[0:2, 384:512] + epsilon)
    out_ref[:, 0:128] = total[:, 0:128] * own_scale * val_scale[0:1]
    out_ref[:, 128:256] = total[:, 128:256] * own_scale * val_scale[1:2]
    for ref, sem in (
        (r0, s0_send), (r1, s1_send), (r2, s2_send), (r3, s3_send), (rz, fz_send),
        (vg.at[0, 0:3], vz_send), (vg.at[0:3], vx_send), (fb.at[0:7], fb_send),
    ):
        drain(ref, sem)


def on_device(
    latent,
    adapter_down_matrix,
    output_gradient_rows,
    output_sketch_factor,
    rank_sketch_factor,
    token_example_index,
    validation_sketches,
):
    tokens, columns = output_gradient_rows.shape
    width = latent.shape[1]
    dma = pltpu.SemaphoreType.DMA
    vm = pltpu.VMEM
    any_spec = pl.BlockSpec(memory_space=pl.ANY)
    vmem_spec = pl.BlockSpec(memory_space=pltpu.VMEM)
    partial_features = pl.pallas_call(
        local_kernel,
        out_shape=vm((2, 4, 2, 8, ROWS), F32),
        in_specs=[any_spec] * 6,
        out_specs=vmem_spec,
        scratch_shapes=[
            vm((tokens, width), BF),
            vm((PB, width), BF),
            vm((tokens // HALF, columns // WIDE, HALF, WIDE), BF),
            vm((columns, PA), BF),
            vm((PB, PB), BF),
            vm((1, tokens), jnp.int32),
            vm((OWN + PB, tokens), BF),
            vm((tokens // HALF, HALF, PA), F32),
            vm((ROWS, PA), F32),
            dma((5,)), dma((tokens // HALF, columns // WIDE)),
        ],
        compiler_params=pltpu.CompilerParams(vmem_limit_bytes=60 * 1024 * 1024),
    )(
        latent,
        adapter_down_matrix,
        output_gradient_rows,
        output_sketch_factor,
        rank_sketch_factor,
        token_example_index.reshape(1, tokens),
    )
    return pl.pallas_call(
        comm_kernel,
        out_shape=vm((EX_DEV, 256), F32),
        in_specs=[vmem_spec, any_spec],
        out_specs=vmem_spec,
        scratch_shapes=[
            vm((2, 4, 8, ROWS), F32),
            vm((2, 4, 8, ROWS), F32),
            vm((3, 2, 8, ROWS), F32),
            vm((2, 8, ROWS), F32),
            vm((8, OWN), F32),
            vm((2, 8, 128), F32),
            vm((4, 4, 16, 512), F32),
            vm((8, 512), F32),
            vm((8, 512), F32),
            vm((8, 8, 512), F32),
        ] + [dma] * 17,
        compiler_params=pltpu.CompilerParams(
            collective_id=0, has_side_effects=True, vmem_limit_bytes=16 * 1024 * 1024
        ),
    )(partial_features, validation_sketches)


def solution(mesh):
    in_specs = (P("dp", None), P(), P("dp", "col"), P("col", None), P(), P("dp"), P("dp", "col"))
    out_specs = P("dp", None)
    return jax.shard_map(
        on_device, mesh=mesh, in_specs=in_specs, out_specs=out_specs, check_vma=False
    )
```

```python
import functools
import math

import jax
import jax.numpy as jnp
from jax import lax
from jax.experimental import pallas as pl
from jax.experimental.pallas import tpu as pltpu
from jax.sharding import PartitionSpec as P

PA = 128
PB = 64
EX_DEV = 8
MESH = pl.DeviceIdType.MESH

epsilon = 1e-06

BF = jnp.bfloat16
F32 = jnp.float32

LAT_ROWS = 1024
GRAD_ROWS = 256
STEP = 512
OWN = EX_DEV * PB
ROWS = OWN + 2 * PB


def nt(x, y):
    return lax.dot_general(x, y, (((1,), (1,)), ((), ())), preferred_element_type=F32)


def kernel(
    lat_h, down_h, grad_h, sketch_h, rank_h, seg_h, val_h, out_ref,
    lat, down, grad, sketch, rank, seg, masked, side, gp, gt,
    r0, a0, r1, a1, r2, r3, vg, fin, rz, fb, local_sem, lat_sem, grad_sem, vown_sem,
    s0_send, s0_recv, s1_send, s1_recv, s2_send, s2_recv, s3_send, s3_recv,
    vz_send, vz_recv, vx_send, vx_recv, vf_send, vf_recv, fz_send, fz_recv, fb_send, fb_recv,
):
    i = lax.axis_index("dp")
    c = lax.axis_index("col")
    zl, x = i // 4, i % 4
    zh, y, core = c // 8, (c // 2) % 4, c % 2
    p = c % 8
    below, above = (i + 15) % 16, (i + 1) % 16

    def at(dp, col):
        return {"dp": dp, "col": col}

    core_peer = at(i, zh * 8 + y * 2 + (1 - core))
    y_peer = [at(i, zh * 8 + ((y + k) % 4) * 2 + core) for k in (1, 2, 3)]
    z_peer = at(i, (1 - zh) * 8 + p)
    p_peer = [at(i, zh * 8 + (p + k) % 8) for k in range(1, 8)]
    vz_peer = [at(((zl + k) % 4) * 4 + x, c) for k in (1, 2, 3)]
    vx_peer = [at(zl * 4 + (x + k) % 4, c) for k in (1, 3)]
    z_col = (1 - zh) * 8 + p

    tokens = grad.shape[0]
    first = i * EX_DEV - 1

    def rows(src, dst, sem, n, size):
        span = pl.ds(n * size, size)
        return pltpu.make_async_copy(src.at[span, :], dst.at[span, :], sem.at[n])

    small = [
        pltpu.make_async_copy(src, dst, local_sem.at[n])
        for n, (src, dst) in enumerate(
            ((down_h, down), (rank_h, rank), (seg_h, seg), (sketch_h, sketch))
        )
    ]
    lats = [rows(lat_h, lat, lat_sem, n, LAT_ROWS) for n in range(tokens // LAT_ROWS)]
    grads = [rows(grad_h, grad, grad_sem, n, GRAD_ROWS) for n in range(tokens // GRAD_ROWS)]
    order = iter(grads)

    def more(count):
        for cp in [cp for _, cp in zip(range(count), order)]:
            cp.start()

    for cp in small[:3]:
        cp.start()
    lats[0].start()
    lats[1].start()
    small[3].start()
    more(2)
    vown = pltpu.make_async_copy(val_h, vg.at[zl, x], vown_sem)
    vown.start()
    barrier = pltpu.get_barrier_semaphore()
    signals = p_peer + [z_peer] + vz_peer + vx_peer + [at(above, c), at(above, z_col)]
    for peer in signals:
        pl.semaphore_signal(barrier, inc=1, device_id=peer, device_id_type=MESH)

    for cp in small[:3]:
        cp.wait()

    for n, cp in enumerate(lats):
        cp.wait()
        more(1)
        span = slice(n * LAT_ROWS, (n + 1) * LAT_ROWS)
        hidden = nt(down[...], lat[span, :]).astype(BF)
        rank_side = lax.dot_general(
            rank[...], hidden, (((0,), (0,)), ((), ())), preferred_element_type=F32
        ).astype(BF).astype(F32)
        ids = seg[:, span] - first
        for e in range(1, EX_DEV + 1):
            masked[(e - 1) * PB : e * PB, span] = jnp.where(ids == e, rank_side, 0.0).astype(BF)
        masked[OWN : OWN + PB, span] = jnp.where(ids == 0, rank_side, 0.0).astype(BF)

    small[3].wait()
    gp[OWN : OWN + PB, :] = jnp.zeros((PB, PA), F32)

    def project(n):
        span = slice(n * STEP, (n + 1) * STEP)
        part = jnp.dot(masked[:, span], side[span, :], preferred_element_type=F32)
        if n == 0:
            gp[0:OWN, :] = part[0:OWN]
            gp[OWN + PB : ROWS, :] = part[OWN:]
        else:
            gp[0:OWN, :] += part[0:OWN]
            gp[OWN + PB : ROWS, :] += part[OWN:]

    per = STEP // GRAD_ROWS
    for n in range(tokens // STEP):
        for cp in grads[n * per : (n + 1) * per]:
            cp.wait()
        more(per)
        span = slice(n * STEP, (n + 1) * STEP)
        side[span, :] = jnp.dot(grad[span, :], sketch[...], preferred_element_type=F32).astype(BF)
        if n:
            project(n - 1)
    project(tokens // STEP - 1)

    for t in range(ROWS // 128):
        piece = gp[t * 128 : (t + 1) * 128, :].T
        gt[:, :, :, :, t * 128 : (t + 1) * 128] = piece.reshape(2, 4, 2, 8, 128)

    pl.semaphore_wait(barrier, len(signals))

    def remote(src, dst, send, recv, peer):
        return pltpu.make_async_remote_copy(
            src_ref=src, dst_ref=dst, send_sem=send, recv_sem=recv,
            device_id=peer, device_id_type=MESH,
        )

    def drain(ref, sem):
        pltpu.make_async_copy(ref, ref, sem).wait()

    c0 = remote(gt.at[:, :, 1 - core], r0, s0_send, s0_recv, core_peer)
    c0.start()
    vz = [remote(val_h, vg.at[zl, x], vz_send, vz_recv, vz_peer[k]) for k in range(3)]
    for cp in vz:
        cp.start()

    c0.wait_recv()
    a0[...] = gt[:, :, core] + r0[...]
    c1 = [
        remote(a0.at[:, (y + k) % 4], r1.at[k - 1], s1_send, s1_recv, y_peer[k - 1])
        for k in (1, 2, 3)
    ]
    for cp in c1:
        cp.start()

    vown.wait()
    drain(vg.at[0, 0:3], vz_recv)
    vx = [remote(vg.at[:, x], vg.at[:, x], vx_send, vx_recv, peer) for peer in vx_peer]
    for cp in vx:
        cp.start()

    drain(r1, s1_recv)
    a1[...] = (a0[:, y] + r1[0]) + (r1[1] + r1[2])
    c2 = remote(a1.at[1 - zh, :, 0:OWN], r2, s2_send, s2_recv, z_peer)
    c3 = [
        remote(a1.at[zh, :, OWN:ROWS], r3.at[0], s3_send, s3_recv, at(below, c)),
        remote(a1.at[1 - zh, :, OWN:ROWS], r3.at[1], s3_send, s3_recv, at(below, z_col)),
    ]
    c2.start()
    for cp in c3:
        cp.start()

    drain(vg.at[0:2], vx_recv)
    left, right = (x + 3) % 4, (x + 1) % 4
    vf = [
        remote(vg.at[0:2, left], vg.at[0:2, left], vf_send, vf_recv, vx_peer[0]),
        remote(vg.at[2:4, right], vg.at[2:4, right], vf_send, vf_recv, vx_peer[1]),
    ]
    for cp in vf:
        cp.start()

    drain(vg.at[0], vf_recv)
    val = vg[...].reshape(256, 512)
    val_hi = val.astype(BF)
    vsum = nt(jnp.ones((16, 512), BF), (val * val).astype(BF))

    c2.wait_recv()
    drain(r3, s3_recv)
    own = a1[zh, :, 0:OWN] + r2[...]
    spill = r3[0] + r3[1]
    own = jnp.concatenate([own[:, : OWN - 128], own[:, OWN - 128 :] + spill], axis=1)

    stack = jnp.concatenate([own[:, e * PB : (e + 1) * PB] for e in range(EX_DEV)], axis=0)
    wide = jnp.concatenate([stack, stack], axis=1)
    wide = jnp.concatenate([wide, wide, wide, wide], axis=1)
    row_a = lax.broadcasted_iota(jnp.int32, (EX_DEV * 8, 512), 0) % 8
    lane_a = lax.broadcasted_iota(jnp.int32, (EX_DEV * 8, 512), 1) // PB
    wide = jnp.where(row_a == lane_a, wide, 0.0)
    hi = wide.astype(BF)
    lo = (wide - hi.astype(F32)).astype(BF)
    dots = nt(jnp.concatenate([hi, lo], axis=0), val_hi)
    dots = dots[0 : EX_DEV * 8] + dots[EX_DEV * 8 :]
    dots = jnp.sum(dots.reshape(EX_DEV, 8, 256), axis=1)
    own_sq = jnp.sum(jnp.sum(wide * wide, axis=1, keepdims=True).reshape(EX_DEV, 8, 1), axis=1)
    fin[:, 0:256] = dots
    fin[:, 256:384] = jnp.broadcast_to(own_sq, (EX_DEV, 128))
    fin[:, 384:512] = jnp.zeros((EX_DEV, 128), F32)
    fin[0:1, 384:512] = vsum[0:1, 0:128]
    fin[1:2, 384:512] = vsum[0:1, 128:256]

    cz = remote(fin, rz, fz_send, fz_recv, z_peer)
    cz.start()
    cz.wait_recv()
    fb[p] = fin[...] + rz[...]
    cb = [
        remote(fb.at[p], fb.at[p], fb_send, fb_recv, p_peer[k]) for k in range(7)
    ]
    for cp in cb:
        cp.start()
    drain(fb.at[0:7], fb_recv)
    total = ((fb[0] + fb[1]) + (fb[2] + fb[3])) + ((fb[4] + fb[5]) + (fb[6] + fb[7]))
    own_scale = math.sqrt(PA * PB) * lax.rsqrt(total[:, 256:257] + epsilon)
    val_scale = lax.rsqrt(total[0:2, 384:512] + epsilon)
    out_ref[:, 0:128] = total[:, 0:128] * own_scale * val_scale[0:1]
    out_ref[:, 128:256] = total[:, 128:256] * own_scale * val_scale[1:2]
    for ref, sem in (
        (r0, s0_send), (r1, s1_send), (r2, s2_send), (r3, s3_send), (rz, fz_send),
        (vg.at[0, 0:3], vz_send), (vg.at[0:2], vx_send), (vg.at[0], vf_send), (fb.at[0:7], fb_send),
    ):
        drain(ref, sem)


def on_device(
    latent,
    adapter_down_matrix,
    output_gradient_rows,
    output_sketch_factor,
    rank_sketch_factor,
    token_example_index,
    validation_sketches,
):
    tokens, columns = output_gradient_rows.shape
    width = latent.shape[1]
    dma = pltpu.SemaphoreType.DMA
    vm = pltpu.VMEM
    return pl.pallas_call(
        kernel,
        out_shape=vm((EX_DEV, 256), F32),
        in_specs=[pl.BlockSpec(memory_space=pl.ANY)] * 7,
        out_specs=pl.BlockSpec(memory_space=pltpu.VMEM),
        scratch_shapes=[
            vm((tokens, width), BF),
            vm((PB, width), BF),
            vm((tokens, columns), BF),
            vm((columns, PA), BF),
            vm((PB, PB), BF),
            vm((1, tokens), jnp.int32),
            vm((OWN + PB, tokens), BF),
            vm((tokens, PA), BF),
            vm((ROWS, PA), F32),
            vm((2, 4, 2, 8, ROWS), F32),
            vm((2, 4, 8, ROWS), F32),
            vm((2, 4, 8, ROWS), F32),
            vm((3, 2, 8, ROWS), F32),
            vm((2, 8, ROWS), F32),
            vm((8, OWN), F32),
            vm((2, 8, 128), F32),
            vm((4, 4, 16, 512), F32),
            vm((8, 512), F32),
            vm((8, 512), F32),
            vm((8, 8, 512), F32),
            dma((4,)), dma((tokens // LAT_ROWS,)), dma((tokens // GRAD_ROWS,)), dma,
        ] + [dma] * 18,
        compiler_params=pltpu.CompilerParams(
            collective_id=0, has_side_effects=True, vmem_limit_bytes=60 * 1024 * 1024
        ),
    )(
        latent,
        adapter_down_matrix,
        output_gradient_rows,
        output_sketch_factor,
        rank_sketch_factor,
        token_example_index.reshape(1, tokens),
        validation_sketches,
    )


def solution(mesh):
    in_specs = (P("dp", None), P(), P("dp", "col"), P("col", None), P(), P("dp"), P("dp", "col"))
    out_specs = P("dp", None)
    return jax.shard_map(
        on_device, mesh=mesh, in_specs=in_specs, out_specs=out_specs, check_vma=False
    )
```

```python
import functools
import math

import jax
import jax.numpy as jnp
from jax import lax
from jax.experimental import pallas as pl
from jax.experimental.pallas import tpu as pltpu
from jax.sharding import PartitionSpec as P

PA = 128
PB = 64
EX_DEV = 8
MESH = pl.DeviceIdType.MESH

epsilon = 1e-06

BF = jnp.bfloat16
F32 = jnp.float32

LAT_ROWS = 1024
GRAD_ROWS = 256
STEP = 512
OWN = EX_DEV * PB
ROWS = OWN + 2 * PB


def nt(x, y):
    return lax.dot_general(x, y, (((1,), (1,)), ((), ())), preferred_element_type=F32)


def kernel(
    lat_h, down_h, grad_h, sketch_h, rank_h, seg_h, val_h, out_ref,
    lat, down, grad, sketch, rank, seg, masked, side, gp, gt,
    r0, a0, r1, a1, r2, r3, vg, fin, rz, fb, local_sem, lat_sem, grad_sem, vown_sem,
    s0_send, s0_recv, s1_send, s1_recv, s2_send, s2_recv, s3_send, s3_recv,
    vz_send, vz_recv, vx_send, vx_recv, vf_send, vf_recv, fz_send, fz_recv, fb_send, fb_recv,
):
    i = lax.axis_index("dp")
    c = lax.axis_index("col")
    zl, x = i // 4, i % 4
    zh, y, core = c // 8, (c // 2) % 4, c % 2
    p = c % 8
    below, above = (i + 15) % 16, (i + 1) % 16

    def at(dp, col):
        return {"dp": dp, "col": col}

    core_peer = at(i, zh * 8 + y * 2 + (1 - core))
    y_peer = [at(i, zh * 8 + ((y + k) % 4) * 2 + core) for k in (1, 2, 3)]
    z_peer = at(i, (1 - zh) * 8 + p)
    p_peer = [at(i, zh * 8 + (p + k) % 8) for k in range(1, 8)]
    vz_peer = [at(((zl + k) % 4) * 4 + x, c) for k in (1, 2, 3)]
    vx_peer = [at(zl * 4 + (x + k) % 4, c) for k in (1, 3)]
    z_col = (1 - zh) * 8 + p

    tokens = grad.shape[0]
    first = i * EX_DEV - 1

    def rows(src, dst, sem, n, size):
        span = pl.ds(n * size, size)
        return pltpu.make_async_copy(src.at[span, :], dst.at[span, :], sem.at[n])

    small = [
        pltpu.make_async_copy(src, dst, local_sem.at[n])
        for n, (src, dst) in enumerate(
            ((down_h, down), (rank_h, rank), (seg_h, seg), (sketch_h, sketch))
        )
    ]
    lats = [rows(lat_h, lat, lat_sem, n, LAT_ROWS) for n in range(tokens // LAT_ROWS)]
    grads = [rows(grad_h, grad, grad_sem, n, GRAD_ROWS) for n in range(tokens // GRAD_ROWS)]
    order = iter(grads)

    def more(count):
        for cp in [cp for _, cp in zip(range(count), order)]:
            cp.start()

    for cp in small[:3]:
        cp.start()
    lats[0].start()
    lats[1].start()
    small[3].start()
    more(2)
    vown = pltpu.make_async_copy(val_h, vg.at[zl, x], vown_sem)
    vown.start()
    barrier = pltpu.get_barrier_semaphore()
    signals = p_peer + [z_peer] + vz_peer + vx_peer + [at(above, c), at(above, z_col)]
    for peer in signals:
        pl.semaphore_signal(barrier, inc=1, device_id=peer, device_id_type=MESH)

    def remote(src, dst, send, recv, peer):
        return pltpu.make_async_remote_copy(
            src_ref=src, dst_ref=dst, send_sem=send, recv_sem=recv,
            device_id=peer, device_id_type=MESH,
        )

    def drain(ref, sem):
        pltpu.make_async_copy(ref, ref, sem).wait()

    def v_begin():
        pl.semaphore_wait(barrier, len(signals))
        for peer in vz_peer:
            remote(val_h, vg.at[zl, x], vz_send, vz_recv, peer).start()

    def v_turn():
        vown.wait()
        drain(vg.at[0, 0:3], vz_recv)
        for peer in vx_peer:
            remote(vg.at[:, x], vg.at[:, x], vx_send, vx_recv, peer).start()

    def v_last():
        drain(vg.at[0:2], vx_recv)
        left, right = (x + 3) % 4, (x + 1) % 4
        remote(vg.at[0:2, left], vg.at[0:2, left], vf_send, vf_recv, vx_peer[0]).start()
        remote(vg.at[2:4, right], vg.at[2:4, right], vf_send, vf_recv, vx_peer[1]).start()

    for cp in small[:3]:
        cp.wait()

    for n, cp in enumerate(lats):
        cp.wait()
        more(1)
        span = slice(n * LAT_ROWS, (n + 1) * LAT_ROWS)
        hidden = nt(down[...], lat[span, :]).astype(BF)
        rank_side = lax.dot_general(
            rank[...], hidden, (((0,), (0,)), ((), ())), preferred_element_type=F32
        ).astype(BF).astype(F32)
        ids = seg[:, span] - first
        for e in range(1, EX_DEV + 1):
            masked[(e - 1) * PB : e * PB, span] = jnp.where(ids == e, rank_side, 0.0).astype(BF)
        masked[OWN : OWN + PB, span] = jnp.where(ids == 0, rank_side, 0.0).astype(BF)

    @pl.when(zh == 1)
    def _():
        v_begin()

    small[3].wait()
    gp[OWN : OWN + PB, :] = jnp.zeros((PB, PA), F32)

    def project(n):
        span = slice(n * STEP, (n + 1) * STEP)
        part = jnp.dot(masked[:, span], side[span, :], preferred_element_type=F32)
        if n == 0:
            gp[0:OWN, :] = part[0:OWN]
            gp[OWN + PB : ROWS, :] = part[OWN:]
        else:
            gp[0:OWN, :] += part[0:OWN]
            gp[OWN + PB : ROWS, :] += part[OWN:]

    per = STEP // GRAD_ROWS
    for n in range(tokens // STEP):
        for cp in grads[n * per : (n + 1) * per]:
            cp.wait()
        more(per)
        span = slice(n * STEP, (n + 1) * STEP)
        side[span, :] = jnp.dot(grad[span, :], sketch[...], preferred_element_type=F32).astype(BF)
        if n:
            project(n - 1)
        if n == 1:

            @pl.when(zh == 1)
            def _():
                v_turn()

    project(tokens // STEP - 1)

    for t in range(ROWS // 128):
        piece = gp[t * 128 : (t + 1) * 128, :].T
        gt[:, :, :, :, t * 128 : (t + 1) * 128] = piece.reshape(2, 4, 2, 8, 128)

    @pl.when(zh == 0)
    def _():
        v_begin()

    c0 = remote(gt.at[:, :, 1 - core], r0, s0_send, s0_recv, core_peer)
    c0.start()

    c0.wait_recv()
    a0[...] = gt[:, :, core] + r0[...]
    c1 = [
        remote(a0.at[:, (y + k) % 4], r1.at[k - 1], s1_send, s1_recv, y_peer[k - 1])
        for k in (1, 2, 3)
    ]
    for cp in c1:
        cp.start()

    @pl.when(zh == 0)
    def _():
        v_turn()

    @pl.when(zh == 1)
    def _():
        v_last()

    drain(r1, s1_recv)
    a1[...] = (a0[:, y] + r1[0]) + (r1[1] + r1[2])
    c2 = remote(a1.at[1 - zh, :, 0:OWN], r2, s2_send, s2_recv, z_peer)
    c3 = [
        remote(a1.at[zh, :, OWN:ROWS], r3.at[0], s3_send, s3_recv, at(below, c)),
        remote(a1.at[1 - zh, :, OWN:ROWS], r3.at[1], s3_send, s3_recv, at(below, z_col)),
    ]
    c2.start()
    for cp in c3:
        cp.start()

    @pl.when(zh == 0)
    def _():
        v_last()

    drain(vg.at[0], vf_recv)
    val = vg[...].reshape(256, 512)
    val_hi = val.astype(BF)
    vsum = nt(jnp.ones((16, 512), BF), (val * val).astype(BF))

    c2.wait_recv()
    drain(r3, s3_recv)
    own = a1[zh, :, 0:OWN] + r2[...]
    spill = r3[0] + r3[1]
    own = jnp.concatenate([own[:, : OWN - 128], own[:, OWN - 128 :] + spill], axis=1)

    stack = jnp.concatenate([own[:, e * PB : (e + 1) * PB] for e in range(EX_DEV)], axis=0)
    wide = jnp.concatenate([stack, stack], axis=1)
    wide = jnp.concatenate([wide, wide, wide, wide], axis=1)
    row_a = lax.broadcasted_iota(jnp.int32, (EX_DEV * 8, 512), 0) % 8
    lane_a = lax.broadcasted_iota(jnp.int32, (EX_DEV * 8, 512), 1) // PB
    wide = jnp.where(row_a == lane_a, wide, 0.0)
    hi = wide.astype(BF)
    lo = (wide - hi.astype(F32)).astype(BF)
    dots = nt(jnp.concatenate([hi, lo], axis=0), val_hi)
    dots = dots[0 : EX_DEV * 8] + dots[EX_DEV * 8 :]
    dots = jnp.sum(dots.reshape(EX_DEV, 8, 256), axis=1)
    own_sq = jnp.sum(jnp.sum(wide * wide, axis=1, keepdims=True).reshape(EX_DEV, 8, 1), axis=1)
    fin[:, 0:256] = dots
    fin[:, 256:384] = jnp.broadcast_to(own_sq, (EX_DEV, 128))
    fin[:, 384:512] = jnp.zeros((EX_DEV, 128), F32)
    fin[0:1, 384:512] = vsum[0:1, 0:128]
    fin[1:2, 384:512] = vsum[0:1, 128:256]

    cz = remote(fin, rz, fz_send, fz_recv, z_peer)
    cz.start()
    cz.wait_recv()
    fb[p] = fin[...] + rz[...]
    cb = [
        remote(fb.at[p], fb.at[p], fb_send, fb_recv, p_peer[k]) for k in range(7)
    ]
    for cp in cb:
        cp.start()
    drain(fb.at[0:7], fb_recv)
    total = ((fb[0] + fb[1]) + (fb[2] + fb[3])) + ((fb[4] + fb[5]) + (fb[6] + fb[7]))
    own_scale = math.sqrt(PA * PB) * lax.rsqrt(total[:, 256:257] + epsilon)
    val_scale = lax.rsqrt(total[0:2, 384:512] + epsilon)
    out_ref[:, 0:128] = total[:, 0:128] * own_scale * val_scale[0:1]
    out_ref[:, 128:256] = total[:, 128:256] * own_scale * val_scale[1:2]
    for ref, sem in (
        (r0, s0_send), (r1, s1_send), (r2, s2_send), (r3, s3_send), (rz, fz_send),
        (vg.at[0, 0:3], vz_send), (vg.at[0:2], vx_send), (vg.at[0], vf_send), (fb.at[0:7], fb_send),
    ):
        drain(ref, sem)


def on_device(
    latent,
    adapter_down_matrix,
    output_gradient_rows,
    output_sketch_factor,
    rank_sketch_factor,
    token_example_index,
    validation_sketches,
):
    tokens, columns = output_gradient_rows.shape
    width = latent.shape[1]
    dma = pltpu.SemaphoreType.DMA
    vm = pltpu.VMEM
    return pl.pallas_call(
        kernel,
        out_shape=vm((EX_DEV, 256), F32),
        in_specs=[pl.BlockSpec(memory_space=pl.ANY)] * 7,
        out_specs=pl.BlockSpec(memory_space=pltpu.VMEM),
        scratch_shapes=[
            vm((tokens, width), BF),
            vm((PB, width), BF),
            vm((tokens, columns), BF),
            vm((columns, PA), BF),
            vm((PB, PB), BF),
            vm((1, tokens), jnp.int32),
            vm((OWN + PB, tokens), BF),
            vm((tokens, PA), BF),
            vm((ROWS, PA), F32),
            vm((2, 4, 2, 8, ROWS), F32),
            vm((2, 4, 8, ROWS), F32),
            vm((2, 4, 8, ROWS), F32),
            vm((3, 2, 8, ROWS), F32),
            vm((2, 8, ROWS), F32),
            vm((8, OWN), F32),
            vm((2, 8, 128), F32),
            vm((4, 4, 16, 512), F32),
            vm((8, 512), F32),
            vm((8, 512), F32),
            vm((8, 8, 512), F32),
            dma((4,)), dma((tokens // LAT_ROWS,)), dma((tokens // GRAD_ROWS,)), dma,
        ] + [dma] * 18,
        compiler_params=pltpu.CompilerParams(
            collective_id=0, has_side_effects=True, vmem_limit_bytes=60 * 1024 * 1024
        ),
    )(
        latent,
        adapter_down_matrix,
        output_gradient_rows,
        output_sketch_factor,
        rank_sketch_factor,
        token_example_index.reshape(1, tokens),
        validation_sketches,
    )


def solution(mesh):
    in_specs = (P("dp", None), P(), P("dp", "col"), P("col", None), P(), P("dp"), P("dp", "col"))
    out_specs = P("dp", None)
    return jax.shard_map(
        on_device, mesh=mesh, in_specs=in_specs, out_specs=out_specs, check_vma=False
    )
```

```python
import functools
import math

import jax
import jax.numpy as jnp
from jax import lax
from jax.experimental import pallas as pl
from jax.experimental.pallas import tpu as pltpu
from jax.sharding import PartitionSpec as P

PA = 128
PB = 64
EX_DEV = 8
MESH = pl.DeviceIdType.MESH

epsilon = 1e-06

BF = jnp.bfloat16
F32 = jnp.float32

LAT_ROWS = 1024
GRAD_ROWS = 256
STEP = 512
OWN = EX_DEV * PB
ROWS = OWN + 2 * PB


def nt(x, y):
    return lax.dot_general(x, y, (((1,), (1,)), ((), ())), preferred_element_type=F32)


def kernel(
    lat_h, down_h, grad_h, sketch_h, rank_h, seg_h, val_h, out_ref,
    lat, down, grad, sketch, rank, seg, masked, side, gp, gt,
    r0, a0, r1, a1, r2, r3, vg, fin, rz, fb, local_sem, lat_sem, grad_sem, vown_sem,
    s0_send, s0_recv, s1_send, s1_recv, s2_send, s2_recv, s3_send, s3_recv,
    vz_send, vz_recv, vx_send, vx_recv, vf_send, vf_recv, fz_send, fz_recv, fb_send, fb_recv,
):
    i = lax.axis_index("dp")
    c = lax.axis_index("col")
    zl, x = i // 4, i % 4
    zh, y, core = c // 8, (c // 2) % 4, c % 2
    p = c % 8
    below, above = (i + 15) % 16, (i + 1) % 16

    def at(dp, col):
        return {"dp": dp, "col": col}

    core_peer = at(i, zh * 8 + y * 2 + (1 - core))
    y_peer = [at(i, zh * 8 + ((y + k) % 4) * 2 + core) for k in (1, 2, 3)]
    z_peer = at(i, (1 - zh) * 8 + p)
    p_peer = [at(i, zh * 8 + (p + k) % 8) for k in range(1, 8)]
    vz_peer = [at(((zl + k) % 4) * 4 + x, c) for k in (1, 2, 3)]
    vx_peer = [at(zl * 4 + (x + k) % 4, c) for k in (1, 3)]
    z_col = (1 - zh) * 8 + p

    tokens = grad.shape[0]
    first = i * EX_DEV - 1

    def rows(src, dst, sem, n, size):
        span = pl.ds(n * size, size)
        return pltpu.make_async_copy(src.at[span, :], dst.at[span, :], sem.at[n])

    small = [
        pltpu.make_async_copy(src, dst, local_sem.at[n])
        for n, (src, dst) in enumerate(
            ((down_h, down), (rank_h, rank), (seg_h, seg), (sketch_h, sketch))
        )
    ]
    lats = [rows(lat_h, lat, lat_sem, n, LAT_ROWS) for n in range(tokens // LAT_ROWS)]
    grads = [rows(grad_h, grad, grad_sem, n, GRAD_ROWS) for n in range(tokens // GRAD_ROWS)]
    order = iter(grads)

    def more(count):
        for cp in [cp for _, cp in zip(range(count), order)]:
            cp.start()

    for cp in small[:3]:
        cp.start()
    lats[0].start()
    lats[1].start()
    small[3].start()
    more(2)
    vown = pltpu.make_async_copy(val_h, vg.at[zl, x], vown_sem)
    vown.start()
    barrier = pltpu.get_barrier_semaphore()
    signals = p_peer + [z_peer] + vz_peer + vx_peer + [at(above, c), at(above, z_col)]
    for peer in signals:
        pl.semaphore_signal(barrier, inc=1, device_id=peer, device_id_type=MESH)

    def remote(src, dst, send, recv, peer):
        return pltpu.make_async_remote_copy(
            src_ref=src, dst_ref=dst, send_sem=send, recv_sem=recv,
            device_id=peer, device_id_type=MESH,
        )

    def drain(ref, sem):
        pltpu.make_async_copy(ref, ref, sem).wait()

    def v_begin():
        pl.semaphore_wait(barrier, len(signals))
        for peer in vz_peer:
            remote(val_h, vg.at[zl, x], vz_send, vz_recv, peer).start()

    def v_turn():
        vown.wait()
        drain(vg.at[0, 0:3], vz_recv)
        for peer in vx_peer:
            remote(vg.at[:, x], vg.at[:, x], vx_send, vx_recv, peer).start()

    def v_last():
        drain(vg.at[0:2], vx_recv)
        left, right = (x + 3) % 4, (x + 1) % 4
        remote(vg.at[0:2, left], vg.at[0:2, left], vf_send, vf_recv, vx_peer[0]).start()
        remote(vg.at[2:4, right], vg.at[2:4, right], vf_send, vf_recv, vx_peer[1]).start()

    for cp in small[:3]:
        cp.wait()

    for n, cp in enumerate(lats):
        cp.wait()
        more(1)
        span = slice(n * LAT_ROWS, (n + 1) * LAT_ROWS)
        hidden = nt(lat[span, :], down[...]).astype(BF)
        rank_side = lax.dot_general(
            rank[...], hidden, (((0,), (1,)), ((), ())), preferred_element_type=F32
        ).astype(BF).astype(F32)
        ids = seg[:, span] - first
        for e in range(1, EX_DEV + 1):
            masked[(e - 1) * PB : e * PB, span] = jnp.where(ids == e, rank_side, 0.0).astype(BF)
        masked[OWN : OWN + PB, span] = jnp.where(ids == 0, rank_side, 0.0).astype(BF)

    @pl.when(zh == 1)
    def _():
        v_begin()

    small[3].wait()
    gp[OWN : OWN + PB, :] = jnp.zeros((PB, PA), F32)

    def project(n):
        span = slice(n * STEP, (n + 1) * STEP)
        part = jnp.dot(masked[:, span], side[span, :], preferred_element_type=F32)
        if n == 0:
            gp[0:OWN, :] = part[0:OWN]
            gp[OWN + PB : ROWS, :] = part[OWN:]
        else:
            gp[0:OWN, :] += part[0:OWN]
            gp[OWN + PB : ROWS, :] += part[OWN:]

    per = STEP // GRAD_ROWS
    for n in range(tokens // STEP):
        for cp in grads[n * per : (n + 1) * per]:
            cp.wait()
        more(per)
        span = slice(n * STEP, (n + 1) * STEP)
        side[span, :] = jnp.dot(grad[span, :], sketch[...], preferred_element_type=F32).astype(BF)
        if n:
            project(n - 1)
        if n == 2:

            @pl.when(zh == 1)
            def _():
                v_turn()

    project(tokens // STEP - 1)

    for t in range(ROWS // 128):
        piece = gp[t * 128 : (t + 1) * 128, :].T
        gt[:, :, :, :, t * 128 : (t + 1) * 128] = piece.reshape(2, 4, 2, 8, 128)

    @pl.when(zh == 0)
    def _():
        v_begin()

    c0 = remote(gt.at[:, :, 1 - core], r0, s0_send, s0_recv, core_peer)
    c0.start()

    c0.wait_recv()
    a0[...] = gt[:, :, core] + r0[...]
    c1 = [
        remote(a0.at[:, (y + k) % 4], r1.at[k - 1], s1_send, s1_recv, y_peer[k - 1])
        for k in (1, 2, 3)
    ]
    for cp in c1:
        cp.start()

    @pl.when(zh == 0)
    def _():
        v_turn()

    @pl.when(zh == 1)
    def _():
        v_last()

    drain(r1, s1_recv)
    a1[...] = (a0[:, y] + r1[0]) + (r1[1] + r1[2])
    c2 = remote(a1.at[1 - zh, :, 0:OWN], r2, s2_send, s2_recv, z_peer)
    c3 = [
        remote(a1.at[zh, :, OWN:ROWS], r3.at[0], s3_send, s3_recv, at(below, c)),
        remote(a1.at[1 - zh, :, OWN:ROWS], r3.at[1], s3_send, s3_recv, at(below, z_col)),
    ]
    c2.start()
    for cp in c3:
        cp.start()

    @pl.when(zh == 0)
    def _():
        v_last()

    drain(vg.at[0], vf_recv)
    val = vg[...].reshape(256, 512)
    val_hi = val.astype(BF)
    ones = jnp.ones((16, 512), BF)
    vsum = nt(ones, (val * val).astype(BF))

    c2.wait_recv()
    drain(r3, s3_recv)
    own = a1[zh, :, 0:OWN] + r2[...]
    spill = r3[0] + r3[1]
    own = jnp.concatenate([own[:, : OWN - 128], own[:, OWN - 128 :] + spill], axis=1)

    stack = jnp.concatenate([own[:, e * PB : (e + 1) * PB] for e in range(EX_DEV)], axis=0)
    wide = jnp.concatenate([stack, stack], axis=1)
    wide = jnp.concatenate([wide, wide, wide, wide], axis=1)
    row_a = lax.broadcasted_iota(jnp.int32, (EX_DEV * 8, 512), 0) % 8
    lane_a = lax.broadcasted_iota(jnp.int32, (EX_DEV * 8, 512), 1) // PB
    wide = jnp.where(row_a == lane_a, wide, 0.0)
    hi = wide.astype(BF)
    lo = (wide - hi.astype(F32)).astype(BF)
    dots = nt(jnp.concatenate([hi, lo], axis=0), val_hi)
    dots = dots[0 : EX_DEV * 8] + dots[EX_DEV * 8 :]
    dots = jnp.sum(dots.reshape(EX_DEV, 8, 256), axis=1)
    fin[:, 0:256] = dots
    fin[:, 256:384] = jnp.zeros((8, 128), F32)
    fin[0:1, 256:384] = vsum[0:1, 0:128]
    fin[1:2, 256:384] = vsum[0:1, 128:256]
    fin[2:3, 256 : 256 + EX_DEV * 8] = nt(ones, (wide * wide).astype(BF))[0:1]

    cz = remote(fin, rz, fz_send, fz_recv, z_peer)
    cz.start()
    cz.wait_recv()
    fb[p] = fin[...] + rz[...]
    cb = [
        remote(fb.at[p], fb.at[p], fb_send, fb_recv, p_peer[k]) for k in range(7)
    ]
    for cp in cb:
        cp.start()
    drain(fb.at[0:7], fb_recv)
    total = ((fb[0] + fb[1]) + (fb[2] + fb[3])) + ((fb[4] + fb[5]) + (fb[6] + fb[7]))
    tail = total[:, 256:384]
    lanes = lax.broadcasted_iota(jnp.int32, (EX_DEV, 128), 1) // 8
    slots = lax.broadcasted_iota(jnp.int32, (EX_DEV, 128), 0)
    own_sq = jnp.sum(jnp.where(lanes == slots, tail[2:3], 0.0), axis=1, keepdims=True)
    own_scale = math.sqrt(PA * PB) * lax.rsqrt(own_sq + epsilon)
    val_scale = lax.rsqrt(tail[0:2] + epsilon)
    out_ref[:, 0:128] = total[:, 0:128] * own_scale * val_scale[0:1]
    out_ref[:, 128:256] = total[:, 128:256] * own_scale * val_scale[1:2]
    for ref, sem in (
        (r0, s0_send), (r1, s1_send), (r2, s2_send), (r3, s3_send), (rz, fz_send),
        (vg.at[0, 0:3], vz_send), (vg.at[0:2], vx_send), (vg.at[0], vf_send), (fb.at[0:7], fb_send),
    ):
        drain(ref, sem)


def on_device(
    latent,
    adapter_down_matrix,
    output_gradient_rows,
    output_sketch_factor,
    rank_sketch_factor,
    token_example_index,
    validation_sketches,
):
    tokens, columns = output_gradient_rows.shape
    width = latent.shape[1]
    dma = pltpu.SemaphoreType.DMA
    vm = pltpu.VMEM
    return pl.pallas_call(
        kernel,
        out_shape=vm((EX_DEV, 256), F32),
        in_specs=[pl.BlockSpec(memory_space=pl.ANY)] * 7,
        out_specs=pl.BlockSpec(memory_space=pltpu.VMEM),
        scratch_shapes=[
            vm((tokens, width), BF),
            vm((PB, width), BF),
            vm((tokens, columns), BF),
            vm((columns, PA), BF),
            vm((PB, PB), BF),
            vm((1, tokens), jnp.int32),
            vm((OWN + PB, tokens), BF),
            vm((tokens, PA), BF),
            vm((ROWS, PA), F32),
            vm((2, 4, 2, 8, ROWS), F32),
            vm((2, 4, 8, ROWS), F32),
            vm((2, 4, 8, ROWS), F32),
            vm((3, 2, 8, ROWS), F32),
            vm((2, 8, ROWS), F32),
            vm((8, OWN), F32),
            vm((2, 8, 128), F32),
            vm((4, 4, 16, 512), F32),
            vm((8, 384), F32),
            vm((8, 384), F32),
            vm((8, 8, 384), F32),
            dma((4,)), dma((tokens // LAT_ROWS,)), dma((tokens // GRAD_ROWS,)), dma,
        ] + [dma] * 18,
        compiler_params=pltpu.CompilerParams(
            collective_id=0, has_side_effects=True, vmem_limit_bytes=60 * 1024 * 1024
        ),
    )(
        latent,
        adapter_down_matrix,
        output_gradient_rows,
        output_sketch_factor,
        rank_sketch_factor,
        token_example_index.reshape(1, tokens),
        validation_sketches,
    )


def solution(mesh):
    in_specs = (P("dp", None), P(), P("dp", "col"), P("col", None), P(), P("dp"), P("dp", "col"))
    out_specs = P("dp", None)
    return jax.shard_map(
        on_device, mesh=mesh, in_specs=in_specs, out_specs=out_specs, check_vma=False
    )
```

```python
import functools
import math

import jax
import jax.numpy as jnp
from jax import lax
from jax.experimental import pallas as pl
from jax.experimental.pallas import tpu as pltpu
from jax.sharding import PartitionSpec as P

PA = 128
PB = 64
EX_DEV = 8
MESH = pl.DeviceIdType.MESH

epsilon = 1e-06

BF = jnp.bfloat16
F32 = jnp.float32

LAT_ROWS = 1024
GRAD_ROWS = 256
STEP = 512
OWN = EX_DEV * PB
ROWS = OWN + 2 * PB


def nt(x, y):
    return lax.dot_general(x, y, (((1,), (1,)), ((), ())), preferred_element_type=F32)


def kernel(
    lat_h, down_h, grad_h, sketch_h, rank_h, seg_h, val_h, out_ref,
    lat, down, grad, sketch, rank, seg, masked, side, gp, gt,
    r0, a0, r1, a1, r2, r3, vg, fin, rz, fb, local_sem, lat_sem, grad_sem, vown_sem,
    s0_send, s0_recv, s1_send, s1_recv, s2_send, s2_recv, s3_send, s3_recv,
    vz_send, vz_recv, vx_send, vx_recv, vf_send, vf_recv, fz_send, fz_recv, fb_send, fb_recv,
):
    i = lax.axis_index("dp")
    c = lax.axis_index("col")
    zl, x = i // 4, i % 4
    zh, y, core = c // 8, (c // 2) % 4, c % 2
    p = c % 8
    below, above = (i + 15) % 16, (i + 1) % 16

    def at(dp, col):
        return {"dp": dp, "col": col}

    core_peer = at(i, zh * 8 + y * 2 + (1 - core))
    y_peer = [at(i, zh * 8 + ((y + k) % 4) * 2 + core) for k in (1, 2, 3)]
    z_peer = at(i, (1 - zh) * 8 + p)
    p_peer = [at(i, zh * 8 + (p + k) % 8) for k in range(1, 8)]
    vz_peer = [at(((zl + k) % 4) * 4 + x, c) for k in (1, 2, 3)]
    vx_peer = [at(zl * 4 + (x + k) % 4, c) for k in (1, 3)]
    z_col = (1 - zh) * 8 + p

    tokens = grad.shape[0]
    first = i * EX_DEV - 1

    def rows(src, dst, sem, n, size):
        span = pl.ds(n * size, size)
        return pltpu.make_async_copy(src.at[span, :], dst.at[span, :], sem.at[n])

    small = [
        pltpu.make_async_copy(src, dst, local_sem.at[n])
        for n, (src, dst) in enumerate(
            ((down_h, down), (rank_h, rank), (seg_h, seg), (sketch_h, sketch))
        )
    ]
    lats = [rows(lat_h, lat, lat_sem, n, LAT_ROWS) for n in range(tokens // LAT_ROWS)]
    grads = [rows(grad_h, grad, grad_sem, n, GRAD_ROWS) for n in range(tokens // GRAD_ROWS)]
    order = iter(grads)

    def more(count):
        for cp in [cp for _, cp in zip(range(count), order)]:
            cp.start()

    for cp in small[:3]:
        cp.start()
    lats[0].start()
    lats[1].start()
    small[3].start()
    more(4)
    vown = pltpu.make_async_copy(val_h, vg.at[zl, x], vown_sem)
    vown.start()
    barrier = pltpu.get_barrier_semaphore()
    signals = p_peer + [z_peer] + vz_peer + vx_peer + [at(above, c), at(above, z_col)]
    for peer in signals:
        pl.semaphore_signal(barrier, inc=1, device_id=peer, device_id_type=MESH)

    def remote(src, dst, send, recv, peer):
        return pltpu.make_async_remote_copy(
            src_ref=src, dst_ref=dst, send_sem=send, recv_sem=recv,
            device_id=peer, device_id_type=MESH,
        )

    def drain(ref, sem):
        pltpu.make_async_copy(ref, ref, sem).wait()

    def v_begin():
        pl.semaphore_wait(barrier, len(signals))
        for peer in vz_peer:
            remote(val_h, vg.at[zl, x], vz_send, vz_recv, peer).start()

    def v_turn():
        vown.wait()
        drain(vg.at[0, 0:3], vz_recv)
        for peer in vx_peer:
            remote(vg.at[:, x], vg.at[:, x], vx_send, vx_recv, peer).start()

    def v_last():
        drain(vg.at[0:2], vx_recv)
        left, right = (x + 3) % 4, (x + 1) % 4
        remote(vg.at[0:2, left], vg.at[0:2, left], vf_send, vf_recv, vx_peer[0]).start()
        remote(vg.at[2:4, right], vg.at[2:4, right], vf_send, vf_recv, vx_peer[1]).start()

    for cp in small[:3]:
        cp.wait()

    for n, cp in enumerate(lats):
        cp.wait()
        more(1)
        span = slice(n * LAT_ROWS, (n + 1) * LAT_ROWS)
        hidden = nt(lat[span, :], down[...]).astype(BF)
        rank_side = lax.dot_general(
            rank[...], hidden, (((0,), (1,)), ((), ())), preferred_element_type=F32
        ).astype(BF).astype(F32)
        ids = seg[:, span] - first
        for e in range(1, EX_DEV + 1):
            masked[(e - 1) * PB : e * PB, span] = jnp.where(ids == e, rank_side, 0.0).astype(BF)
        masked[OWN : OWN + PB, span] = jnp.where(ids == 0, rank_side, 0.0).astype(BF)

    @pl.when(zh == 1)
    def _():
        v_begin()

    small[3].wait()
    gp[OWN : OWN + PB, :] = jnp.zeros((PB, PA), F32)

    spans = [slice(n * STEP, (n + 1) * STEP) for n in range(tokens // STEP - 1)]
    spans += [slice(tokens - STEP, tokens - STEP // 2), slice(tokens - STEP // 2, tokens)]

    def project(n):
        part = jnp.dot(masked[:, spans[n]], side[spans[n], :], preferred_element_type=F32)
        if n == 0:
            gp[0:OWN, :] = part[0:OWN]
            gp[OWN + PB : ROWS, :] = part[OWN:]
        else:
            gp[0:OWN, :] += part[0:OWN]
            gp[OWN + PB : ROWS, :] += part[OWN:]

    deep = sketch.shape[0] // 2
    for n, span in enumerate(spans):
        for cp in grads[span.start // GRAD_ROWS : span.stop // GRAD_ROWS]:
            cp.wait()
        more((span.stop - span.start) // GRAD_ROWS)
        low = jnp.dot(grad[span, 0:deep], sketch[0:deep, :], preferred_element_type=F32)
        high = jnp.dot(grad[span, deep:], sketch[deep:, :], preferred_element_type=F32)
        side[span, :] = (low + high).astype(BF)
        if n:
            project(n - 1)
        if n == 2:

            @pl.when(zh == 1)
            def _():
                v_turn()

    project(len(spans) - 1)

    for t in range(ROWS // 128):
        piece = gp[t * 128 : (t + 1) * 128, :].T
        gt[:, :, :, :, t * 128 : (t + 1) * 128] = piece.reshape(2, 4, 2, 8, 128)

    @pl.when(zh == 0)
    def _():
        v_begin()

    c0 = remote(gt.at[:, :, 1 - core], r0, s0_send, s0_recv, core_peer)
    c0.start()

    c0.wait_recv()
    a0[...] = gt[:, :, core] + r0[...]
    c1 = [
        remote(a0.at[:, (y + k) % 4], r1.at[k - 1], s1_send, s1_recv, y_peer[k - 1])
        for k in (1, 2, 3)
    ]
    for cp in c1:
        cp.start()

    @pl.when(zh == 0)
    def _():
        v_turn()

    @pl.when(zh == 1)
    def _():
        v_last()

    drain(r1, s1_recv)
    a1[...] = (a0[:, y] + r1[0]) + (r1[1] + r1[2])
    c3 = [
        remote(a1.at[1 - zh, :, OWN:ROWS], r3.at[1], s3_send, s3_recv, at(below, z_col)),
        remote(a1.at[zh, :, OWN:ROWS], r3.at[0], s3_send, s3_recv, at(below, c)),
    ]
    c2 = remote(a1.at[1 - zh, :, 0:OWN], r2, s2_send, s2_recv, z_peer)
    c3[0].start()
    c2.start()
    c3[1].start()

    @pl.when(zh == 0)
    def _():
        v_last()

    drain(vg.at[0], vf_recv)
    val = vg[...].reshape(256, 512)
    val_hi = val.astype(BF)
    ones = jnp.ones((16, 512), BF)
    vsum = nt(ones, (val * val).astype(BF))

    c2.wait_recv()
    drain(r3, s3_recv)
    own = a1[zh, :, 0:OWN] + r2[...]
    spill = r3[0] + r3[1]
    own = jnp.concatenate([own[:, : OWN - 128], own[:, OWN - 128 :] + spill], axis=1)

    stack = jnp.concatenate([own[:, e * PB : (e + 1) * PB] for e in range(EX_DEV)], axis=0)
    wide = jnp.concatenate([stack, stack], axis=1)
    wide = jnp.concatenate([wide, wide, wide, wide], axis=1)
    row_a = lax.broadcasted_iota(jnp.int32, (EX_DEV * 8, 512), 0) % 8
    lane_a = lax.broadcasted_iota(jnp.int32, (EX_DEV * 8, 512), 1) // PB
    wide = jnp.where(row_a == lane_a, wide, 0.0)
    hi = wide.astype(BF)
    lo = (wide - hi.astype(F32)).astype(BF)
    dots = nt(jnp.concatenate([hi, lo], axis=0), val_hi)
    dots = dots[0 : EX_DEV * 8] + dots[EX_DEV * 8 :]
    dots = jnp.sum(dots.reshape(EX_DEV, 8, 256), axis=1)
    fin[:, 0:256] = dots
    fin[:, 256:384] = jnp.zeros((8, 128), F32)
    fin[0:1, 256:384] = vsum[0:1, 0:128]
    fin[1:2, 256:384] = vsum[0:1, 128:256]
    fin[2:3, 256 : 256 + EX_DEV * 8] = nt(ones, (wide * wide).astype(BF))[0:1]

    cz = remote(fin, rz, fz_send, fz_recv, z_peer)
    cz.start()
    cz.wait_recv()
    fb[p] = fin[...] + rz[...]
    cb = [
        remote(fb.at[p], fb.at[p], fb_send, fb_recv, p_peer[k]) for k in range(7)
    ]
    for cp in cb:
        cp.start()
    drain(fb.at[0:7], fb_recv)
    total = ((fb[0] + fb[1]) + (fb[2] + fb[3])) + ((fb[4] + fb[5]) + (fb[6] + fb[7]))
    tail = total[:, 256:384]
    lanes = lax.broadcasted_iota(jnp.int32, (EX_DEV, 128), 1) // 8
    slots = lax.broadcasted_iota(jnp.int32, (EX_DEV, 128), 0)
    own_sq = jnp.sum(jnp.where(lanes == slots, tail[2:3], 0.0), axis=1, keepdims=True)
    own_scale = math.sqrt(PA * PB) * lax.rsqrt(own_sq + epsilon)
    val_scale = lax.rsqrt(tail[0:2] + epsilon)
    out_ref[:, 0:128] = total[:, 0:128] * own_scale * val_scale[0:1]
    out_ref[:, 128:256] = total[:, 128:256] * own_scale * val_scale[1:2]
    for ref, sem in (
        (r0, s0_send), (r1, s1_send), (r2, s2_send), (r3, s3_send), (rz, fz_send),
        (vg.at[0, 0:3], vz_send), (vg.at[0:2], vx_send), (vg.at[0], vf_send), (fb.at[0:7], fb_send),
    ):
        drain(ref, sem)


def on_device(
    latent,
    adapter_down_matrix,
    output_gradient_rows,
    output_sketch_factor,
    rank_sketch_factor,
    token_example_index,
    validation_sketches,
):
    tokens, columns = output_gradient_rows.shape
    width = latent.shape[1]
    dma = pltpu.SemaphoreType.DMA
    vm = pltpu.VMEM
    return pl.pallas_call(
        kernel,
        out_shape=vm((EX_DEV, 256), F32),
        in_specs=[pl.BlockSpec(memory_space=pl.ANY)] * 7,
        out_specs=pl.BlockSpec(memory_space=pltpu.VMEM),
        scratch_shapes=[
            vm((tokens, width), BF),
            vm((PB, width), BF),
            vm((tokens, columns), BF),
            vm((columns, PA), BF),
            vm((PB, PB), BF),
            vm((1, tokens), jnp.int32),
            vm((OWN + PB, tokens), BF),
            vm((tokens, PA), BF),
            vm((ROWS, PA), F32),
            vm((2, 4, 2, 8, ROWS), F32),
            vm((2, 4, 8, ROWS), F32),
            vm((2, 4, 8, ROWS), F32),
            vm((3, 2, 8, ROWS), F32),
            vm((2, 8, ROWS), F32),
            vm((8, OWN), F32),
            vm((2, 8, 128), F32),
            vm((4, 4, 16, 512), F32),
            vm((8, 384), F32),
            vm((8, 384), F32),
            vm((8, 8, 384), F32),
            dma((4,)), dma((tokens // LAT_ROWS,)), dma((tokens // GRAD_ROWS,)), dma,
        ] + [dma] * 18,
        compiler_params=pltpu.CompilerParams(
            collective_id=0, has_side_effects=True, vmem_limit_bytes=60 * 1024 * 1024
        ),
    )(
        latent,
        adapter_down_matrix,
        output_gradient_rows,
        output_sketch_factor,
        rank_sketch_factor,
        token_example_index.reshape(1, tokens),
        validation_sketches,
    )


def solution(mesh):
    in_specs = (P("dp", None), P(), P("dp", "col"), P("col", None), P(), P("dp"), P("dp", "col"))
    out_specs = P("dp", None)
    return jax.shard_map(
        on_device, mesh=mesh, in_specs=in_specs, out_specs=out_specs, check_vma=False
    )
```

```python
import functools
import math

import jax
import jax.numpy as jnp
from jax import lax
from jax.experimental import pallas as pl
from jax.experimental.pallas import tpu as pltpu
from jax.sharding import PartitionSpec as P

PA = 128
PB = 64
EX_DEV = 8
MESH = pl.DeviceIdType.MESH

epsilon = 1e-06

BF = jnp.bfloat16
F32 = jnp.float32

STEP = 512
OWN = EX_DEV * PB
ROWS = OWN + 2 * PB


def nt(x, y):
    return lax.dot_general(x, y, (((1,), (1,)), ((), ())), preferred_element_type=F32)


def kernel(
    lat_h, down_h, grad_h, sketch_h, rank_h, seg_h, val_h, out_ref,
    lat, down, grad, sketch, rank, seg, masked, side, gp, gt,
    r0, a0, r1, a1, r2, r3, vg, fin, rz, fb, local_sem, lat_sem, grad_sem, vown_sem,
    s0_send, s0_recv, s1_send, s1_recv, s2_send, s2_recv, s3_send, s3_recv,
    vz_send, vz_recv, vx_send, vx_recv, vf_send, vf_recv, fz_send, fz_recv, fb_send, fb_recv,
):
    i = lax.axis_index("dp")
    c = lax.axis_index("col")
    zl, x = i // 4, i % 4
    zh, y, core = c // 8, (c // 2) % 4, c % 2
    p = c % 8
    below, above = (i + 15) % 16, (i + 1) % 16

    def at(dp, col):
        return {"dp": dp, "col": col}

    core_peer = at(i, zh * 8 + y * 2 + (1 - core))
    y_peer = [at(i, zh * 8 + ((y + k) % 4) * 2 + core) for k in (1, 2, 3)]
    z_peer = at(i, (1 - zh) * 8 + p)
    p_peer = [at(i, zh * 8 + (p + k) % 8) for k in range(1, 8)]
    vz_peer = [at(((zl + k) % 4) * 4 + x, c) for k in (1, 2, 3)]
    vx_peer = [at(zl * 4 + (x + k) % 4, c) for k in (1, 3)]
    z_col = (1 - zh) * 8 + p

    tokens = grad.shape[0]
    first = i * EX_DEV - 1

    steps = tokens // STEP
    small = [
        pltpu.make_async_copy(src, dst, local_sem.at[n])
        for n, (src, dst) in enumerate(
            ((down_h, down), (rank_h, rank), (seg_h, seg), (sketch_h, sketch))
        )
    ]

    def block(n):
        return pl.ds(pl.multiple_of(n * STEP, STEP), STEP)

    def lat_copy(n):
        return pltpu.make_async_copy(lat_h.at[block(n), :], lat.at[block(n), :], lat_sem.at[n])

    def grad_copy(n):
        return pltpu.make_async_copy(grad_h.at[block(n), :], grad.at[block(n), :], grad_sem.at[n])

    for cp in small[:3]:
        cp.start()
    for n in range(steps):
        lat_copy(n).start()
    small[3].start()
    grad_copy(0).start()
    grad_copy(1).start()
    vown = pltpu.make_async_copy(val_h, vg.at[zl, x], vown_sem)
    vown.start()
    barrier = pltpu.get_barrier_semaphore()
    signals = p_peer + [z_peer] + vz_peer + vx_peer + [at(above, c), at(above, z_col)]
    for peer in signals:
        pl.semaphore_signal(barrier, inc=1, device_id=peer, device_id_type=MESH)

    def remote(src, dst, send, recv, peer):
        return pltpu.make_async_remote_copy(
            src_ref=src, dst_ref=dst, send_sem=send, recv_sem=recv,
            device_id=peer, device_id_type=MESH,
        )

    def drain(ref, sem):
        pltpu.make_async_copy(ref, ref, sem).wait()

    def v_begin():
        pl.semaphore_wait(barrier, len(signals))
        for peer in vz_peer:
            remote(val_h, vg.at[zl, x], vz_send, vz_recv, peer).start()

    def v_turn():
        vown.wait()
        drain(vg.at[0, 0:3], vz_recv)
        for peer in vx_peer:
            remote(vg.at[:, x], vg.at[:, x], vx_send, vx_recv, peer).start()

    def v_last():
        drain(vg.at[0:2], vx_recv)
        left, right = (x + 3) % 4, (x + 1) % 4
        remote(vg.at[0:2, left], vg.at[0:2, left], vf_send, vf_recv, vx_peer[0]).start()
        remote(vg.at[2:4, right], vg.at[2:4, right], vf_send, vf_recv, vx_peer[1]).start()

    for cp in small[:3]:
        cp.wait()

    def rank_step(n, carry):
        lat_copy(n).wait()
        hidden = nt(lat[block(n), :], down[...]).astype(BF)
        rank_side = lax.dot_general(
            rank[...], hidden, (((0,), (1,)), ((), ())), preferred_element_type=F32
        ).astype(BF).astype(F32)
        ids = seg[n] - first
        for e in range(1, EX_DEV + 1):
            masked[n, (e - 1) * PB : e * PB, :] = jnp.where(ids == e, rank_side, 0.0).astype(BF)
        masked[n, OWN : OWN + PB, :] = jnp.where(ids == 0, rank_side, 0.0).astype(BF)
        return carry

    lax.fori_loop(0, steps, rank_step, 0)
    for n in range(2, steps):
        grad_copy(n).start()

    @pl.when(zh == 1)
    def _():
        v_begin()

    small[3].wait()
    gp[...] = jnp.zeros_like(gp)
    side[steps - 1] = jnp.zeros((STEP, PA), BF)

    def project(n):
        part = jnp.dot(masked[n], side[n], preferred_element_type=F32)
        gp[0:OWN, :] += part[0:OWN]
        gp[OWN + PB : ROWS, :] += part[OWN:]

    def grad_step(n, carry):
        grad_copy(n).wait()
        out_side = jnp.dot(grad[block(n), :], sketch[...], preferred_element_type=F32)
        project(lax.rem(n + steps - 1, steps))
        side[n] = out_side.astype(BF)
        return carry

    lax.fori_loop(0, steps, grad_step, 0)

    @pl.when(zh == 1)
    def _():
        v_turn()

    project(steps - 1)

    for t in range(ROWS // 128):
        piece = gp[t * 128 : (t + 1) * 128, :].T
        gt[:, :, :, :, t * 128 : (t + 1) * 128] = piece.reshape(2, 4, 2, 8, 128)

    @pl.when(zh == 0)
    def _():
        v_begin()

    c0 = remote(gt.at[:, :, 1 - core], r0, s0_send, s0_recv, core_peer)
    c0.start()

    c0.wait_recv()
    a0[...] = gt[:, :, core] + r0[...]
    c1 = [
        remote(a0.at[:, (y + k) % 4], r1.at[k - 1], s1_send, s1_recv, y_peer[k - 1])
        for k in (1, 2, 3)
    ]
    for cp in c1:
        cp.start()

    @pl.when(zh == 0)
    def _():
        v_turn()

    @pl.when(zh == 1)
    def _():
        v_last()

    drain(r1, s1_recv)
    a1[...] = (a0[:, y] + r1[0]) + (r1[1] + r1[2])
    c3 = [
        remote(a1.at[1 - zh, :, OWN:ROWS], r3.at[1], s3_send, s3_recv, at(below, z_col)),
        remote(a1.at[zh, :, OWN:ROWS], r3.at[0], s3_send, s3_recv, at(below, c)),
    ]
    c2 = remote(a1.at[1 - zh, :, 0:OWN], r2, s2_send, s2_recv, z_peer)
    c3[0].start()
    c2.start()
    c3[1].start()

    @pl.when(zh == 0)
    def _():
        v_last()

    drain(vg.at[0], vf_recv)
    val = vg[...].reshape(256, 512)
    val_hi = val.astype(BF)
    ones = jnp.ones((16, 512), BF)
    vsum = nt(ones, (val * val).astype(BF))

    c2.wait_recv()
    drain(r3, s3_recv)
    own = a1[zh, :, 0:OWN] + r2[...]
    spill = r3[0] + r3[1]
    own = jnp.concatenate([own[:, : OWN - 128], own[:, OWN - 128 :] + spill], axis=1)

    stack = jnp.concatenate([own[:, e * PB : (e + 1) * PB] for e in range(EX_DEV)], axis=0)
    wide = jnp.concatenate([stack, stack], axis=1)
    wide = jnp.concatenate([wide, wide, wide, wide], axis=1)
    row_a = lax.broadcasted_iota(jnp.int32, (EX_DEV * 8, 512), 0) % 8
    lane_a = lax.broadcasted_iota(jnp.int32, (EX_DEV * 8, 512), 1) // PB
    wide = jnp.where(row_a == lane_a, wide, 0.0)
    hi = wide.astype(BF)
    lo = (wide - hi.astype(F32)).astype(BF)
    dots = nt(jnp.concatenate([hi, lo], axis=0), val_hi)
    dots = dots[0 : EX_DEV * 8] + dots[EX_DEV * 8 :]
    dots = jnp.sum(dots.reshape(EX_DEV, 8, 256), axis=1)
    fin[:, 0:256] = dots
    fin[:, 256:384] = jnp.zeros((8, 128), F32)
    fin[0:1, 256:384] = vsum[0:1, 0:128]
    fin[1:2, 256:384] = vsum[0:1, 128:256]
    fin[2:3, 256 : 256 + EX_DEV * 8] = nt(ones, (wide * wide).astype(BF))[0:1]

    cz = remote(fin, rz, fz_send, fz_recv, z_peer)
    cz.start()
    cz.wait_recv()
    fb[p] = fin[...] + rz[...]
    cb = [
        remote(fb.at[p], fb.at[p], fb_send, fb_recv, p_peer[k]) for k in range(7)
    ]
    for cp in cb:
        cp.start()
    drain(fb.at[0:7], fb_recv)
    total = ((fb[0] + fb[1]) + (fb[2] + fb[3])) + ((fb[4] + fb[5]) + (fb[6] + fb[7]))
    tail = total[:, 256:384]
    lanes = lax.broadcasted_iota(jnp.int32, (EX_DEV, 128), 1) // 8
    slots = lax.broadcasted_iota(jnp.int32, (EX_DEV, 128), 0)
    own_sq = jnp.sum(jnp.where(lanes == slots, tail[2:3], 0.0), axis=1, keepdims=True)
    own_scale = math.sqrt(PA * PB) * lax.rsqrt(own_sq + epsilon)
    val_scale = lax.rsqrt(tail[0:2] + epsilon)
    out_ref[:, 0:128] = total[:, 0:128] * own_scale * val_scale[0:1]
    out_ref[:, 128:256] = total[:, 128:256] * own_scale * val_scale[1:2]
    for ref, sem in (
        (r0, s0_send), (r1, s1_send), (r2, s2_send), (r3, s3_send), (rz, fz_send),
        (vg.at[0, 0:3], vz_send), (vg.at[0:2], vx_send), (vg.at[0], vf_send), (fb.at[0:7], fb_send),
    ):
        drain(ref, sem)


def on_device(
    latent,
    adapter_down_matrix,
    output_gradient_rows,
    output_sketch_factor,
    rank_sketch_factor,
    token_example_index,
    validation_sketches,
):
    tokens, columns = output_gradient_rows.shape
    width = latent.shape[1]
    steps = tokens // STEP
    dma = pltpu.SemaphoreType.DMA
    vm = pltpu.VMEM
    return pl.pallas_call(
        kernel,
        out_shape=vm((EX_DEV, 256), F32),
        in_specs=[pl.BlockSpec(memory_space=pl.ANY)] * 7,
        out_specs=pl.BlockSpec(memory_space=pltpu.VMEM),
        scratch_shapes=[
            vm((tokens, width), BF),
            vm((PB, width), BF),
            vm((tokens, columns), BF),
            vm((columns, PA), BF),
            vm((PB, PB), BF),
            vm((steps, 1, STEP), jnp.int32),
            vm((steps, OWN + PB, STEP), BF),
            vm((steps, STEP, PA), BF),
            vm((ROWS, PA), F32),
            vm((2, 4, 2, 8, ROWS), F32),
            vm((2, 4, 8, ROWS), F32),
            vm((2, 4, 8, ROWS), F32),
            vm((3, 2, 8, ROWS), F32),
            vm((2, 8, ROWS), F32),
            vm((8, OWN), F32),
            vm((2, 8, 128), F32),
            vm((4, 4, 16, 512), F32),
            vm((8, 384), F32),
            vm((8, 384), F32),
            vm((8, 8, 384), F32),
            dma((4,)), dma((steps,)), dma((steps,)), dma,
        ] + [dma] * 18,
        compiler_params=pltpu.CompilerParams(
            collective_id=0, has_side_effects=True, vmem_limit_bytes=60 * 1024 * 1024
        ),
    )(
        latent,
        adapter_down_matrix,
        output_gradient_rows,
        output_sketch_factor,
        rank_sketch_factor,
        token_example_index.reshape(steps, 1, STEP),
        validation_sketches,
    )


def solution(mesh):
    in_specs = (P("dp", None), P(), P("dp", "col"), P("col", None), P(), P("dp"), P("dp", "col"))
    out_specs = P("dp", None)
    return jax.shard_map(
        on_device, mesh=mesh, in_specs=in_specs, out_specs=out_specs, check_vma=False
    )
```

```python
import functools
import math

import jax
import jax.numpy as jnp
from jax import lax
from jax.experimental import pallas as pl
from jax.experimental.pallas import tpu as pltpu
from jax.sharding import PartitionSpec as P

PA = 128
PB = 64
EX_DEV = 8
MESH = pl.DeviceIdType.MESH

epsilon = 1e-06

BF = jnp.bfloat16
F32 = jnp.float32

STEP = 512
OWN = EX_DEV * PB
ROWS = OWN + 2 * PB

FAR_FIRST = ((4, 0), (4, 1), (2, 0), (2, 1), (6, 0), (6, 1), (0, 1))


def nt(x, y):
    return lax.dot_general(x, y, (((1,), (1,)), ((), ())), preferred_element_type=F32)


def kernel(
    lat_h, down_h, grad_h, sketch_h, rank_h, seg_h, val_h, out_ref,
    lat, down, grad, sketch, rank, seg, masked, side, gp, gt,
    r0, a0, r1, a1, r2, r3, vg, fin, rz, fb, local_sem, lat_sem, grad_sem, vown_sem,
    s0_send, s0_recv, s1_send, s1_recv, s2_send, s2_recv, s3_send, s3_recv,
    ready, vz_send, vz_recv, vo_send, vo_recv, vx_send, vx_recv, vf_send, vf_recv, fz_send, fz_recv, fb_send, fb_recv,
):
    i = lax.axis_index("dp")
    c = lax.axis_index("col")
    zl, x = i // 4, i % 4
    zh, y, core = c // 8, (c // 2) % 4, c % 2
    p = c % 8
    below, above = (i + 15) % 16, (i + 1) % 16

    def at(dp, col):
        return {"dp": dp, "col": col}

    core_peer = at(i, zh * 8 + y * 2 + (1 - core))
    y_peer = [at(i, zh * 8 + ((y + k) % 4) * 2 + core) for k in (2, 1, 3)]
    z_peer = at(i, (1 - zh) * 8 + p)
    p_peer = [at(i, zh * 8 + (p // 2 * 2 + k) % 8 + (core + j) % 2) for k, j in FAR_FIRST]
    vz_peer = [at(((zl + k) % 4) * 4 + x, c) for k in (2, 1, 3)]
    vo_peer = [at(zl * 4 + (x + k) % 4, c) for k in (2, 1, 3)]
    vx_peer = [at(zl * 4 + (x + k) % 4, c) for k in (1, 3)]
    z_col = (1 - zh) * 8 + p

    tokens = grad.shape[0]
    first = i * EX_DEV - 1

    steps = tokens // STEP
    small = [
        pltpu.make_async_copy(src, dst, local_sem.at[n])
        for n, (src, dst) in enumerate(
            ((down_h, down), (rank_h, rank), (seg_h, seg), (sketch_h, sketch))
        )
    ]

    def block(n):
        return pl.ds(pl.multiple_of(n * STEP, STEP), STEP)

    def lat_copy(n):
        return pltpu.make_async_copy(lat_h.at[block(n), :], lat.at[block(n), :], lat_sem.at[n])

    def grad_copy(n):
        return pltpu.make_async_copy(grad_h.at[block(n), :], grad.at[block(n), :], grad_sem.at[n])

    for cp in small[:3]:
        cp.start()
    for n in range(steps):
        lat_copy(n).start()
    small[3].start()
    grad_copy(0).start()
    grad_copy(1).start()
    vown = pltpu.make_async_copy(val_h, vg.at[0, x], vown_sem)
    vown.start()
    barrier = pltpu.get_barrier_semaphore()
    near = p_peer + vz_peer + vo_peer + [at(above, c)]
    far = [z_peer, at(above, z_col)]
    for peer in near:
        pl.semaphore_signal(barrier, inc=1, device_id=peer, device_id_type=MESH)

    @pl.when(zh == 0)
    def _():
        for peer in far + [at(below, z_col)]:
            pl.semaphore_signal(barrier, inc=1, device_id=peer, device_id_type=MESH)

    def remote(src, dst, send, recv, peer):
        return pltpu.make_async_remote_copy(
            src_ref=src, dst_ref=dst, send_sem=send, recv_sem=recv,
            device_id=peer, device_id_type=MESH,
        )

    def drain(ref, sem):
        pltpu.make_async_copy(ref, ref, sem).wait()

    def v_begin():
        for k, peer in zip((2, 1, 3), vz_peer):
            remote(val_h, vg.at[4 - k, x], vz_send, vz_recv, peer).start()
        for peer in vo_peer:
            remote(val_h, vg.at[0, x], vo_send, vo_recv, peer).start()

    def v_turn():
        drain(vg.at[0, 0:3], vz_recv)
        for peer in vx_peer:
            remote(vg.at[1:4, x], vg.at[1:4, x], vx_send, vx_recv, peer).start()

    def v_last():
        drain(vg.at[1:4, 0:2], vx_recv)
        left, right = (x + 3) % 4, (x + 1) % 4
        for peer, source, half in ((vx_peer[0], left, pl.ds(0, 8)), (vx_peer[1], right, pl.ds(8, 8))):
            part = vg.at[1:4, source, half]
            remote(part, part, vf_send, vf_recv, peer).start()

    for cp in small[:3]:
        cp.wait()

    def rank_step(n, carry):
        lat_copy(n).wait()
        hidden = nt(lat[block(n), :], down[...]).astype(BF)
        rank_side = lax.dot_general(
            rank[...], hidden, (((0,), (1,)), ((), ())), preferred_element_type=F32
        ).astype(BF).astype(F32)
        ids = seg[n] - first
        for e in range(1, EX_DEV + 1):
            masked[n, (e - 1) * PB : e * PB, :] = jnp.where(ids == e, rank_side, 0.0).astype(BF)
        masked[n, OWN : OWN + PB, :] = jnp.where(ids == 0, rank_side, 0.0).astype(BF)
        return carry

    lax.fori_loop(0, steps, rank_step, 0)
    for n in range(2, steps):
        grad_copy(n).start()

    small[3].wait()
    gp[...] = jnp.zeros_like(gp)
    side[steps - 1] = jnp.zeros((STEP, PA), BF)

    def project(n):
        part = jnp.dot(masked[n], side[n], preferred_element_type=F32)
        gp[0:OWN, :] += part[0:OWN]
        gp[OWN + PB : ROWS, :] += part[OWN:]

    def grad_step(n, carry):
        grad_copy(n).wait()
        out_side = jnp.dot(grad[block(n), :], sketch[...], preferred_element_type=F32)
        project(lax.rem(n + steps - 1, steps))
        side[n] = out_side.astype(BF)

        @pl.when((zh == 1) & (n == 0))
        def _():
            pl.semaphore_wait(barrier, len(near) + len(far) + 1)
            v_begin()
            for peer in far:
                pl.semaphore_signal(ready, inc=1, device_id=peer, device_id_type=MESH)

        return carry

    lax.fori_loop(0, steps, grad_step, 0)

    project(steps - 1)

    for t in range(ROWS // 128):
        piece = gp[t * 128 : (t + 1) * 128, :].T
        gt[:, :, :, :, t * 128 : (t + 1) * 128] = piece.reshape(2, 4, 2, 8, 128)

    @pl.when(zh == 0)
    def _():
        pl.semaphore_wait(barrier, len(near))

    c0 = remote(gt.at[:, :, 1 - core], r0, s0_send, s0_recv, core_peer)
    c0.start()

    @pl.when(zh == 0)
    def _():
        v_begin()

    @pl.when(zh == 1)
    def _():
        v_turn()


    c0.wait_recv()
    a0[...] = gt[:, :, core] + r0[...]
    c1 = [
        remote(a0.at[:, (y + k) % 4], r1.at[k - 1], s1_send, s1_recv, peer)
        for k, peer in zip((2, 1, 3), y_peer)
    ]
    for cp in c1:
        cp.start()

    @pl.when(zh == 0)
    def _():
        v_turn()

    @pl.when(zh == 1)
    def _():
        v_last()

    drain(r1, s1_recv)
    a1[...] = (a0[:, y] + r1[0]) + (r1[1] + r1[2])
    c3 = [
        remote(a1.at[1 - zh, :, OWN:ROWS], r3.at[1], s3_send, s3_recv, at(below, z_col)),
        remote(a1.at[zh, :, OWN:ROWS], r3.at[0], s3_send, s3_recv, at(below, c)),
    ]
    c2 = remote(a1.at[1 - zh, :, 0:OWN], r2, s2_send, s2_recv, z_peer)
    @pl.when(zh == 0)
    def _():
        pl.semaphore_wait(ready, len(far))

    c3[0].start()
    c2.start()
    c3[1].start()

    @pl.when(zh == 0)
    def _():
        v_last()

    vown.wait()
    drain(vg.at[0, 0:3], vo_recv)
    drain(vg.at[1:4, 0], vf_recv)
    val = jnp.concatenate([vg[(z - zl + 4) % 4].reshape(64, 512) for z in range(4)], axis=0)
    val_hi = val.astype(BF)
    ones = jnp.ones((16, 512), BF)
    vsum = nt(ones, (val * val).astype(BF))

    c2.wait_recv()
    drain(r3, s3_recv)
    own = a1[zh, :, 0:OWN] + r2[...]
    spill = r3[0] + r3[1]
    own = jnp.concatenate([own[:, : OWN - 128], own[:, OWN - 128 :] + spill], axis=1)

    stack = jnp.concatenate([own[:, e * PB : (e + 1) * PB] for e in range(EX_DEV)], axis=0)
    wide = jnp.concatenate([stack, stack], axis=1)
    wide = jnp.concatenate([wide, wide, wide, wide], axis=1)
    row_a = lax.broadcasted_iota(jnp.int32, (EX_DEV * 8, 512), 0) % 8
    lane_a = lax.broadcasted_iota(jnp.int32, (EX_DEV * 8, 512), 1) // PB
    wide = jnp.where(row_a == lane_a, wide, 0.0)
    hi = wide.astype(BF)
    lo = (wide - hi.astype(F32)).astype(BF)
    dots = nt(jnp.concatenate([hi, lo], axis=0), val_hi)
    dots = dots[0 : EX_DEV * 8] + dots[EX_DEV * 8 :]
    dots = jnp.sum(dots.reshape(EX_DEV, 8, 256), axis=1)
    fin[:, 0:256] = dots
    fin[:, 256:384] = jnp.zeros((8, 128), F32)
    fin[0:1, 256:384] = vsum[0:1, 0:128]
    fin[1:2, 256:384] = vsum[0:1, 128:256]
    fin[2:3, 256 : 256 + EX_DEV * 8] = nt(ones, (wide * wide).astype(BF))[0:1]

    cz = remote(fin, rz, fz_send, fz_recv, z_peer)
    cz.start()
    cz.wait_recv()
    fb[p] = fin[...] + rz[...]
    cb = [
        remote(fb.at[p], fb.at[p], fb_send, fb_recv, p_peer[k]) for k in range(7)
    ]
    for cp in cb:
        cp.start()
    drain(fb.at[0:7], fb_recv)
    total = ((fb[0] + fb[1]) + (fb[2] + fb[3])) + ((fb[4] + fb[5]) + (fb[6] + fb[7]))
    tail = total[:, 256:384]
    lanes = lax.broadcasted_iota(jnp.int32, (EX_DEV, 128), 1) // 8
    slots = lax.broadcasted_iota(jnp.int32, (EX_DEV, 128), 0)
    own_sq = jnp.sum(jnp.where(lanes == slots, tail[2:3], 0.0), axis=1, keepdims=True)
    own_scale = math.sqrt(PA * PB) * lax.rsqrt(own_sq + epsilon)
    val_scale = lax.rsqrt(tail[0:2] + epsilon)
    out_ref[:, 0:128] = total[:, 0:128] * own_scale * val_scale[0:1]
    out_ref[:, 128:256] = total[:, 128:256] * own_scale * val_scale[1:2]
    for ref, sem in (
        (r0, s0_send), (r1, s1_send), (r2, s2_send), (r3, s3_send), (rz, fz_send),
        (vg.at[0, 0:3], vz_send), (vg.at[0, 0:3], vo_send),
        (vg.at[1:4, 0:2], vx_send), (vg.at[1:4, 0], vf_send), (fb.at[0:7], fb_send),
    ):
        drain(ref, sem)


def on_device(
    latent,
    adapter_down_matrix,
    output_gradient_rows,
    output_sketch_factor,
    rank_sketch_factor,
    token_example_index,
    validation_sketches,
):
    tokens, columns = output_gradient_rows.shape
    width = latent.shape[1]
    steps = tokens // STEP
    dma = pltpu.SemaphoreType.DMA
    vm = pltpu.VMEM
    return pl.pallas_call(
        kernel,
        out_shape=vm((EX_DEV, 256), F32),
        in_specs=[pl.BlockSpec(memory_space=pl.ANY)] * 7,
        out_specs=pl.BlockSpec(memory_space=pltpu.VMEM),
        scratch_shapes=[
            vm((tokens, width), BF),
            vm((PB, width), BF),
            vm((tokens, columns), BF),
            vm((columns, PA), BF),
            vm((PB, PB), BF),
            vm((steps, 1, STEP), jnp.int32),
            vm((steps, OWN + PB, STEP), BF),
            vm((steps, STEP, PA), BF),
            vm((ROWS, PA), F32),
            vm((2, 4, 2, 8, ROWS), F32),
            vm((2, 4, 8, ROWS), F32),
            vm((2, 4, 8, ROWS), F32),
            vm((3, 2, 8, ROWS), F32),
            vm((2, 8, ROWS), F32),
            vm((8, OWN), F32),
            vm((2, 8, 128), F32),
            vm((4, 4, 16, 512), F32),
            vm((8, 384), F32),
            vm((8, 384), F32),
            vm((8, 8, 384), F32),
            dma((4,)), dma((steps,)), dma((steps,)), dma,
        ] + [dma] * 8 + [pltpu.SemaphoreType.REGULAR] + [dma] * 12,
        compiler_params=pltpu.CompilerParams(
            collective_id=0, has_side_effects=True, vmem_limit_bytes=60 * 1024 * 1024
        ),
    )(
        latent,
        adapter_down_matrix,
        output_gradient_rows,
        output_sketch_factor,
        rank_sketch_factor,
        token_example_index.reshape(steps, 1, STEP),
        validation_sketches,
    )


def solution(mesh):
    in_specs = (P("dp", None), P(), P("dp", "col"), P("col", None), P(), P("dp"), P("dp", "col"))
    out_specs = P("dp", None)
    return jax.shard_map(
        on_device, mesh=mesh, in_specs=in_specs, out_specs=out_specs, check_vma=False
    )
```

```python
import functools
import math

import jax
import jax.numpy as jnp
from jax import lax
from jax.experimental import pallas as pl
from jax.experimental.pallas import tpu as pltpu
from jax.sharding import PartitionSpec as P

PA = 128
PB = 64
EX_DEV = 8
MESH = pl.DeviceIdType.MESH

epsilon = 1e-06

BF = jnp.bfloat16
F32 = jnp.float32

STEP = 512
OWN = EX_DEV * PB
ROWS = OWN + 2 * PB

FAR_FIRST = ((4, 0), (4, 1), (2, 0), (2, 1), (6, 0), (6, 1), (0, 1))


def nt(x, y):
    return lax.dot_general(x, y, (((1,), (1,)), ((), ())), preferred_element_type=F32)


def kernel(
    lat_h, down_h, grad_h, sketch_h, rank_h, seg_h, val_h, out_ref,
    lat, down, grad, sketch, rank, seg, masked, side, gp, gt,
    r0, a0, r1, a1, r2, r3, vg, fin, rz, fb, local_sem, lat_sem, grad_sem, vown_sem,
    s0_send, s0_recv, s1_send, s1_recv, s2_send, s2_recv, s3_send, s3_recv,
    ready, vz_send, vz_recv, vo_send, vo_recv, vx_send, vx_recv, vf_send, vf_recv, fz_send, fz_recv, fb_send, fb_recv,
):
    i = lax.axis_index("dp")
    c = lax.axis_index("col")
    zl, x = i // 4, i % 4
    zh, y, core = c // 8, (c // 2) % 4, c % 2
    p = c % 8
    below, above = (i + 15) % 16, (i + 1) % 16

    def at(dp, col):
        return {"dp": dp, "col": col}

    core_peer = at(i, zh * 8 + y * 2 + (1 - core))
    y_peer = [at(i, zh * 8 + ((y + k) % 4) * 2 + core) for k in (2, 1, 3)]
    z_peer = at(i, (1 - zh) * 8 + p)
    p_peer = [at(i, zh * 8 + (p // 2 * 2 + k) % 8 + (core + j) % 2) for k, j in FAR_FIRST]
    vz_peer = [at(((zl + k) % 4) * 4 + x, c) for k in (2, 1, 3)]
    vo_peer = [at(zl * 4 + (x + k) % 4, c) for k in (2, 1, 3)]
    vx_peer = [at(zl * 4 + (x + k) % 4, c) for k in (1, 3)]
    z_col = (1 - zh) * 8 + p

    tokens = grad.shape[0]
    first = i * EX_DEV - 1

    steps = tokens // STEP
    small = [
        pltpu.make_async_copy(src, dst, local_sem.at[n])
        for n, (src, dst) in enumerate(
            ((down_h, down), (rank_h, rank), (seg_h, seg), (sketch_h, sketch))
        )
    ]

    def block(n):
        return pl.ds(pl.multiple_of(n * STEP, STEP), STEP)

    def lat_copy(n):
        return pltpu.make_async_copy(lat_h.at[block(n), :], lat.at[block(n), :], lat_sem.at[n])

    def grad_copy(n):
        return pltpu.make_async_copy(grad_h.at[block(n), :], grad.at[block(n), :], grad_sem.at[n])

    for cp in small[:3]:
        cp.start()
    for n in range(steps):
        lat_copy(n).start()
    small[3].start()
    grad_copy(0).start()
    grad_copy(1).start()
    vown = pltpu.make_async_copy(val_h, vg.at[0, x], vown_sem)
    vown.start()
    barrier = pltpu.get_barrier_semaphore()
    near = p_peer + vz_peer + vo_peer + [at(above, c)]
    far = [z_peer, at(above, z_col)]
    for peer in near:
        pl.semaphore_signal(barrier, inc=1, device_id=peer, device_id_type=MESH)

    @pl.when(zh == 0)
    def _():
        for peer in far + [at(below, z_col)]:
            pl.semaphore_signal(barrier, inc=1, device_id=peer, device_id_type=MESH)

    def remote(src, dst, send, recv, peer):
        return pltpu.make_async_remote_copy(
            src_ref=src, dst_ref=dst, send_sem=send, recv_sem=recv,
            device_id=peer, device_id_type=MESH,
        )

    def drain(ref, sem):
        pltpu.make_async_copy(ref, ref, sem).wait()

    def v_begin():
        for k, peer in zip((2, 1, 3), vz_peer):
            remote(val_h, vg.at[4 - k, x], vz_send, vz_recv, peer).start()
        for peer in vo_peer:
            remote(val_h, vg.at[0, x], vo_send, vo_recv, peer).start()

    def v_turn():
        drain(vg.at[0, 0:3], vz_recv)
        for peer in vx_peer:
            remote(vg.at[1:4, x], vg.at[1:4, x], vx_send, vx_recv, peer).start()

    def v_last():
        drain(vg.at[1:4, 0:2], vx_recv)
        left, right = (x + 3) % 4, (x + 1) % 4
        for peer, source, half in ((vx_peer[0], left, pl.ds(0, 8)), (vx_peer[1], right, pl.ds(8, 8))):
            part = vg.at[1:4, source, half]
            remote(part, part, vf_send, vf_recv, peer).start()

    for cp in small[:3]:
        cp.wait()

    def rank_block(n):
        hidden = nt(lat[block(n), :], down[...]).astype(BF)
        rank_side = lax.dot_general(
            rank[...], hidden, (((0,), (1,)), ((), ())), preferred_element_type=F32
        ).astype(BF).astype(F32)
        ids = seg[n] - first
        for e in range(1, EX_DEV + 1):
            masked[n, (e - 1) * PB : e * PB, :] = jnp.where(ids == e, rank_side, 0.0).astype(BF)
        masked[n, OWN : OWN + PB, :] = jnp.where(ids == 0, rank_side, 0.0).astype(BF)

    def rank_step(n, carry):
        lat_copy(2 * n).wait()
        lat_copy(2 * n + 1).wait()
        rank_block(2 * n)
        rank_block(2 * n + 1)
        return carry

    lax.fori_loop(0, steps // 2, rank_step, 0)
    for n in range(2, steps):
        grad_copy(n).start()

    @pl.when(zh == 1)
    def _():
        pl.semaphore_wait(barrier, len(near) + len(far) + 1)
        v_begin()
        for peer in far:
            pl.semaphore_signal(ready, inc=1, device_id=peer, device_id_type=MESH)

    small[3].wait()
    gp[...] = jnp.zeros_like(gp)
    side[steps - 1] = jnp.zeros((STEP, PA), BF)

    def project(n):
        part = jnp.dot(masked[n], side[n], preferred_element_type=F32)
        gp[0:OWN, :] += part[0:OWN]
        gp[OWN + PB : ROWS, :] += part[OWN:]

    def grad_step(n, carry):
        grad_copy(n).wait()
        out_side = jnp.dot(grad[block(n), :], sketch[...], preferred_element_type=F32)
        project(lax.rem(n + steps - 1, steps))
        side[n] = out_side.astype(BF)
        return carry

    lax.fori_loop(0, steps, grad_step, 0)

    project(steps - 1)

    for t in range(ROWS // 128):
        piece = gp[t * 128 : (t + 1) * 128, :].T
        gt[:, :, :, :, t * 128 : (t + 1) * 128] = piece.reshape(2, 4, 2, 8, 128)

    @pl.when(zh == 0)
    def _():
        pl.semaphore_wait(barrier, len(near))

    c0 = remote(gt.at[:, :, 1 - core], r0, s0_send, s0_recv, core_peer)
    c0.start()

    @pl.when(zh == 0)
    def _():
        v_begin()

    @pl.when(zh == 1)
    def _():
        v_turn()


    c0.wait_recv()
    a0[...] = gt[:, :, core] + r0[...]
    c1 = [
        remote(a0.at[:, (y + k) % 4], r1.at[k - 1], s1_send, s1_recv, peer)
        for k, peer in zip((2, 1, 3), y_peer)
    ]
    for cp in c1:
        cp.start()

    @pl.when(zh == 0)
    def _():
        v_turn()

    @pl.when(zh == 1)
    def _():
        v_last()

    drain(r1, s1_recv)
    a1[...] = (a0[:, y] + r1[0]) + (r1[1] + r1[2])
    c3 = [
        remote(a1.at[1 - zh, :, OWN:ROWS], r3.at[1], s3_send, s3_recv, at(below, z_col)),
        remote(a1.at[zh, :, OWN:ROWS], r3.at[0], s3_send, s3_recv, at(below, c)),
    ]
    c2 = remote(a1.at[1 - zh, :, 0:OWN], r2, s2_send, s2_recv, z_peer)
    @pl.when(zh == 0)
    def _():
        pl.semaphore_wait(ready, len(far))

    c3[0].start()
    c2.start()
    c3[1].start()

    @pl.when(zh == 0)
    def _():
        v_last()

    vown.wait()
    drain(vg.at[0, 0:3], vo_recv)
    drain(vg.at[1:4, 0], vf_recv)
    val = jnp.concatenate([vg[(z - zl + 4) % 4].reshape(64, 512) for z in range(4)], axis=0)
    val_hi = val.astype(BF)
    ones = jnp.ones((16, 512), BF)
    vsum = nt(ones, (val * val).astype(BF))

    c2.wait_recv()
    drain(r3, s3_recv)
    own = a1[zh, :, 0:OWN] + r2[...]
    spill = r3[0] + r3[1]
    own = jnp.concatenate([own[:, : OWN - 128], own[:, OWN - 128 :] + spill], axis=1)

    stack = jnp.concatenate([own[:, e * PB : (e + 1) * PB] for e in range(EX_DEV)], axis=0)
    wide = jnp.concatenate([stack, stack], axis=1)
    wide = jnp.concatenate([wide, wide, wide, wide], axis=1)
    row_a = lax.broadcasted_iota(jnp.int32, (EX_DEV * 8, 512), 0) % 8
    lane_a = lax.broadcasted_iota(jnp.int32, (EX_DEV * 8, 512), 1) // PB
    wide = jnp.where(row_a == lane_a, wide, 0.0)
    hi = wide.astype(BF)
    lo = (wide - hi.astype(F32)).astype(BF)
    dots = nt(jnp.concatenate([hi, lo], axis=0), val_hi)
    dots = dots[0 : EX_DEV * 8] + dots[EX_DEV * 8 :]
    dots = jnp.sum(dots.reshape(EX_DEV, 8, 256), axis=1)
    fin[:, 0:256] = dots
    fin[:, 256:384] = jnp.zeros((8, 128), F32)
    fin[0:1, 256:384] = vsum[0:1, 0:128]
    fin[1:2, 256:384] = vsum[0:1, 128:256]
    fin[2:3, 256 : 256 + EX_DEV * 8] = nt(ones, (wide * wide).astype(BF))[0:1]

    cz = remote(fin, rz, fz_send, fz_recv, z_peer)
    cz.start()
    for ref, sem in (
        (r0, s0_send), (r1, s1_send), (r2, s2_send), (r3, s3_send),
        (vg.at[0, 0:3], vz_send), (vg.at[0, 0:3], vo_send),
        (vg.at[1:4, 0:2], vx_send), (vg.at[1:4, 0], vf_send),
    ):
        drain(ref, sem)
    cz.wait_recv()
    fb[p] = fin[...] + rz[...]
    cb = [
        remote(fb.at[p], fb.at[p], fb_send, fb_recv, p_peer[k]) for k in range(7)
    ]
    for cp in cb:
        cp.start()
    drain(fb.at[0:7], fb_recv)
    total = ((fb[0] + fb[1]) + (fb[2] + fb[3])) + ((fb[4] + fb[5]) + (fb[6] + fb[7]))
    tail = total[:, 256:384]
    lanes = lax.broadcasted_iota(jnp.int32, (EX_DEV, 128), 1) // 8
    slots = lax.broadcasted_iota(jnp.int32, (EX_DEV, 128), 0)
    own_sq = jnp.sum(jnp.where(lanes == slots, tail[2:3], 0.0), axis=1, keepdims=True)
    own_scale = math.sqrt(PA * PB) * lax.rsqrt(own_sq + epsilon)
    val_scale = lax.rsqrt(tail[0:2] + epsilon)
    out_ref[:, 0:128] = total[:, 0:128] * own_scale * val_scale[0:1]
    out_ref[:, 128:256] = total[:, 128:256] * own_scale * val_scale[1:2]
    drain(rz, fz_send)
    drain(fb.at[0:7], fb_send)


def on_device(
    latent,
    adapter_down_matrix,
    output_gradient_rows,
    output_sketch_factor,
    rank_sketch_factor,
    token_example_index,
    validation_sketches,
):
    tokens, columns = output_gradient_rows.shape
    width = latent.shape[1]
    steps = tokens // STEP
    dma = pltpu.SemaphoreType.DMA
    vm = pltpu.VMEM
    return pl.pallas_call(
        kernel,
        out_shape=vm((EX_DEV, 256), F32),
        in_specs=[pl.BlockSpec(memory_space=pl.ANY)] * 7,
        out_specs=pl.BlockSpec(memory_space=pltpu.VMEM),
        scratch_shapes=[
            vm((tokens, width), BF),
            vm((PB, width), BF),
            vm((tokens, columns), BF),
            vm((columns, PA), BF),
            vm((PB, PB), BF),
            vm((steps, 1, STEP), jnp.int32),
            vm((steps, OWN + PB, STEP), BF),
            vm((steps, STEP, PA), BF),
            vm((ROWS, PA), F32),
            vm((2, 4, 2, 8, ROWS), F32),
            vm((2, 4, 8, ROWS), F32),
            vm((2, 4, 8, ROWS), F32),
            vm((3, 2, 8, ROWS), F32),
            vm((2, 8, ROWS), F32),
            vm((8, OWN), F32),
            vm((2, 8, 128), F32),
            vm((4, 4, 16, 512), F32),
            vm((8, 384), F32),
            vm((8, 384), F32),
            vm((8, 8, 384), F32),
            dma((4,)), dma((steps,)), dma((steps,)), dma,
        ] + [dma] * 8 + [pltpu.SemaphoreType.REGULAR] + [dma] * 12,
        compiler_params=pltpu.CompilerParams(
            collective_id=0, has_side_effects=True, vmem_limit_bytes=60 * 1024 * 1024
        ),
    )(
        latent,
        adapter_down_matrix,
        output_gradient_rows,
        output_sketch_factor,
        rank_sketch_factor,
        token_example_index.reshape(steps, 1, STEP),
        validation_sketches,
    )


def solution(mesh):
    in_specs = (P("dp", None), P(), P("dp", "col"), P("col", None), P(), P("dp"), P("dp", "col"))
    out_specs = P("dp", None)
    return jax.shard_map(
        on_device, mesh=mesh, in_specs=in_specs, out_specs=out_specs, check_vma=False
    )
```

```python
import functools
import math

import jax
import jax.numpy as jnp
from jax import lax
from jax.experimental import pallas as pl
from jax.experimental.pallas import tpu as pltpu
from jax.sharding import PartitionSpec as P

PA = 128
PB = 64
EX_DEV = 8
MESH = pl.DeviceIdType.MESH

epsilon = 1e-06

BF = jnp.bfloat16
F32 = jnp.float32

STEP = 512
OWN = EX_DEV * PB
ROWS = OWN + 2 * PB

FAR_FIRST = ((4, 0), (4, 1), (2, 0), (2, 1), (6, 0), (6, 1), (0, 1))


def nt(x, y):
    return lax.dot_general(x, y, (((1,), (1,)), ((), ())), preferred_element_type=F32)


def kernel(
    lat_h, down_h, grad_h, sketch_h, rank_h, seg_h, val_h, out_ref,
    lat, down, grad, sketch, rank, seg, masked, side, gp, gt,
    r0, a0, r1, a1, r2, r3, vg, fin, rz, fb, local_sem, lat_sem, grad_sem, vown_sem,
    s0_send, s0_recv, s1_send, s1_recv, s2_send, s2_recv, s3_send, s3_recv,
    ready, vz_send, vz_recv, vo_send, vo_recv, vx_send, vx_recv, vf_send, vf_recv, fz_send, fz_recv, fb_send, fb_recv,
):
    i = lax.axis_index("dp")
    c = lax.axis_index("col")
    zl, x = i // 4, i % 4
    zh, y, core = c // 8, (c // 2) % 4, c % 2
    p = c % 8
    below, above = (i + 15) % 16, (i + 1) % 16

    def at(dp, col):
        return {"dp": dp, "col": col}

    core_peer = at(i, zh * 8 + y * 2 + (1 - core))
    y_peer = [at(i, zh * 8 + ((y + k) % 4) * 2 + core) for k in (2, 1, 3)]
    z_peer = at(i, (1 - zh) * 8 + p)
    p_peer = [at(i, zh * 8 + (p // 2 * 2 + k) % 8 + (core + j) % 2) for k, j in FAR_FIRST]
    vz_peer = [at(((zl + k) % 4) * 4 + x, c) for k in (2, 1, 3)]
    vo_peer = [at(zl * 4 + (x + k) % 4, c) for k in (2, 1, 3)]
    vx_peer = [at(zl * 4 + (x + k) % 4, c) for k in (1, 3)]
    z_col = (1 - zh) * 8 + p

    tokens = grad.shape[0]
    first = i * EX_DEV - 1

    steps = tokens // STEP
    small = [
        pltpu.make_async_copy(src, dst, local_sem.at[n])
        for n, (src, dst) in enumerate(
            ((down_h, down), (rank_h, rank), (seg_h, seg), (sketch_h, sketch))
        )
    ]

    def block(n):
        return pl.ds(pl.multiple_of(n * STEP, STEP), STEP)

    def lat_copy(n):
        return pltpu.make_async_copy(lat_h.at[block(n), :], lat.at[block(n), :], lat_sem.at[n])

    def grad_copy(n):
        return pltpu.make_async_copy(grad_h.at[block(n), :], grad.at[block(n), :], grad_sem.at[n])

    for cp in small[:3]:
        cp.start()
    lat_copy(0).start()
    small[3].start()
    grad_copy(0).start()
    lat_copy(1).start()
    grad_copy(1).start()
    vown = pltpu.make_async_copy(val_h, vg.at[0, x], vown_sem)
    vown.start()
    barrier = pltpu.get_barrier_semaphore()
    near = p_peer + vz_peer + vo_peer + [at(above, c)]
    far = [z_peer, at(above, z_col)]
    for peer in near:
        pl.semaphore_signal(barrier, inc=1, device_id=peer, device_id_type=MESH)

    @pl.when(zh == 0)
    def _():
        for peer in far + [at(below, z_col)]:
            pl.semaphore_signal(barrier, inc=1, device_id=peer, device_id_type=MESH)

    def remote(src, dst, send, recv, peer):
        return pltpu.make_async_remote_copy(
            src_ref=src, dst_ref=dst, send_sem=send, recv_sem=recv,
            device_id=peer, device_id_type=MESH,
        )

    def drain(ref, sem):
        pltpu.make_async_copy(ref, ref, sem).wait()

    def v_begin():
        for k, peer in zip((2, 1, 3), vz_peer):
            remote(val_h, vg.at[4 - k, x], vz_send, vz_recv, peer).start()
        for peer in vo_peer:
            remote(val_h, vg.at[0, x], vo_send, vo_recv, peer).start()

    def v_turn():
        drain(vg.at[0, 0:3], vz_recv)
        for peer in vx_peer:
            remote(vg.at[1:4, x], vg.at[1:4, x], vx_send, vx_recv, peer).start()

    def v_last():
        drain(vg.at[1:4, 0:2], vx_recv)
        left, right = (x + 3) % 4, (x + 1) % 4
        for peer, source, half in ((vx_peer[0], left, pl.ds(0, 8)), (vx_peer[1], right, pl.ds(8, 8))):
            part = vg.at[1:4, source, half]
            remote(part, part, vf_send, vf_recv, peer).start()

    gp[...] = jnp.zeros_like(gp)
    side[steps - 1] = jnp.zeros((STEP, PA), BF)
    masked[steps - 1] = jnp.zeros((OWN + PB, STEP), BF)
    for cp in small:
        cp.wait()

    def project(n):
        part = jnp.dot(masked[n], side[n], preferred_element_type=F32)
        gp[0:OWN, :] += part[0:OWN]
        gp[OWN + PB : ROWS, :] += part[OWN:]

    def local_step(n, carry):
        lat_copy(n).wait()
        grad_copy(n).wait()

        @pl.when(n < steps - 2)
        def _():
            lat_copy(n + 2).start()
            grad_copy(n + 2).start()

        hidden = nt(lat[block(n), :], down[...]).astype(BF)
        out_side = jnp.dot(grad[block(n), :], sketch[...], preferred_element_type=F32)
        rank_side = lax.dot_general(
            rank[...], hidden, (((0,), (1,)), ((), ())), preferred_element_type=F32
        ).astype(BF).astype(F32)
        project(lax.rem(n + steps - 1, steps))
        ids = seg[n] - first
        for e in range(1, EX_DEV + 1):
            masked[n, (e - 1) * PB : e * PB, :] = jnp.where(ids == e, rank_side, 0.0).astype(BF)
        masked[n, OWN : OWN + PB, :] = jnp.where(ids == 0, rank_side, 0.0).astype(BF)
        side[n] = out_side.astype(BF)

        @pl.when((zh == 1) & (n == 0))
        def _():
            pl.semaphore_wait(barrier, len(near) + len(far) + 1)
            v_begin()
            for peer in far:
                pl.semaphore_signal(ready, inc=1, device_id=peer, device_id_type=MESH)

        return carry

    lax.fori_loop(0, steps, local_step, 0)
    project(steps - 1)

    for t in range(ROWS // 128):
        piece = gp[t * 128 : (t + 1) * 128, :].T
        gt[:, :, :, :, t * 128 : (t + 1) * 128] = piece.reshape(2, 4, 2, 8, 128)

    @pl.when(zh == 0)
    def _():
        pl.semaphore_wait(barrier, len(near))

    c0 = remote(gt.at[:, :, 1 - core], r0, s0_send, s0_recv, core_peer)
    c0.start()

    @pl.when(zh == 0)
    def _():
        v_begin()

    @pl.when(zh == 1)
    def _():
        v_turn()


    c0.wait_recv()
    a0[...] = gt[:, :, core] + r0[...]
    c1 = [
        remote(a0.at[:, (y + k) % 4], r1.at[k - 1], s1_send, s1_recv, peer)
        for k, peer in zip((2, 1, 3), y_peer)
    ]
    for cp in c1:
        cp.start()

    @pl.when(zh == 0)
    def _():
        v_turn()

    @pl.when(zh == 1)
    def _():
        v_last()

    drain(r1, s1_recv)
    a1[...] = (a0[:, y] + r1[0]) + (r1[1] + r1[2])
    c3 = [
        remote(a1.at[1 - zh, :, OWN:ROWS], r3.at[1], s3_send, s3_recv, at(below, z_col)),
        remote(a1.at[zh, :, OWN:ROWS], r3.at[0], s3_send, s3_recv, at(below, c)),
    ]
    c2 = remote(a1.at[1 - zh, :, 0:OWN], r2, s2_send, s2_recv, z_peer)
    @pl.when(zh == 0)
    def _():
        pl.semaphore_wait(ready, len(far))

    c3[0].start()
    c2.start()
    c3[1].start()

    @pl.when(zh == 0)
    def _():
        v_last()

    vown.wait()
    drain(vg.at[0, 0:3], vo_recv)
    drain(vg.at[1:4, 0], vf_recv)
    val = jnp.concatenate([vg[(z - zl + 4) % 4].reshape(64, 512) for z in range(4)], axis=0)
    val_hi = val.astype(BF)
    ones = jnp.ones((16, 512), BF)
    vsum = nt(ones, (val * val).astype(BF))

    c2.wait_recv()
    drain(r3, s3_recv)
    own = a1[zh, :, 0:OWN] + r2[...]
    spill = r3[0] + r3[1]
    own = jnp.concatenate([own[:, : OWN - 128], own[:, OWN - 128 :] + spill], axis=1)

    stack = jnp.concatenate([own[:, e * PB : (e + 1) * PB] for e in range(EX_DEV)], axis=0)
    wide = jnp.concatenate([stack, stack], axis=1)
    wide = jnp.concatenate([wide, wide, wide, wide], axis=1)
    row_a = lax.broadcasted_iota(jnp.int32, (EX_DEV * 8, 512), 0) % 8
    lane_a = lax.broadcasted_iota(jnp.int32, (EX_DEV * 8, 512), 1) // PB
    wide = jnp.where(row_a == lane_a, wide, 0.0)
    hi = wide.astype(BF)
    lo = (wide - hi.astype(F32)).astype(BF)
    dots = nt(jnp.concatenate([hi, lo], axis=0), val_hi)
    dots = dots[0 : EX_DEV * 8] + dots[EX_DEV * 8 :]
    dots = jnp.sum(dots.reshape(EX_DEV, 8, 256), axis=1)
    fin[:, 0:256] = dots
    fin[:, 256:384] = jnp.zeros((8, 128), F32)
    fin[0:1, 256:384] = vsum[0:1, 0:128]
    fin[1:2, 256:384] = vsum[0:1, 128:256]
    fin[2:3, 256 : 256 + EX_DEV * 8] = nt(ones, (wide * wide).astype(BF))[0:1]

    cz = remote(fin, rz, fz_send, fz_recv, z_peer)
    cz.start()
    for ref, sem in (
        (r0, s0_send), (r1, s1_send), (r2, s2_send), (r3, s3_send),
        (vg.at[0, 0:3], vz_send), (vg.at[0, 0:3], vo_send),
        (vg.at[1:4, 0:2], vx_send), (vg.at[1:4, 0], vf_send),
    ):
        drain(ref, sem)
    cz.wait_recv()
    fb[p] = fin[...] + rz[...]
    cb = [
        remote(fb.at[p], fb.at[p], fb_send, fb_recv, p_peer[k]) for k in range(7)
    ]
    for cp in cb:
        cp.start()
    drain(fb.at[0:7], fb_recv)
    total = ((fb[0] + fb[1]) + (fb[2] + fb[3])) + ((fb[4] + fb[5]) + (fb[6] + fb[7]))
    tail = total[:, 256:384]
    lanes = lax.broadcasted_iota(jnp.int32, (EX_DEV, 128), 1) // 8
    slots = lax.broadcasted_iota(jnp.int32, (EX_DEV, 128), 0)
    own_sq = jnp.sum(jnp.where(lanes == slots, tail[2:3], 0.0), axis=1, keepdims=True)
    own_scale = math.sqrt(PA * PB) * lax.rsqrt(own_sq + epsilon)
    val_scale = lax.rsqrt(tail[0:2] + epsilon)
    out_ref[:, 0:128] = total[:, 0:128] * own_scale * val_scale[0:1]
    out_ref[:, 128:256] = total[:, 128:256] * own_scale * val_scale[1:2]
    drain(rz, fz_send)
    drain(fb.at[0:7], fb_send)


def on_device(
    latent,
    adapter_down_matrix,
    output_gradient_rows,
    output_sketch_factor,
    rank_sketch_factor,
    token_example_index,
    validation_sketches,
):
    tokens, columns = output_gradient_rows.shape
    width = latent.shape[1]
    steps = tokens // STEP
    dma = pltpu.SemaphoreType.DMA
    vm = pltpu.VMEM
    return pl.pallas_call(
        kernel,
        out_shape=vm((EX_DEV, 256), F32),
        in_specs=[pl.BlockSpec(memory_space=pl.ANY)] * 7,
        out_specs=pl.BlockSpec(memory_space=pltpu.VMEM),
        scratch_shapes=[
            vm((tokens, width), BF),
            vm((PB, width), BF),
            vm((tokens, columns), BF),
            vm((columns, PA), BF),
            vm((PB, PB), BF),
            vm((steps, 1, STEP), jnp.int32),
            vm((steps, OWN + PB, STEP), BF),
            vm((steps, STEP, PA), BF),
            vm((ROWS, PA), F32),
            vm((2, 4, 2, 8, ROWS), F32),
            vm((2, 4, 8, ROWS), F32),
            vm((2, 4, 8, ROWS), F32),
            vm((3, 2, 8, ROWS), F32),
            vm((2, 8, ROWS), F32),
            vm((8, OWN), F32),
            vm((2, 8, 128), F32),
            vm((4, 4, 16, 512), F32),
            vm((8, 384), F32),
            vm((8, 384), F32),
            vm((8, 8, 384), F32),
            dma((4,)), dma((steps,)), dma((steps,)), dma,
        ] + [dma] * 8 + [pltpu.SemaphoreType.REGULAR] + [dma] * 12,
        compiler_params=pltpu.CompilerParams(
            collective_id=0, has_side_effects=True, vmem_limit_bytes=60 * 1024 * 1024
        ),
    )(
        latent,
        adapter_down_matrix,
        output_gradient_rows,
        output_sketch_factor,
        rank_sketch_factor,
        token_example_index.reshape(steps, 1, STEP),
        validation_sketches,
    )


def solution(mesh):
    in_specs = (P("dp", None), P(), P("dp", "col"), P("col", None), P(), P("dp"), P("dp", "col"))
    out_specs = P("dp", None)
    return jax.shard_map(
        on_device, mesh=mesh, in_specs=in_specs, out_specs=out_specs, check_vma=False
    )
```

```python
import functools
import math

import jax
import jax.numpy as jnp
from jax import lax
from jax.experimental import pallas as pl
from jax.experimental.pallas import tpu as pltpu
from jax.sharding import PartitionSpec as P

PA = 128
PB = 64
EX_DEV = 8
MESH = pl.DeviceIdType.MESH

epsilon = 1e-06

BF = jnp.bfloat16
F32 = jnp.float32

STEP = 512
OWN = EX_DEV * PB
ROWS = OWN + 2 * PB

FAR_FIRST = ((4, 0), (4, 1), (2, 0), (2, 1), (6, 0), (6, 1), (0, 1))


def nt(x, y):
    return lax.dot_general(x, y, (((1,), (1,)), ((), ())), preferred_element_type=F32)


def kernel(
    lat_h, down_h, grad_h, sketch_h, rank_h, seg_h, val_h, out_ref,
    lat, down, grad, sketch, rank, seg, masked, side, gp, gt,
    r0, a0, r1, a1, r2, r3, vg, vb, fin, rz, fb, local_sem, lat_sem, grad_sem, vown_sem,
    s0_send, s0_far, s0_near, s1_send, s1_far, s1_near, s2_send, s2_recv, s3_send, s3_recv,
    ready, vz_send, vz_recv, vo_send, vo_recv, vx_send, vx_recv, vf_send, vf_recv, fz_send, fz_recv, fb_send, fb_recv,
):
    i = lax.axis_index("dp")
    c = lax.axis_index("col")
    zl, x = i // 4, i % 4
    zh, y, core = c // 8, (c // 2) % 4, c % 2
    p = c % 8
    below, above = (i + 15) % 16, (i + 1) % 16

    def at(dp, col):
        return {"dp": dp, "col": col}

    core_peer = at(i, zh * 8 + y * 2 + (1 - core))
    y_peer = [at(i, zh * 8 + ((y + k) % 4) * 2 + core) for k in (2, 1, 3)]
    z_peer = at(i, (1 - zh) * 8 + p)
    p_peer = [at(i, zh * 8 + (p // 2 * 2 + k) % 8 + (core + j) % 2) for k, j in FAR_FIRST]
    vz_peer = [at(((zl + k) % 4) * 4 + x, c) for k in (2, 1, 3)]
    vo_peer = [at(zl * 4 + (x + k) % 4, c) for k in (2, 1, 3)]
    vx_peer = [at(zl * 4 + (x + k) % 4, c) for k in (1, 3)]
    z_col = (1 - zh) * 8 + p

    tokens = grad.shape[0]
    first = i * EX_DEV - 1

    steps = tokens // STEP
    small = [
        pltpu.make_async_copy(src, dst, local_sem.at[n])
        for n, (src, dst) in enumerate(
            ((down_h, down), (rank_h, rank), (seg_h, seg), (sketch_h, sketch))
        )
    ]

    def block(n):
        return pl.ds(pl.multiple_of(n * STEP, STEP), STEP)

    def lat_copy(n):
        return pltpu.make_async_copy(lat_h.at[block(n), :], lat.at[block(n), :], lat_sem.at[n])

    def grad_copy(n):
        return pltpu.make_async_copy(grad_h.at[block(n), :], grad.at[block(n), :], grad_sem.at[n])

    for cp in small[:3]:
        cp.start()
    lat_copy(0).start()
    small[3].start()
    grad_copy(0).start()
    lat_copy(1).start()
    grad_copy(1).start()
    vown = pltpu.make_async_copy(val_h, vg.at[0, x], vown_sem)
    vown.start()
    barrier = pltpu.get_barrier_semaphore()
    near = p_peer + vz_peer + vo_peer + [at(above, c)]
    far = [z_peer, at(above, z_col)]
    for peer in near:
        pl.semaphore_signal(barrier, inc=1, device_id=peer, device_id_type=MESH)

    @pl.when(zh == 0)
    def _():
        for peer in far + [at(below, z_col)]:
            pl.semaphore_signal(barrier, inc=1, device_id=peer, device_id_type=MESH)

    def remote(src, dst, send, recv, peer):
        return pltpu.make_async_remote_copy(
            src_ref=src, dst_ref=dst, send_sem=send, recv_sem=recv,
            device_id=peer, device_id_type=MESH,
        )

    def drain(ref, sem):
        pltpu.make_async_copy(ref, ref, sem).wait()

    def v_begin():
        for k, peer in zip((2, 1, 3), vz_peer):
            remote(val_h, vg.at[4 - k, x], vz_send, vz_recv, peer).start()
        for peer in vo_peer:
            remote(val_h, vg.at[0, x], vo_send, vo_recv, peer).start()

    def v_turn():
        drain(vg.at[0, 0:3], vz_recv)
        for peer in vx_peer:
            remote(vg.at[1:4, x], vg.at[1:4, x], vx_send, vx_recv, peer).start()

    left, right, opposite = (x + 3) % 4, (x + 1) % 4, (x + 2) % 4

    def v_cast(source):
        for z in range(4):
            vb[z, source] = vg[(z - zl + 4) % 4, source].astype(BF)

    def v_last():
        drain(vg.at[1:4, 0:2], vx_recv)
        for peer, source, half in ((vx_peer[0], left, pl.ds(0, 8)), (vx_peer[1], right, pl.ds(8, 8))):
            part = vg.at[1:4, source, half]
            remote(part, part, vf_send, vf_recv, peer).start()
        vown.wait()
        drain(vg.at[0, 0:3], vo_recv)
        v_cast(x)
        v_cast(left)
        v_cast(right)

    gp[...] = jnp.zeros_like(gp)
    side[steps - 1] = jnp.zeros((STEP, PA), BF)
    masked[steps - 1] = jnp.zeros((OWN + PB, STEP), BF)
    for cp in small:
        cp.wait()

    def project(n):
        part = jnp.dot(masked[n], side[n], preferred_element_type=F32)
        gp[0:OWN, :] += part[0:OWN]
        gp[OWN + PB : ROWS, :] += part[OWN:]

    def local_step(n, carry):
        lat_copy(n).wait()
        grad_copy(n).wait()

        @pl.when(n < steps - 2)
        def _():
            lat_copy(n + 2).start()
            grad_copy(n + 2).start()

        hidden = nt(lat[block(n), :], down[...]).astype(BF)
        out_side = jnp.dot(grad[block(n), :], sketch[...], preferred_element_type=F32)
        rank_side = lax.dot_general(
            rank[...], hidden, (((0,), (1,)), ((), ())), preferred_element_type=F32
        ).astype(BF).astype(F32)
        project(lax.rem(n + steps - 1, steps))
        ids = seg[n] - first
        for e in range(1, EX_DEV + 1):
            masked[n, (e - 1) * PB : e * PB, :] = jnp.where(ids == e, rank_side, 0.0).astype(BF)
        masked[n, OWN : OWN + PB, :] = jnp.where(ids == 0, rank_side, 0.0).astype(BF)
        side[n] = out_side.astype(BF)

        @pl.when((zh == 1) & (n == 0))
        def _():
            pl.semaphore_wait(barrier, len(near) + len(far) + 1)
            v_begin()
            for peer in far:
                pl.semaphore_signal(ready, inc=1, device_id=peer, device_id_type=MESH)

        return carry

    lax.fori_loop(0, steps, local_step, 0)
    project(steps - 1)

    for t in range(ROWS // 128):
        piece = gp[t * 128 : (t + 1) * 128, :].T
        gt[:, :, :, :, t * 128 : (t + 1) * 128] = piece.reshape(2, 4, 2, 8, 128)

    @pl.when(zh == 0)
    def _():
        pl.semaphore_wait(barrier, len(near))

    c0 = [
        remote(gt.at[z, :, 1 - core], r0.at[z], s0_send, sem, core_peer)
        for z, sem in ((1 - zh, s0_far), (zh, s0_near))
    ]
    for cp in c0:
        cp.start()

    @pl.when(zh == 0)
    def _():
        v_begin()

    @pl.when(zh == 1)
    def _():
        v_turn()

    for n, (z, sem) in enumerate(((1 - zh, s1_far), (zh, s1_near))):
        c0[n].wait_recv()
        a0[z] = gt[z, :, core] + r0[z]
        for k, peer in zip((2, 1, 3), y_peer):
            remote(a0.at[z, (y + k) % 4], r1.at[n, k - 1], s1_send, sem, peer).start()

    drain(r1.at[0], s1_far)
    a1[0] = (a0[1 - zh, y] + r1[0, 0]) + (r1[0, 1] + r1[0, 2])

    @pl.when(zh == 0)
    def _():
        pl.semaphore_wait(ready, len(far))

    remote(a1.at[0, :, OWN:ROWS], r3.at[1], s3_send, s3_recv, at(below, z_col)).start()
    c2 = remote(a1.at[0, :, 0:OWN], r2, s2_send, s2_recv, z_peer)
    c2.start()
    drain(r1.at[1], s1_near)
    a1[1] = (a0[zh, y] + r1[1, 0]) + (r1[1, 1] + r1[1, 2])
    remote(a1.at[1, :, OWN:ROWS], r3.at[0], s3_send, s3_recv, at(below, c)).start()

    @pl.when(zh == 0)
    def _():
        v_turn()

    v_last()

    drain(vg.at[1:4, 0], vf_recv)
    v_cast(opposite)
    val_hi = vb[...].reshape(256, 512)
    val = val_hi.astype(F32)
    ones = jnp.ones((16, 512), BF)
    vsum = nt(ones, (val * val).astype(BF))

    c2.wait_recv()
    drain(r3, s3_recv)
    own = a1[1, :, 0:OWN] + r2[...]
    spill = r3[0] + r3[1]
    own = jnp.concatenate([own[:, : OWN - 128], own[:, OWN - 128 :] + spill], axis=1)

    stack = jnp.concatenate([own[:, e * PB : (e + 1) * PB] for e in range(EX_DEV)], axis=0)
    wide = jnp.concatenate([stack, stack], axis=1)
    wide = jnp.concatenate([wide, wide, wide, wide], axis=1)
    row_a = lax.broadcasted_iota(jnp.int32, (EX_DEV * 8, 512), 0) % 8
    lane_a = lax.broadcasted_iota(jnp.int32, (EX_DEV * 8, 512), 1) // PB
    wide = jnp.where(row_a == lane_a, wide, 0.0)
    hi = wide.astype(BF)
    lo = (wide - hi.astype(F32)).astype(BF)
    dots = nt(jnp.concatenate([hi, lo], axis=0), val_hi)
    dots = dots[0 : EX_DEV * 8] + dots[EX_DEV * 8 :]
    dots = jnp.sum(dots.reshape(EX_DEV, 8, 256), axis=1)
    fin[:, 0:256] = dots
    fin[:, 256:384] = jnp.zeros((8, 128), F32)
    fin[0:1, 256:384] = vsum[0:1, 0:128]
    fin[1:2, 256:384] = vsum[0:1, 128:256]
    fin[2:3, 256 : 256 + EX_DEV * 8] = nt(ones, (wide * wide).astype(BF))[0:1]

    cz = remote(fin, rz, fz_send, fz_recv, z_peer)
    cz.start()
    for ref, sem in (
        (r0, s0_send), (r1, s1_send), (r2, s2_send), (r3, s3_send),
        (vg.at[0, 0:3], vz_send), (vg.at[0, 0:3], vo_send),
        (vg.at[1:4, 0:2], vx_send), (vg.at[1:4, 0], vf_send),
    ):
        drain(ref, sem)
    cz.wait_recv()
    fb[p] = fin[...] + rz[...]
    cb = [
        remote(fb.at[p], fb.at[p], fb_send, fb_recv, p_peer[k]) for k in range(7)
    ]
    for cp in cb:
        cp.start()
    drain(fb.at[0:7], fb_recv)
    total = ((fb[0] + fb[1]) + (fb[2] + fb[3])) + ((fb[4] + fb[5]) + (fb[6] + fb[7]))
    tail = total[:, 256:384]
    lanes = lax.broadcasted_iota(jnp.int32, (EX_DEV, 128), 1) // 8
    slots = lax.broadcasted_iota(jnp.int32, (EX_DEV, 128), 0)
    own_sq = jnp.sum(jnp.where(lanes == slots, tail[2:3], 0.0), axis=1, keepdims=True)
    own_scale = math.sqrt(PA * PB) * lax.rsqrt(own_sq + epsilon)
    val_scale = lax.rsqrt(tail[0:2] + epsilon)
    out_ref[:, 0:128] = total[:, 0:128] * own_scale * val_scale[0:1]
    out_ref[:, 128:256] = total[:, 128:256] * own_scale * val_scale[1:2]
    drain(rz, fz_send)
    drain(fb.at[0:7], fb_send)


def on_device(
    latent,
    adapter_down_matrix,
    output_gradient_rows,
    output_sketch_factor,
    rank_sketch_factor,
    token_example_index,
    validation_sketches,
):
    tokens, columns = output_gradient_rows.shape
    width = latent.shape[1]
    steps = tokens // STEP
    dma = pltpu.SemaphoreType.DMA
    vm = pltpu.VMEM
    return pl.pallas_call(
        kernel,
        out_shape=vm((EX_DEV, 256), F32),
        in_specs=[pl.BlockSpec(memory_space=pl.ANY)] * 7,
        out_specs=pl.BlockSpec(memory_space=pltpu.VMEM),
        scratch_shapes=[
            vm((tokens, width), BF),
            vm((PB, width), BF),
            vm((tokens, columns), BF),
            vm((columns, PA), BF),
            vm((PB, PB), BF),
            vm((steps, 1, STEP), jnp.int32),
            vm((steps, OWN + PB, STEP), BF),
            vm((steps, STEP, PA), BF),
            vm((ROWS, PA), F32),
            vm((2, 4, 2, 8, ROWS), F32),
            vm((2, 4, 8, ROWS), F32),
            vm((2, 4, 8, ROWS), F32),
            vm((2, 3, 8, ROWS), F32),
            vm((2, 8, ROWS), F32),
            vm((8, OWN), F32),
            vm((2, 8, 128), F32),
            vm((4, 4, 16, 512), F32),
            vm((4, 4, 16, 512), BF),
            vm((8, 384), F32),
            vm((8, 384), F32),
            vm((8, 8, 384), F32),
            dma((4,)), dma((steps,)), dma((steps,)), dma,
        ] + [dma] * 10 + [pltpu.SemaphoreType.REGULAR] + [dma] * 12,
        compiler_params=pltpu.CompilerParams(
            collective_id=0, has_side_effects=True, vmem_limit_bytes=60 * 1024 * 1024
        ),
    )(
        latent,
        adapter_down_matrix,
        output_gradient_rows,
        output_sketch_factor,
        rank_sketch_factor,
        token_example_index.reshape(steps, 1, STEP),
        validation_sketches,
    )


def solution(mesh):
    in_specs = (P("dp", None), P(), P("dp", "col"), P("col", None), P(), P("dp"), P("dp", "col"))
    out_specs = P("dp", None)
    return jax.shard_map(
        on_device, mesh=mesh, in_specs=in_specs, out_specs=out_specs, check_vma=False
    )
```

```python
import functools
import math

import jax
import jax.numpy as jnp
from jax import lax
from jax.experimental import pallas as pl
from jax.experimental.pallas import tpu as pltpu
from jax.sharding import PartitionSpec as P

PA = 128
PB = 64
EX_DEV = 8
MESH = pl.DeviceIdType.MESH

epsilon = 1e-06

BF = jnp.bfloat16
F32 = jnp.float32

STEP = 512
OWN = EX_DEV * PB
ROWS = OWN + 2 * PB

FAR_FIRST = ((4, 0), (4, 1), (2, 0), (2, 1), (6, 0), (6, 1), (0, 1))


def nt(x, y):
    return lax.dot_general(x, y, (((1,), (1,)), ((), ())), preferred_element_type=F32)


def kernel(
    lat_h, down_h, grad_h, sketch_h, rank_h, seg_h, val_h, out_ref,
    lat, down, grad, sketch, rank, seg, masked, side, gp, gt,
    r0, a0, r1, a1, r2, r3, vg, fin, rz, fb, local_sem, lat_sem, grad_sem, vown_sem,
    s0_send, s0_recv, s1_send, s1_recv, s2_send, s2_recv, s3_send, s3_recv,
    ready, vz_send, vz_recv, vo_send, vo_recv, vx_send, vx_recv, vd_send, vd_recv, fz_send, fz_recv, fb_send, fb_recv,
):
    i = lax.axis_index("dp")
    c = lax.axis_index("col")
    zl, x = i // 4, i % 4
    zh, y, core = c // 8, (c // 2) % 4, c % 2
    p = c % 8
    below, above = (i + 15) % 16, (i + 1) % 16

    def at(dp, col):
        return {"dp": dp, "col": col}

    core_peer = at(i, zh * 8 + y * 2 + (1 - core))
    y_peer = [at(i, zh * 8 + ((y + k) % 4) * 2 + core) for k in (2, 1, 3)]
    z_peer = at(i, (1 - zh) * 8 + p)
    p_peer = [at(i, zh * 8 + (p // 2 * 2 + k) % 8 + (core + j) % 2) for k, j in FAR_FIRST]
    vz_peer = [at(((zl + k) % 4) * 4 + x, c) for k in (2, 1, 3)]
    vd_peer = [at(((zl + k) % 4) * 4 + (x + 2) % 4, c) for k in (2, 1, 3)]
    vo_peer = [at(zl * 4 + (x + k) % 4, c) for k in (2, 1, 3)]
    vx_peer = [at(zl * 4 + (x + k) % 4, c) for k in (1, 3)]
    z_col = (1 - zh) * 8 + p

    tokens = grad.shape[0]
    first = i * EX_DEV - 1

    steps = tokens // STEP
    small = [
        pltpu.make_async_copy(src, dst, local_sem.at[n])
        for n, (src, dst) in enumerate(
            ((down_h, down), (rank_h, rank), (seg_h, seg), (sketch_h, sketch))
        )
    ]

    def block(n):
        return pl.ds(pl.multiple_of(n * STEP, STEP), STEP)

    def lat_copy(n):
        return pltpu.make_async_copy(lat_h.at[block(n), :], lat.at[block(n), :], lat_sem.at[n])

    def grad_copy(n):
        return pltpu.make_async_copy(grad_h.at[block(n), :], grad.at[block(n), :], grad_sem.at[n])

    for cp in small[:3]:
        cp.start()
    lat_copy(0).start()
    small[3].start()
    grad_copy(0).start()
    lat_copy(1).start()
    grad_copy(1).start()
    vown = pltpu.make_async_copy(val_h, vg.at[0, x], vown_sem)
    vown.start()
    barrier = pltpu.get_barrier_semaphore()
    near = p_peer + vz_peer + vo_peer + vd_peer + [at(above, c)]
    far = [z_peer, at(above, z_col)]
    for peer in near:
        pl.semaphore_signal(barrier, inc=1, device_id=peer, device_id_type=MESH)

    @pl.when(zh == 0)
    def _():
        for peer in far + [at(below, z_col)]:
            pl.semaphore_signal(barrier, inc=1, device_id=peer, device_id_type=MESH)

    def remote(src, dst, send, recv, peer):
        return pltpu.make_async_remote_copy(
            src_ref=src, dst_ref=dst, send_sem=send, recv_sem=recv,
            device_id=peer, device_id_type=MESH,
        )

    def drain(ref, sem):
        pltpu.make_async_copy(ref, ref, sem).wait()

    def v_begin():
        for k, peer in zip((2, 1, 3), vz_peer):
            remote(val_h, vg.at[4 - k, x], vz_send, vz_recv, peer).start()
        for peer in vo_peer:
            remote(val_h, vg.at[0, x], vo_send, vo_recv, peer).start()
        for k, peer in zip((2, 1, 3), vd_peer):
            remote(val_h, vg.at[4 - k, x], vd_send, vd_recv, peer).start()

    def v_turn():
        drain(vg.at[0, 0:3], vz_recv)
        for peer in vx_peer:
            remote(vg.at[1:4, x], vg.at[1:4, x], vx_send, vx_recv, peer).start()

    gp[...] = jnp.zeros_like(gp)
    side[steps - 1] = jnp.zeros((STEP, PA), BF)
    masked[steps - 1] = jnp.zeros((OWN + PB, STEP), BF)
    for cp in small:
        cp.wait()

    def project(n):
        part = jnp.dot(masked[n], side[n], preferred_element_type=F32)
        gp[0:OWN, :] += part[0:OWN]
        gp[OWN + PB : ROWS, :] += part[OWN:]

    def local_step(n, carry):
        lat_copy(n).wait()
        grad_copy(n).wait()

        @pl.when(n < steps - 2)
        def _():
            lat_copy(n + 2).start()
            grad_copy(n + 2).start()

        hidden = nt(lat[block(n), :], down[...]).astype(BF)
        out_side = jnp.dot(grad[block(n), :], sketch[...], preferred_element_type=F32)
        rank_side = lax.dot_general(
            rank[...], hidden, (((0,), (1,)), ((), ())), preferred_element_type=F32
        ).astype(BF).astype(F32)
        project(lax.rem(n + steps - 1, steps))
        ids = seg[n] - first
        for e in range(1, EX_DEV + 1):
            masked[n, (e - 1) * PB : e * PB, :] = jnp.where(ids == e, rank_side, 0.0).astype(BF)
        masked[n, OWN : OWN + PB, :] = jnp.where(ids == 0, rank_side, 0.0).astype(BF)
        side[n] = out_side.astype(BF)

        @pl.when((zh == 1) & (n == 0))
        def _():
            pl.semaphore_wait(barrier, len(near) + len(far) + 1)
            v_begin()
            for peer in far:
                pl.semaphore_signal(ready, inc=1, device_id=peer, device_id_type=MESH)

        return carry

    lax.fori_loop(0, steps, local_step, 0)
    project(steps - 1)

    for t in range(ROWS // 128):
        piece = gp[t * 128 : (t + 1) * 128, :].T
        gt[:, :, :, :, t * 128 : (t + 1) * 128] = piece.reshape(2, 4, 2, 8, 128)

    @pl.when(zh == 0)
    def _():
        pl.semaphore_wait(barrier, len(near))

    c0 = remote(gt.at[:, :, 1 - core], r0, s0_send, s0_recv, core_peer)
    c0.start()

    @pl.when(zh == 0)
    def _():
        v_begin()

    @pl.when(zh == 1)
    def _():
        v_turn()


    c0.wait_recv()
    a0[...] = gt[:, :, core] + r0[...]
    c1 = [
        remote(a0.at[:, (y + k) % 4], r1.at[k - 1], s1_send, s1_recv, peer)
        for k, peer in zip((2, 1, 3), y_peer)
    ]
    for cp in c1:
        cp.start()

    @pl.when(zh == 0)
    def _():
        v_turn()

    drain(r1, s1_recv)
    a1[...] = (a0[:, y] + r1[0]) + (r1[1] + r1[2])
    c3 = [
        remote(a1.at[1 - zh, :, OWN:ROWS], r3.at[1], s3_send, s3_recv, at(below, z_col)),
        remote(a1.at[zh, :, OWN:ROWS], r3.at[0], s3_send, s3_recv, at(below, c)),
    ]
    c2 = remote(a1.at[1 - zh, :, 0:OWN], r2, s2_send, s2_recv, z_peer)
    @pl.when(zh == 0)
    def _():
        pl.semaphore_wait(ready, len(far))

    c3[0].start()
    c2.start()
    c3[1].start()

    vown.wait()
    drain(vg.at[0, 0:3], vo_recv)
    drain(vg.at[1:4, 0], vd_recv)
    drain(vg.at[1:4, 0:2], vx_recv)
    val = jnp.concatenate([vg[(z - zl + 4) % 4].reshape(64, 512) for z in range(4)], axis=0)
    val_hi = val.astype(BF)
    ones = jnp.ones((16, 512), BF)
    vsum = nt(ones, (val * val).astype(BF))

    c2.wait_recv()
    drain(r3, s3_recv)
    own = a1[zh, :, 0:OWN] + r2[...]
    spill = r3[0] + r3[1]
    own = jnp.concatenate([own[:, : OWN - 128], own[:, OWN - 128 :] + spill], axis=1)

    stack = jnp.concatenate([own[:, e * PB : (e + 1) * PB] for e in range(EX_DEV)], axis=0)
    wide = jnp.concatenate([stack, stack], axis=1)
    wide = jnp.concatenate([wide, wide, wide, wide], axis=1)
    row_a = lax.broadcasted_iota(jnp.int32, (EX_DEV * 8, 512), 0) % 8
    lane_a = lax.broadcasted_iota(jnp.int32, (EX_DEV * 8, 512), 1) // PB
    wide = jnp.where(row_a == lane_a, wide, 0.0)
    hi = wide.astype(BF)
    lo = (wide - hi.astype(F32)).astype(BF)
    dots = nt(jnp.concatenate([hi, lo], axis=0), val_hi)
    dots = dots[0 : EX_DEV * 8] + dots[EX_DEV * 8 :]
    dots = jnp.sum(dots.reshape(EX_DEV, 8, 256), axis=1)
    fin[:, 0:256] = dots
    fin[:, 256:384] = jnp.zeros((8, 128), F32)
    fin[0:1, 256:384] = vsum[0:1, 0:128]
    fin[1:2, 256:384] = vsum[0:1, 128:256]
    fin[2:3, 256 : 256 + EX_DEV * 8] = nt(ones, (wide * wide).astype(BF))[0:1]

    cz = remote(fin, rz, fz_send, fz_recv, z_peer)
    cz.start()
    for ref, sem in (
        (r0, s0_send), (r1, s1_send), (r2, s2_send), (r3, s3_send),
        (vg.at[0, 0:3], vz_send), (vg.at[0, 0:3], vo_send),
        (vg.at[1:4, 0:2], vx_send), (vg.at[1:4, 0], vd_send),
    ):
        drain(ref, sem)
    cz.wait_recv()
    fb[p] = fin[...] + rz[...]
    cb = [
        remote(fb.at[p], fb.at[p], fb_send, fb_recv, p_peer[k]) for k in range(7)
    ]
    for cp in cb:
        cp.start()
    drain(fb.at[0:7], fb_recv)
    total = ((fb[0] + fb[1]) + (fb[2] + fb[3])) + ((fb[4] + fb[5]) + (fb[6] + fb[7]))
    tail = total[:, 256:384]
    lanes = lax.broadcasted_iota(jnp.int32, (EX_DEV, 128), 1) // 8
    slots = lax.broadcasted_iota(jnp.int32, (EX_DEV, 128), 0)
    own_sq = jnp.sum(jnp.where(lanes == slots, tail[2:3], 0.0), axis=1, keepdims=True)
    own_scale = math.sqrt(PA * PB) * lax.rsqrt(own_sq + epsilon)
    val_scale = lax.rsqrt(tail[0:2] + epsilon)
    out_ref[:, 0:128] = total[:, 0:128] * own_scale * val_scale[0:1]
    out_ref[:, 128:256] = total[:, 128:256] * own_scale * val_scale[1:2]
    drain(rz, fz_send)
    drain(fb.at[0:7], fb_send)


def on_device(
    latent,
    adapter_down_matrix,
    output_gradient_rows,
    output_sketch_factor,
    rank_sketch_factor,
    token_example_index,
    validation_sketches,
):
    tokens, columns = output_gradient_rows.shape
    width = latent.shape[1]
    steps = tokens // STEP
    dma = pltpu.SemaphoreType.DMA
    vm = pltpu.VMEM
    return pl.pallas_call(
        kernel,
        out_shape=vm((EX_DEV, 256), F32),
        in_specs=[pl.BlockSpec(memory_space=pl.ANY)] * 7,
        out_specs=pl.BlockSpec(memory_space=pltpu.VMEM),
        scratch_shapes=[
            vm((tokens, width), BF),
            vm((PB, width), BF),
            vm((tokens, columns), BF),
            vm((columns, PA), BF),
            vm((PB, PB), BF),
            vm((steps, 1, STEP), jnp.int32),
            vm((steps, OWN + PB, STEP), BF),
            vm((steps, STEP, PA), BF),
            vm((ROWS, PA), F32),
            vm((2, 4, 2, 8, ROWS), F32),
            vm((2, 4, 8, ROWS), F32),
            vm((2, 4, 8, ROWS), F32),
            vm((3, 2, 8, ROWS), F32),
            vm((2, 8, ROWS), F32),
            vm((8, OWN), F32),
            vm((2, 8, 128), F32),
            vm((4, 4, 16, 512), F32),
            vm((8, 384), F32),
            vm((8, 384), F32),
            vm((8, 8, 384), F32),
            dma((4,)), dma((steps,)), dma((steps,)), dma,
        ] + [dma] * 8 + [pltpu.SemaphoreType.REGULAR] + [dma] * 12,
        compiler_params=pltpu.CompilerParams(
            collective_id=0, has_side_effects=True, vmem_limit_bytes=60 * 1024 * 1024
        ),
    )(
        latent,
        adapter_down_matrix,
        output_gradient_rows,
        output_sketch_factor,
        rank_sketch_factor,
        token_example_index.reshape(steps, 1, STEP),
        validation_sketches,
    )


def solution(mesh):
    in_specs = (P("dp", None), P(), P("dp", "col"), P("col", None), P(), P("dp"), P("dp", "col"))
    out_specs = P("dp", None)
    return jax.shard_map(
        on_device, mesh=mesh, in_specs=in_specs, out_specs=out_specs, check_vma=False
    )
```

```python
import functools
import math

import jax
import jax.numpy as jnp
from jax import lax
from jax.experimental import pallas as pl
from jax.experimental.pallas import tpu as pltpu
from jax.sharding import PartitionSpec as P

PA = 128
PB = 64
EX_DEV = 8
MESH = pl.DeviceIdType.MESH

epsilon = 1e-06

BF = jnp.bfloat16
F32 = jnp.float32

STEP = 512
OWN = EX_DEV * PB
ROWS = OWN + 2 * PB

FAR_FIRST = ((4, 0), (4, 1), (2, 0), (2, 1), (6, 0), (6, 1), (0, 1))


def nt(x, y):
    return lax.dot_general(x, y, (((1,), (1,)), ((), ())), preferred_element_type=F32)


def kernel(
    lat_h, down_h, grad_h, sketch_h, rank_h, seg_h, val_h, out_ref,
    lat, down, grad, sketch, rank, seg, masked, side, gp, gt,
    r0, a0, r1, a1, r2, r3, vg, fin, rz, fb, local_sem, lat_sem, grad_sem, vown_sem,
    s0_send, s0_far, s0_near, s1_send, s1_far, s1_near, s2_send, s2_recv, s3_send, s3_recv,
    ready, vz_send, vz_recv, vo_send, vo_recv, vx_send, vx_recv, vd_send, vd_recv, fz_send, fz_recv, fb_send, fb_recv,
):
    i = lax.axis_index("dp")
    c = lax.axis_index("col")
    zl, x = i // 4, i % 4
    zh, y, core = c // 8, (c // 2) % 4, c % 2
    p = c % 8
    below, above = (i + 15) % 16, (i + 1) % 16

    def at(dp, col):
        return {"dp": dp, "col": col}

    core_peer = at(i, zh * 8 + y * 2 + (1 - core))
    y_peer = [at(i, zh * 8 + ((y + k) % 4) * 2 + core) for k in (2, 1, 3)]
    z_peer = at(i, (1 - zh) * 8 + p)
    p_peer = [at(i, zh * 8 + (p // 2 * 2 + k) % 8 + (core + j) % 2) for k, j in FAR_FIRST]
    vz_peer = [at(((zl + k) % 4) * 4 + x, c) for k in (2, 1, 3)]
    vd_peer = [at(((zl + k) % 4) * 4 + (x + 2) % 4, c) for k in (2, 1, 3)]
    vo_peer = [at(zl * 4 + (x + k) % 4, c) for k in (2, 1, 3)]
    vx_peer = [at(zl * 4 + (x + k) % 4, c) for k in (1, 3)]
    z_col = (1 - zh) * 8 + p

    tokens = grad.shape[0]
    first = i * EX_DEV - 1

    steps = tokens // STEP
    small = [
        pltpu.make_async_copy(src, dst, local_sem.at[n])
        for n, (src, dst) in enumerate(
            ((down_h, down), (rank_h, rank), (seg_h, seg), (sketch_h, sketch))
        )
    ]

    def block(n):
        return pl.ds(pl.multiple_of(n * STEP, STEP), STEP)

    def lat_copy(n):
        return pltpu.make_async_copy(lat_h.at[block(n), :], lat.at[block(n), :], lat_sem.at[n])

    def grad_copy(n):
        return pltpu.make_async_copy(grad_h.at[block(n), :], grad.at[block(n), :], grad_sem.at[n])

    for cp in small[:3]:
        cp.start()
    lat_copy(0).start()
    small[3].start()
    grad_copy(0).start()
    lat_copy(1).start()
    grad_copy(1).start()
    vown = pltpu.make_async_copy(val_h, vg.at[0, x], vown_sem)
    vown.start()
    barrier = pltpu.get_barrier_semaphore()
    near = p_peer + vz_peer + vo_peer + vd_peer + [at(above, c)]
    far = [z_peer, at(above, z_col)]
    for peer in near:
        pl.semaphore_signal(barrier, inc=1, device_id=peer, device_id_type=MESH)

    @pl.when(zh == 0)
    def _():
        for peer in far + [at(below, z_col)]:
            pl.semaphore_signal(barrier, inc=1, device_id=peer, device_id_type=MESH)

    def remote(src, dst, send, recv, peer):
        return pltpu.make_async_remote_copy(
            src_ref=src, dst_ref=dst, send_sem=send, recv_sem=recv,
            device_id=peer, device_id_type=MESH,
        )

    def drain(ref, sem):
        pltpu.make_async_copy(ref, ref, sem).wait()

    def v_begin():
        for k, peer in zip((2, 1, 3), vz_peer):
            remote(val_h, vg.at[4 - k, x], vz_send, vz_recv, peer).start()
        for peer in vo_peer:
            remote(val_h, vg.at[0, x], vo_send, vo_recv, peer).start()
        for k, peer in zip((2, 1, 3), vd_peer):
            remote(val_h, vg.at[4 - k, x], vd_send, vd_recv, peer).start()

    def v_turn():
        drain(vg.at[0, 0:3], vz_recv)
        for peer in vx_peer:
            remote(vg.at[1:4, x], vg.at[1:4, x], vx_send, vx_recv, peer).start()

    gp[...] = jnp.zeros_like(gp)
    side[steps - 1] = jnp.zeros((STEP, PA), BF)
    masked[steps - 1] = jnp.zeros((OWN + PB, STEP), BF)
    for cp in small:
        cp.wait()

    def project(n):
        part = jnp.dot(masked[n], side[n], preferred_element_type=F32)
        gp[0:OWN, :] += part[0:OWN]
        gp[OWN + PB : ROWS, :] += part[OWN:]

    def local_step(n, carry):
        lat_copy(n).wait()
        grad_copy(n).wait()

        @pl.when(n < steps - 2)
        def _():
            lat_copy(n + 2).start()
            grad_copy(n + 2).start()

        hidden = nt(lat[block(n), :], down[...]).astype(BF)
        out_side = jnp.dot(grad[block(n), :], sketch[...], preferred_element_type=F32)
        rank_side = lax.dot_general(
            rank[...], hidden, (((0,), (1,)), ((), ())), preferred_element_type=F32
        ).astype(BF).astype(F32)
        project(lax.rem(n + steps - 1, steps))
        ids = seg[n] - first
        for e in range(1, EX_DEV + 1):
            masked[n, (e - 1) * PB : e * PB, :] = jnp.where(ids == e, rank_side, 0.0).astype(BF)
        masked[n, OWN : OWN + PB, :] = jnp.where(ids == 0, rank_side, 0.0).astype(BF)
        side[n] = out_side.astype(BF)

        @pl.when((zh == 1) & (n == 0))
        def _():
            pl.semaphore_wait(barrier, len(near) + len(far) + 1)
            v_begin()
            for peer in far:
                pl.semaphore_signal(ready, inc=1, device_id=peer, device_id_type=MESH)

        return carry

    lax.fori_loop(0, steps, local_step, 0)
    project(steps - 1)

    for t in range(ROWS // 128):
        piece = gp[t * 128 : (t + 1) * 128, :].T
        gt[:, :, :, :, t * 128 : (t + 1) * 128] = piece.reshape(2, 4, 2, 8, 128)

    @pl.when(zh == 0)
    def _():
        pl.semaphore_wait(barrier, len(near))

    c0 = [
        remote(gt.at[z, :, 1 - core], r0.at[z], s0_send, sem, core_peer)
        for z, sem in ((1 - zh, s0_far), (zh, s0_near))
    ]
    for cp in c0:
        cp.start()

    @pl.when(zh == 0)
    def _():
        v_begin()

    for n, (z, sem) in enumerate(((1 - zh, s1_far), (zh, s1_near))):
        c0[n].wait_recv()
        a0[z] = gt[z, :, core] + r0[z]
        for k, peer in zip((2, 1, 3), y_peer):
            remote(a0.at[z, (y + k) % 4], r1.at[n, k - 1], s1_send, sem, peer).start()

    @pl.when(zh == 1)
    def _():
        v_turn()

    drain(r1.at[0], s1_far)
    a1[0] = (a0[1 - zh, y] + r1[0, 0]) + (r1[0, 1] + r1[0, 2])

    @pl.when(zh == 0)
    def _():
        pl.semaphore_wait(ready, len(far))

    remote(a1.at[0, :, OWN:ROWS], r3.at[1], s3_send, s3_recv, at(below, z_col)).start()
    c2 = remote(a1.at[0, :, 0:OWN], r2, s2_send, s2_recv, z_peer)
    c2.start()
    drain(r1.at[1], s1_near)
    a1[1] = (a0[zh, y] + r1[1, 0]) + (r1[1, 1] + r1[1, 2])
    remote(a1.at[1, :, OWN:ROWS], r3.at[0], s3_send, s3_recv, at(below, c)).start()

    @pl.when(zh == 0)
    def _():
        v_turn()

    vown.wait()
    drain(vg.at[0, 0:3], vo_recv)
    drain(vg.at[1:4, 0], vd_recv)
    drain(vg.at[1:4, 0:2], vx_recv)
    val = jnp.concatenate([vg[(z - zl + 4) % 4].reshape(64, 512) for z in range(4)], axis=0)
    val_hi = val.astype(BF)
    ones = jnp.ones((16, 512), BF)
    vsum = nt(ones, (val * val).astype(BF))

    c2.wait_recv()
    drain(r3, s3_recv)
    own = a1[1, :, 0:OWN] + r2[...]
    spill = r3[0] + r3[1]
    own = jnp.concatenate([own[:, : OWN - 128], own[:, OWN - 128 :] + spill], axis=1)

    stack = jnp.concatenate([own[:, e * PB : (e + 1) * PB] for e in range(EX_DEV)], axis=0)
    wide = jnp.concatenate([stack, stack], axis=1)
    wide = jnp.concatenate([wide, wide, wide, wide], axis=1)
    row_a = lax.broadcasted_iota(jnp.int32, (EX_DEV * 8, 512), 0) % 8
    lane_a = lax.broadcasted_iota(jnp.int32, (EX_DEV * 8, 512), 1) // PB
    wide = jnp.where(row_a == lane_a, wide, 0.0)
    hi = wide.astype(BF)
    lo = (wide - hi.astype(F32)).astype(BF)
    dots = nt(jnp.concatenate([hi, lo], axis=0), val_hi)
    dots = dots[0 : EX_DEV * 8] + dots[EX_DEV * 8 :]
    dots = jnp.sum(dots.reshape(EX_DEV, 8, 256), axis=1)
    fin[:, 0:256] = dots
    fin[:, 256:384] = jnp.zeros((8, 128), F32)
    fin[0:1, 256:384] = vsum[0:1, 0:128]
    fin[1:2, 256:384] = vsum[0:1, 128:256]
    fin[2:3, 256 : 256 + EX_DEV * 8] = nt(ones, (wide * wide).astype(BF))[0:1]

    cz = remote(fin, rz, fz_send, fz_recv, z_peer)
    cz.start()
    for ref, sem in (
        (r0, s0_send), (r1, s1_send), (r2, s2_send), (r3, s3_send),
        (vg.at[0, 0:3], vz_send), (vg.at[0, 0:3], vo_send),
        (vg.at[1:4, 0:2], vx_send), (vg.at[1:4, 0], vd_send),
    ):
        drain(ref, sem)
    cz.wait_recv()
    fb[p] = fin[...] + rz[...]
    cb = [
        remote(fb.at[p], fb.at[p], fb_send, fb_recv, p_peer[k]) for k in range(7)
    ]
    for cp in cb:
        cp.start()
    drain(fb.at[0:7], fb_recv)
    total = ((fb[0] + fb[1]) + (fb[2] + fb[3])) + ((fb[4] + fb[5]) + (fb[6] + fb[7]))
    tail = total[:, 256:384]
    lanes = lax.broadcasted_iota(jnp.int32, (EX_DEV, 128), 1) // 8
    slots = lax.broadcasted_iota(jnp.int32, (EX_DEV, 128), 0)
    own_sq = jnp.sum(jnp.where(lanes == slots, tail[2:3], 0.0), axis=1, keepdims=True)
    own_scale = math.sqrt(PA * PB) * lax.rsqrt(own_sq + epsilon)
    val_scale = lax.rsqrt(tail[0:2] + epsilon)
    out_ref[:, 0:128] = total[:, 0:128] * own_scale * val_scale[0:1]
    out_ref[:, 128:256] = total[:, 128:256] * own_scale * val_scale[1:2]
    drain(rz, fz_send)
    drain(fb.at[0:7], fb_send)


def on_device(
    latent,
    adapter_down_matrix,
    output_gradient_rows,
    output_sketch_factor,
    rank_sketch_factor,
    token_example_index,
    validation_sketches,
):
    tokens, columns = output_gradient_rows.shape
    width = latent.shape[1]
    steps = tokens // STEP
    dma = pltpu.SemaphoreType.DMA
    vm = pltpu.VMEM
    return pl.pallas_call(
        kernel,
        out_shape=vm((EX_DEV, 256), F32),
        in_specs=[pl.BlockSpec(memory_space=pl.ANY)] * 7,
        out_specs=pl.BlockSpec(memory_space=pltpu.VMEM),
        scratch_shapes=[
            vm((tokens, width), BF),
            vm((PB, width), BF),
            vm((tokens, columns), BF),
            vm((columns, PA), BF),
            vm((PB, PB), BF),
            vm((steps, 1, STEP), jnp.int32),
            vm((steps, OWN + PB, STEP), BF),
            vm((steps, STEP, PA), BF),
            vm((ROWS, PA), F32),
            vm((2, 4, 2, 8, ROWS), F32),
            vm((2, 4, 8, ROWS), F32),
            vm((2, 4, 8, ROWS), F32),
            vm((2, 3, 8, ROWS), F32),
            vm((2, 8, ROWS), F32),
            vm((8, OWN), F32),
            vm((2, 8, 128), F32),
            vm((4, 4, 16, 512), F32),
            vm((8, 384), F32),
            vm((8, 384), F32),
            vm((8, 8, 384), F32),
            dma((4,)), dma((steps,)), dma((steps,)), dma,
        ] + [dma] * 10 + [pltpu.SemaphoreType.REGULAR] + [dma] * 12,
        compiler_params=pltpu.CompilerParams(
            collective_id=0, has_side_effects=True, vmem_limit_bytes=60 * 1024 * 1024
        ),
    )(
        latent,
        adapter_down_matrix,
        output_gradient_rows,
        output_sketch_factor,
        rank_sketch_factor,
        token_example_index.reshape(steps, 1, STEP),
        validation_sketches,
    )


def solution(mesh):
    in_specs = (P("dp", None), P(), P("dp", "col"), P("col", None), P(), P("dp"), P("dp", "col"))
    out_specs = P("dp", None)
    return jax.shard_map(
        on_device, mesh=mesh, in_specs=in_specs, out_specs=out_specs, check_vma=False
    )
```

```python
import functools
import math

import jax
import jax.numpy as jnp
from jax import lax
from jax.experimental import pallas as pl
from jax.experimental.pallas import tpu as pltpu
from jax.sharding import PartitionSpec as P

PA = 128
PB = 64
EX_DEV = 8
MESH = pl.DeviceIdType.MESH

epsilon = 1e-06

BF = jnp.bfloat16
F32 = jnp.float32

STEP = 512
OWN = EX_DEV * PB
ROWS = OWN + 2 * PB

FAR_FIRST = ((4, 0), (4, 1), (2, 0), (2, 1), (6, 0), (6, 1), (0, 1))


def nt(x, y):
    return lax.dot_general(x, y, (((1,), (1,)), ((), ())), preferred_element_type=F32)


def kernel(
    lat_h, down_h, grad_h, sketch_h, rank_h, seg_h, val_h, out_ref,
    lat, down, grad, sketch, rank, seg, masked, side, gp, gt,
    r0, a0, r1, a1, r2, r3, vg, vb, spread_ref, fin, rz, fb, local_sem, lat_sem, grad_sem, vown_sem,
    s0_send, s0_far, s0_near, s1_send, s1_far, s1_near, s2_send, s2_recv, s3_send, s3_recv,
    ready, vz_send, vz_recv, vo_send, vo_recv, vx_send, vx_recv, vd_send, vd_recv, fz_send, fz_recv, fb_send, fb_recv,
):
    i = lax.axis_index("dp")
    c = lax.axis_index("col")
    zl, x = i // 4, i % 4
    zh, y, core = c // 8, (c // 2) % 4, c % 2
    p = c % 8
    below, above = (i + 15) % 16, (i + 1) % 16

    def at(dp, col):
        return {"dp": dp, "col": col}

    core_peer = at(i, zh * 8 + y * 2 + (1 - core))
    y_peer = [at(i, zh * 8 + ((y + k) % 4) * 2 + core) for k in (2, 1, 3)]
    z_peer = at(i, (1 - zh) * 8 + p)
    p_peer = [at(i, zh * 8 + (p // 2 * 2 + k) % 8 + (core + j) % 2) for k, j in FAR_FIRST]
    vz_peer = [at(((zl + k) % 4) * 4 + x, c) for k in (2, 1, 3)]
    vd_peer = [at(((zl + k) % 4) * 4 + (x + 2) % 4, c) for k in (2, 1, 3)]
    vo_peer = [at(zl * 4 + (x + k) % 4, c) for k in (2, 1, 3)]
    vx_peer = [at(zl * 4 + (x + k) % 4, c) for k in (1, 3)]
    z_col = (1 - zh) * 8 + p

    tokens = grad.shape[0]
    first = i * EX_DEV - 1

    steps = tokens // STEP
    small = [
        pltpu.make_async_copy(src, dst, local_sem.at[n])
        for n, (src, dst) in enumerate(
            ((down_h, down), (rank_h, rank), (seg_h, seg), (sketch_h, sketch))
        )
    ]

    def block(n):
        return pl.ds(pl.multiple_of(n * STEP, STEP), STEP)

    def lat_copy(n):
        return pltpu.make_async_copy(lat_h.at[block(n), :], lat.at[block(n), :], lat_sem.at[n])

    def grad_copy(n):
        return pltpu.make_async_copy(grad_h.at[block(n), :], grad.at[block(n), :], grad_sem.at[n])

    for cp in small[:3]:
        cp.start()
    lat_copy(0).start()
    small[3].start()
    grad_copy(0).start()
    lat_copy(1).start()
    grad_copy(1).start()
    vown = pltpu.make_async_copy(val_h, vg.at[0, x], vown_sem)
    vown.start()
    barrier = pltpu.get_barrier_semaphore()
    near = p_peer + vz_peer + vo_peer + vd_peer + [at(above, c)]
    far = [z_peer, at(above, z_col)]
    for peer in near:
        pl.semaphore_signal(barrier, inc=1, device_id=peer, device_id_type=MESH)

    @pl.when(zh == 0)
    def _():
        for peer in far + [at(below, z_col)]:
            pl.semaphore_signal(barrier, inc=1, device_id=peer, device_id_type=MESH)

    def remote(src, dst, send, recv, peer):
        return pltpu.make_async_remote_copy(
            src_ref=src, dst_ref=dst, send_sem=send, recv_sem=recv,
            device_id=peer, device_id_type=MESH,
        )

    def drain(ref, sem):
        pltpu.make_async_copy(ref, ref, sem).wait()

    def v_begin():
        for k, peer in zip((2, 1, 3), vz_peer):
            remote(val_h, vg.at[4 - k, x], vz_send, vz_recv, peer).start()
        for peer in vo_peer:
            remote(val_h, vg.at[0, x], vo_send, vo_recv, peer).start()
        for k, peer in zip((2, 1, 3), vd_peer):
            remote(val_h, vg.at[4 - k, x], vd_send, vd_recv, peer).start()

    def v_turn():
        drain(vg.at[0, 0:3], vz_recv)
        for peer in vx_peer:
            remote(vg.at[1:4, x], vg.at[1:4, x], vx_send, vx_recv, peer).start()

    gp[...] = jnp.zeros_like(gp)
    side[steps - 1] = jnp.zeros((STEP, PA), BF)
    masked[steps - 1] = jnp.zeros((OWN + PB, STEP), BF)
    for cp in small:
        cp.wait()

    def project(n):
        part = jnp.dot(masked[n], side[n], preferred_element_type=F32)
        gp[0:OWN, :] += part[0:OWN]
        gp[OWN + PB : ROWS, :] += part[OWN:]

    def local_step(n, carry):
        lat_copy(n).wait()
        grad_copy(n).wait()

        @pl.when(n < steps - 2)
        def _():
            lat_copy(n + 2).start()
            grad_copy(n + 2).start()

        hidden = nt(lat[block(n), :], down[...]).astype(BF)
        out_side = jnp.dot(grad[block(n), :], sketch[...], preferred_element_type=F32)
        rank_side = lax.dot_general(
            rank[...], hidden, (((0,), (1,)), ((), ())), preferred_element_type=F32
        ).astype(BF).astype(F32)
        project(lax.rem(n + steps - 1, steps))
        ids = seg[n] - first
        for e in range(1, EX_DEV + 1):
            masked[n, (e - 1) * PB : e * PB, :] = jnp.where(ids == e, rank_side, 0.0).astype(BF)
        masked[n, OWN : OWN + PB, :] = jnp.where(ids == 0, rank_side, 0.0).astype(BF)
        side[n] = out_side.astype(BF)

        @pl.when((zh == 1) & (n == 0))
        def _():
            pl.semaphore_wait(barrier, len(near) + len(far) + 1)
            v_begin()
            for peer in far:
                pl.semaphore_signal(ready, inc=1, device_id=peer, device_id_type=MESH)

        return carry

    lax.fori_loop(0, steps, local_step, 0)
    project(steps - 1)

    for t in range(ROWS // 128):
        piece = gp[t * 128 : (t + 1) * 128, :].T
        gt[:, :, :, :, t * 128 : (t + 1) * 128] = piece.reshape(2, 4, 2, 8, 128)

    @pl.when(zh == 0)
    def _():
        pl.semaphore_wait(barrier, len(near))

    c0 = [
        remote(gt.at[z, :, 1 - core], r0.at[z], s0_send, sem, core_peer)
        for z, sem in ((1 - zh, s0_far), (zh, s0_near))
    ]
    for cp in c0:
        cp.start()

    @pl.when(zh == 0)
    def _():
        v_begin()

    for n, (z, sem) in enumerate(((1 - zh, s1_far), (zh, s1_near))):
        c0[n].wait_recv()
        a0[z] = gt[z, :, core] + r0[z]
        for k, peer in zip((2, 1, 3), y_peer):
            remote(a0.at[z, (y + k) % 4], r1.at[n, k - 1], s1_send, sem, peer).start()

    @pl.when(zh == 1)
    def _():
        v_turn()

    drain(r1.at[0], s1_far)
    a1[0] = (a0[1 - zh, y] + r1[0, 0]) + (r1[0, 1] + r1[0, 2])

    @pl.when(zh == 0)
    def _():
        pl.semaphore_wait(ready, len(far))

    remote(a1.at[0, :, OWN:ROWS], r3.at[1], s3_send, s3_recv, at(below, z_col)).start()
    c2 = remote(a1.at[0, :, 0:OWN], r2, s2_send, s2_recv, z_peer)
    c2.start()
    drain(r1.at[1], s1_near)
    a1[1] = (a0[zh, y] + r1[1, 0]) + (r1[1, 1] + r1[1, 2])
    remote(a1.at[1, :, OWN:ROWS], r3.at[0], s3_send, s3_recv, at(below, c)).start()

    @pl.when(zh == 0)
    def _():
        v_turn()

    ones = jnp.ones((16, 512), BF)

    def spread():
        c2.wait_recv()
        drain(r3, s3_recv)
        own = a1[1, :, 0:OWN] + r2[...]
        spill = r3[0] + r3[1]
        own = jnp.concatenate([own[:, : OWN - 128], own[:, OWN - 128 :] + spill], axis=1)
        stack = jnp.concatenate([own[:, e * PB : (e + 1) * PB] for e in range(EX_DEV)], axis=0)
        wide = jnp.concatenate([stack, stack], axis=1)
        wide = jnp.concatenate([wide, wide, wide, wide], axis=1)
        row_a = lax.broadcasted_iota(jnp.int32, (EX_DEV * 8, 512), 0) % 8
        lane_a = lax.broadcasted_iota(jnp.int32, (EX_DEV * 8, 512), 1) // PB
        wide = jnp.where(row_a == lane_a, wide, 0.0)
        hi = wide.astype(BF)
        spread_ref[0 : EX_DEV * 8, :] = hi
        spread_ref[EX_DEV * 8 :, :] = (wide - hi.astype(F32)).astype(BF)
        fin[2:3, 256 : 256 + EX_DEV * 8] = nt(ones, (wide * wide).astype(BF))[0:1]

    fin[:, 256:384] = jnp.zeros((8, 128), F32)

    @pl.when(zh == 1)
    def _():
        spread()

    vown.wait()
    drain(vg.at[0, 0:3], vo_recv)
    drain(vg.at[1:4, 0], vd_recv)
    drain(vg.at[1:4, 0:2], vx_recv)
    val = jnp.concatenate([vg[(z - zl + 4) % 4].reshape(64, 512) for z in range(4)], axis=0)
    val_hi = val.astype(BF)
    vb[...] = val_hi
    vsum = nt(ones, (val * val).astype(BF))
    fin[0:1, 256:384] = vsum[0:1, 0:128]
    fin[1:2, 256:384] = vsum[0:1, 128:256]

    @pl.when(zh == 0)
    def _():
        spread()

    dots = nt(spread_ref[...], vb[...])
    dots = dots[0 : EX_DEV * 8] + dots[EX_DEV * 8 :]
    fin[:, 0:256] = jnp.sum(dots.reshape(EX_DEV, 8, 256), axis=1)

    cz = remote(fin, rz, fz_send, fz_recv, z_peer)
    cz.start()
    for ref, sem in (
        (r0, s0_send), (r1, s1_send), (r2, s2_send), (r3, s3_send),
        (vg.at[0, 0:3], vz_send), (vg.at[0, 0:3], vo_send),
        (vg.at[1:4, 0:2], vx_send), (vg.at[1:4, 0], vd_send),
    ):
        drain(ref, sem)
    cz.wait_recv()
    fb[p] = fin[...] + rz[...]
    cb = [
        remote(fb.at[p], fb.at[p], fb_send, fb_recv, p_peer[k]) for k in range(7)
    ]
    for cp in cb:
        cp.start()
    drain(fb.at[0:7], fb_recv)
    total = ((fb[0] + fb[1]) + (fb[2] + fb[3])) + ((fb[4] + fb[5]) + (fb[6] + fb[7]))
    tail = total[:, 256:384]
    lanes = lax.broadcasted_iota(jnp.int32, (EX_DEV, 128), 1) // 8
    slots = lax.broadcasted_iota(jnp.int32, (EX_DEV, 128), 0)
    own_sq = jnp.sum(jnp.where(lanes == slots, tail[2:3], 0.0), axis=1, keepdims=True)
    own_scale = math.sqrt(PA * PB) * lax.rsqrt(own_sq + epsilon)
    val_scale = lax.rsqrt(tail[0:2] + epsilon)
    out_ref[:, 0:128] = total[:, 0:128] * own_scale * val_scale[0:1]
    out_ref[:, 128:256] = total[:, 128:256] * own_scale * val_scale[1:2]
    drain(rz, fz_send)
    drain(fb.at[0:7], fb_send)


def on_device(
    latent,
    adapter_down_matrix,
    output_gradient_rows,
    output_sketch_factor,
    rank_sketch_factor,
    token_example_index,
    validation_sketches,
):
    tokens, columns = output_gradient_rows.shape
    width = latent.shape[1]
    steps = tokens // STEP
    dma = pltpu.SemaphoreType.DMA
    vm = pltpu.VMEM
    return pl.pallas_call(
        kernel,
        out_shape=vm((EX_DEV, 256), F32),
        in_specs=[pl.BlockSpec(memory_space=pl.ANY)] * 7,
        out_specs=pl.BlockSpec(memory_space=pltpu.VMEM),
        scratch_shapes=[
            vm((tokens, width), BF),
            vm((PB, width), BF),
            vm((tokens, columns), BF),
            vm((columns, PA), BF),
            vm((PB, PB), BF),
            vm((steps, 1, STEP), jnp.int32),
            vm((steps, OWN + PB, STEP), BF),
            vm((steps, STEP, PA), BF),
            vm((ROWS, PA), F32),
            vm((2, 4, 2, 8, ROWS), F32),
            vm((2, 4, 8, ROWS), F32),
            vm((2, 4, 8, ROWS), F32),
            vm((2, 3, 8, ROWS), F32),
            vm((2, 8, ROWS), F32),
            vm((8, OWN), F32),
            vm((2, 8, 128), F32),
            vm((4, 4, 16, 512), F32),
            vm((256, 512), BF),
            vm((2 * EX_DEV * 8, 512), BF),
            vm((8, 384), F32),
            vm((8, 384), F32),
            vm((8, 8, 384), F32),
            dma((4,)), dma((steps,)), dma((steps,)), dma,
        ] + [dma] * 10 + [pltpu.SemaphoreType.REGULAR] + [dma] * 12,
        compiler_params=pltpu.CompilerParams(
            collective_id=0, has_side_effects=True, vmem_limit_bytes=60 * 1024 * 1024
        ),
    )(
        latent,
        adapter_down_matrix,
        output_gradient_rows,
        output_sketch_factor,
        rank_sketch_factor,
        token_example_index.reshape(steps, 1, STEP),
        validation_sketches,
    )


def solution(mesh):
    in_specs = (P("dp", None), P(), P("dp", "col"), P("col", None), P(), P("dp"), P("dp", "col"))
    out_specs = P("dp", None)
    return jax.shard_map(
        on_device, mesh=mesh, in_specs=in_specs, out_specs=out_specs, check_vma=False
    )
```

```python
import functools
import math

import jax
import jax.numpy as jnp
from jax import lax
from jax.experimental import pallas as pl
from jax.experimental.pallas import tpu as pltpu
from jax.sharding import PartitionSpec as P

PA = 128
PB = 64
EX_DEV = 8
MESH = pl.DeviceIdType.MESH

epsilon = 1e-06

BF = jnp.bfloat16
F32 = jnp.float32

STEP = 256
AHEAD = 4
OWN = EX_DEV * PB
ROWS = OWN + 2 * PB

FAR_FIRST = ((4, 0), (4, 1), (2, 0), (2, 1), (6, 0), (6, 1), (0, 1))


def nt(x, y):
    return lax.dot_general(x, y, (((1,), (1,)), ((), ())), preferred_element_type=F32)


def kernel(
    lat_h, down_h, grad_h, sketch_h, rank_h, seg_h, val_h, out_ref,
    lat, down, grad, sketch, rank, seg, masked, side, gp, gt,
    r0, a0, r1, a1, r2, r3, vg, vb, spread_ref, fin, rz, fb, local_sem, lat_sem, grad_sem, vown_sem,
    s0_send, s0_far, s0_near, s1_send, s1_far, s1_near, s2_send, s2_recv, s3_send, s3_recv,
    ready, vz_send, vz_recv, vo_send, vo_recv, vx_send, vx_recv, vd_send, vd_recv, fz_send, fz_recv, fb_send, fb_recv,
):
    i = lax.axis_index("dp")
    c = lax.axis_index("col")
    zl, x = i // 4, i % 4
    zh, y, core = c // 8, (c // 2) % 4, c % 2
    p = c % 8
    below, above = (i + 15) % 16, (i + 1) % 16

    def at(dp, col):
        return {"dp": dp, "col": col}

    core_peer = at(i, zh * 8 + y * 2 + (1 - core))
    y_peer = [at(i, zh * 8 + ((y + k) % 4) * 2 + core) for k in (2, 1, 3)]
    z_peer = at(i, (1 - zh) * 8 + p)
    p_peer = [at(i, zh * 8 + (p // 2 * 2 + k) % 8 + (core + j) % 2) for k, j in FAR_FIRST]
    vz_peer = [at(((zl + k) % 4) * 4 + x, c) for k in (2, 1, 3)]
    vd_peer = [at(((zl + k) % 4) * 4 + (x + 2) % 4, c) for k in (2, 1, 3)]
    vo_peer = [at(zl * 4 + (x + k) % 4, c) for k in (2, 1, 3)]
    vx_peer = [at(zl * 4 + (x + k) % 4, c) for k in (1, 3)]
    z_col = (1 - zh) * 8 + p

    tokens = grad.shape[0]
    first = i * EX_DEV - 1

    steps = tokens // STEP
    small = [
        pltpu.make_async_copy(src, dst, local_sem.at[n])
        for n, (src, dst) in enumerate(
            ((down_h, down), (rank_h, rank), (seg_h, seg), (sketch_h, sketch))
        )
    ]

    def block(n):
        return pl.ds(pl.multiple_of(n * STEP, STEP), STEP)

    def lat_copy(n):
        return pltpu.make_async_copy(lat_h.at[block(n), :], lat.at[block(n), :], lat_sem.at[n])

    def grad_copy(n):
        return pltpu.make_async_copy(grad_h.at[block(n), :], grad.at[block(n), :], grad_sem.at[n])

    for cp in small[:3]:
        cp.start()
    lat_copy(0).start()
    small[3].start()
    grad_copy(0).start()
    for n in range(1, AHEAD):
        lat_copy(n).start()
        grad_copy(n).start()
    vown = pltpu.make_async_copy(val_h, vg.at[0, x], vown_sem)
    vown.start()
    barrier = pltpu.get_barrier_semaphore()
    near = p_peer + vz_peer + vo_peer + vd_peer + [at(above, c)]
    far = [z_peer, at(above, z_col)]
    for peer in near:
        pl.semaphore_signal(barrier, inc=1, device_id=peer, device_id_type=MESH)

    @pl.when(zh == 0)
    def _():
        for peer in far + [at(below, z_col)]:
            pl.semaphore_signal(barrier, inc=1, device_id=peer, device_id_type=MESH)

    def remote(src, dst, send, recv, peer):
        return pltpu.make_async_remote_copy(
            src_ref=src, dst_ref=dst, send_sem=send, recv_sem=recv,
            device_id=peer, device_id_type=MESH,
        )

    def drain(ref, sem):
        pltpu.make_async_copy(ref, ref, sem).wait()

    def v_begin():
        for k, peer in zip((2, 1, 3), vz_peer):
            remote(val_h, vg.at[4 - k, x], vz_send, vz_recv, peer).start()
        for peer in vo_peer:
            remote(val_h, vg.at[0, x], vo_send, vo_recv, peer).start()
        for k, peer in zip((2, 1, 3), vd_peer):
            remote(val_h, vg.at[4 - k, x], vd_send, vd_recv, peer).start()

    def v_turn():
        drain(vg.at[0, 0:3], vz_recv)
        for peer in vx_peer:
            remote(vg.at[1:4, x], vg.at[1:4, x], vx_send, vx_recv, peer).start()

    gp[...] = jnp.zeros_like(gp)
    side[steps - 1] = jnp.zeros((STEP, PA), BF)
    masked[steps - 1] = jnp.zeros((OWN + PB, STEP), BF)
    for cp in small:
        cp.wait()

    def project(n):
        part = jnp.dot(masked[n], side[n], preferred_element_type=F32)
        gp[0:OWN, :] += part[0:OWN]
        gp[OWN + PB : ROWS, :] += part[OWN:]

    def local_step(n, carry):
        lat_copy(n).wait()
        grad_copy(n).wait()

        @pl.when(n < steps - AHEAD)
        def _():
            lat_copy(n + AHEAD).start()
            grad_copy(n + AHEAD).start()

        hidden = nt(lat[block(n), :], down[...]).astype(BF)
        out_side = jnp.dot(grad[block(n), :], sketch[...], preferred_element_type=F32)
        rank_side = lax.dot_general(
            rank[...], hidden, (((0,), (1,)), ((), ())), preferred_element_type=F32
        ).astype(BF).astype(F32)
        project(lax.rem(n + steps - 1, steps))
        ids = seg[n] - first
        for e in range(1, EX_DEV + 1):
            masked[n, (e - 1) * PB : e * PB, :] = jnp.where(ids == e, rank_side, 0.0).astype(BF)
        masked[n, OWN : OWN + PB, :] = jnp.where(ids == 0, rank_side, 0.0).astype(BF)
        side[n] = out_side.astype(BF)

        @pl.when((zh == 1) & (n == 1))
        def _():
            pl.semaphore_wait(barrier, len(near) + len(far) + 1)
            v_begin()
            for peer in far:
                pl.semaphore_signal(ready, inc=1, device_id=peer, device_id_type=MESH)

        return carry

    lax.fori_loop(0, steps, local_step, 0)
    project(steps - 1)

    for t in range(ROWS // 128):
        piece = gp[t * 128 : (t + 1) * 128, :].T
        gt[:, :, :, :, t * 128 : (t + 1) * 128] = piece.reshape(2, 4, 2, 8, 128)

    @pl.when(zh == 0)
    def _():
        pl.semaphore_wait(barrier, len(near))

    c0 = [
        remote(gt.at[z, :, 1 - core], r0.at[z], s0_send, sem, core_peer)
        for z, sem in ((1 - zh, s0_far), (zh, s0_near))
    ]
    for cp in c0:
        cp.start()

    @pl.when(zh == 0)
    def _():
        v_begin()

    for n, (z, sem) in enumerate(((1 - zh, s1_far), (zh, s1_near))):
        c0[n].wait_recv()
        a0[z] = gt[z, :, core] + r0[z]
        for k, peer in zip((2, 1, 3), y_peer):
            remote(a0.at[z, (y + k) % 4], r1.at[n, k - 1], s1_send, sem, peer).start()

    @pl.when(zh == 1)
    def _():
        v_turn()

    drain(r1.at[0], s1_far)
    a1[0] = (a0[1 - zh, y] + r1[0, 0]) + (r1[0, 1] + r1[0, 2])

    @pl.when(zh == 0)
    def _():
        pl.semaphore_wait(ready, len(far))

    remote(a1.at[0, :, OWN:ROWS], r3.at[1], s3_send, s3_recv, at(below, z_col)).start()
    c2 = remote(a1.at[0, :, 0:OWN], r2, s2_send, s2_recv, z_peer)
    c2.start()
    drain(r1.at[1], s1_near)
    a1[1] = (a0[zh, y] + r1[1, 0]) + (r1[1, 1] + r1[1, 2])
    remote(a1.at[1, :, OWN:ROWS], r3.at[0], s3_send, s3_recv, at(below, c)).start()

    @pl.when(zh == 0)
    def _():
        v_turn()

    ones = jnp.ones((16, 512), BF)

    def spread():
        c2.wait_recv()
        drain(r3, s3_recv)
        own = a1[1, :, 0:OWN] + r2[...]
        spill = r3[0] + r3[1]
        own = jnp.concatenate([own[:, : OWN - 128], own[:, OWN - 128 :] + spill], axis=1)
        stack = jnp.concatenate([own[:, e * PB : (e + 1) * PB] for e in range(EX_DEV)], axis=0)
        wide = jnp.concatenate([stack, stack], axis=1)
        wide = jnp.concatenate([wide, wide, wide, wide], axis=1)
        row_a = lax.broadcasted_iota(jnp.int32, (EX_DEV * 8, 512), 0) % 8
        lane_a = lax.broadcasted_iota(jnp.int32, (EX_DEV * 8, 512), 1) // PB
        wide = jnp.where(row_a == lane_a, wide, 0.0)
        hi = wide.astype(BF)
        spread_ref[0 : EX_DEV * 8, :] = hi
        spread_ref[EX_DEV * 8 :, :] = (wide - hi.astype(F32)).astype(BF)
        fin[2:3, 256 : 256 + EX_DEV * 8] = nt(ones, (wide * wide).astype(BF))[0:1]

    fin[:, 256:384] = jnp.zeros((8, 128), F32)

    @pl.when(zh == 1)
    def _():
        spread()

    vown.wait()
    drain(vg.at[0, 0:3], vo_recv)
    drain(vg.at[1:4, 0], vd_recv)
    drain(vg.at[1:4, 0:2], vx_recv)
    val = jnp.concatenate([vg[(z - zl + 4) % 4].reshape(64, 512) for z in range(4)], axis=0)
    val_hi = val.astype(BF)
    vb[...] = val_hi
    vsum = nt(ones, (val * val).astype(BF))
    fin[0:1, 256:384] = vsum[0:1, 0:128]
    fin[1:2, 256:384] = vsum[0:1, 128:256]

    @pl.when(zh == 0)
    def _():
        spread()

    dots = nt(spread_ref[...], vb[...])
    dots = dots[0 : EX_DEV * 8] + dots[EX_DEV * 8 :]
    fin[:, 0:256] = jnp.sum(dots.reshape(EX_DEV, 8, 256), axis=1)

    cz = remote(fin, rz, fz_send, fz_recv, z_peer)
    cz.start()
    for ref, sem in (
        (r0, s0_send), (r1, s1_send), (r2, s2_send), (r3, s3_send),
        (vg.at[0, 0:3], vz_send), (vg.at[0, 0:3], vo_send),
        (vg.at[1:4, 0:2], vx_send), (vg.at[1:4, 0], vd_send),
    ):
        drain(ref, sem)
    cz.wait_recv()
    fb[p] = fin[...] + rz[...]
    cb = [
        remote(fb.at[p], fb.at[p], fb_send, fb_recv, p_peer[k]) for k in range(7)
    ]
    for cp in cb:
        cp.start()
    drain(fb.at[0:7], fb_recv)
    total = ((fb[0] + fb[1]) + (fb[2] + fb[3])) + ((fb[4] + fb[5]) + (fb[6] + fb[7]))
    tail = total[:, 256:384]
    lanes = lax.broadcasted_iota(jnp.int32, (EX_DEV, 128), 1) // 8
    slots = lax.broadcasted_iota(jnp.int32, (EX_DEV, 128), 0)
    own_sq = jnp.sum(jnp.where(lanes == slots, tail[2:3], 0.0), axis=1, keepdims=True)
    own_scale = math.sqrt(PA * PB) * lax.rsqrt(own_sq + epsilon)
    val_scale = lax.rsqrt(tail[0:2] + epsilon)
    out_ref[:, 0:128] = total[:, 0:128] * own_scale * val_scale[0:1]
    out_ref[:, 128:256] = total[:, 128:256] * own_scale * val_scale[1:2]
    drain(rz, fz_send)
    drain(fb.at[0:7], fb_send)


def on_device(
    latent,
    adapter_down_matrix,
    output_gradient_rows,
    output_sketch_factor,
    rank_sketch_factor,
    token_example_index,
    validation_sketches,
):
    tokens, columns = output_gradient_rows.shape
    width = latent.shape[1]
    steps = tokens // STEP
    dma = pltpu.SemaphoreType.DMA
    vm = pltpu.VMEM
    return pl.pallas_call(
        kernel,
        out_shape=vm((EX_DEV, 256), F32),
        in_specs=[pl.BlockSpec(memory_space=pl.ANY)] * 7,
        out_specs=pl.BlockSpec(memory_space=pltpu.VMEM),
        scratch_shapes=[
            vm((tokens, width), BF),
            vm((PB, width), BF),
            vm((tokens, columns), BF),
            vm((columns, PA), BF),
            vm((PB, PB), BF),
            vm((steps, 1, STEP), jnp.int32),
            vm((steps, OWN + PB, STEP), BF),
            vm((steps, STEP, PA), BF),
            vm((ROWS, PA), F32),
            vm((2, 4, 2, 8, ROWS), F32),
            vm((2, 4, 8, ROWS), F32),
            vm((2, 4, 8, ROWS), F32),
            vm((2, 3, 8, ROWS), F32),
            vm((2, 8, ROWS), F32),
            vm((8, OWN), F32),
            vm((2, 8, 128), F32),
            vm((4, 4, 16, 512), F32),
            vm((256, 512), BF),
            vm((2 * EX_DEV * 8, 512), BF),
            vm((8, 384), F32),
            vm((8, 384), F32),
            vm((8, 8, 384), F32),
            dma((4,)), dma((steps,)), dma((steps,)), dma,
        ] + [dma] * 10 + [pltpu.SemaphoreType.REGULAR] + [dma] * 12,
        compiler_params=pltpu.CompilerParams(
            collective_id=0, has_side_effects=True, vmem_limit_bytes=60 * 1024 * 1024
        ),
    )(
        latent,
        adapter_down_matrix,
        output_gradient_rows,
        output_sketch_factor,
        rank_sketch_factor,
        token_example_index.reshape(steps, 1, STEP),
        validation_sketches,
    )


def solution(mesh):
    in_specs = (P("dp", None), P(), P("dp", "col"), P("col", None), P(), P("dp"), P("dp", "col"))
    out_specs = P("dp", None)
    return jax.shard_map(
        on_device, mesh=mesh, in_specs=in_specs, out_specs=out_specs, check_vma=False
    )
```

```python
import functools
import math

import jax
import jax.numpy as jnp
from jax import lax
from jax.experimental import pallas as pl
from jax.experimental.pallas import tpu as pltpu
from jax.sharding import PartitionSpec as P

PA = 128
PB = 64
EX_DEV = 8
MESH = pl.DeviceIdType.MESH

epsilon = 1e-06

BF = jnp.bfloat16
F32 = jnp.float32

STEP = 512
OWN = EX_DEV * PB
ROWS = OWN + 2 * PB

FAR_FIRST = ((4, 0), (4, 1), (2, 0), (2, 1), (6, 0), (6, 1), (0, 1))


def nt(x, y):
    return lax.dot_general(x, y, (((1,), (1,)), ((), ())), preferred_element_type=F32)


def kernel(
    lat_h, down_h, grad_h, sketch_h, rank_h, seg_h, val_h, out_ref,
    lat, down, grad, sketch, rank, seg, masked, side, gp, gt,
    r0, a0, r1, a1, r2, r3, vg, vb, spread_ref, fin, rz, fb, local_sem, lat_sem, grad_sem, vown_sem,
    s0_send, s0_far, s0_near, s1_send, s1_far, s1_near, s2_send, s2_recv, s3_send, s3_recv,
    ready, vz_send, vz_recv, vo_send, vo_recv, vx_send, vx_recv, vd_send, vd_recv, fz_send, fz_recv, fb_send, fb_recv,
):
    i = lax.axis_index("dp")
    c = lax.axis_index("col")
    zl, x = i // 4, i % 4
    zh, y, core = c // 8, (c // 2) % 4, c % 2
    p = c % 8
    below, above = (i + 15) % 16, (i + 1) % 16

    def at(dp, col):
        return {"dp": dp, "col": col}

    core_peer = at(i, zh * 8 + y * 2 + (1 - core))
    y_peer = [at(i, zh * 8 + ((y + k) % 4) * 2 + core) for k in (2, 1, 3)]
    z_peer = at(i, (1 - zh) * 8 + p)
    p_peer = [at(i, zh * 8 + (p // 2 * 2 + k) % 8 + (core + j) % 2) for k, j in FAR_FIRST]
    vz_peer = [at(((zl + k) % 4) * 4 + x, c) for k in (2, 1, 3)]
    vd_peer = [at(((zl + k) % 4) * 4 + (x + 2) % 4, c) for k in (2, 1, 3)]
    vo_peer = [at(zl * 4 + (x + k) % 4, c) for k in (2, 1, 3)]
    vx_peer = [at(zl * 4 + (x + k) % 4, c) for k in (1, 3)]
    z_col = (1 - zh) * 8 + p

    tokens = grad.shape[0]
    first = i * EX_DEV - 1

    steps = tokens // STEP
    small = [
        pltpu.make_async_copy(src, dst, local_sem.at[n])
        for n, (src, dst) in enumerate(
            ((down_h, down), (rank_h, rank), (seg_h, seg), (sketch_h, sketch))
        )
    ]

    def block(n):
        return pl.ds(pl.multiple_of(n * STEP, STEP), STEP)

    def lat_copy(n):
        return pltpu.make_async_copy(lat_h.at[block(n), :], lat.at[block(n), :], lat_sem.at[n])

    def grad_copy(n):
        return pltpu.make_async_copy(grad_h.at[block(n), :], grad.at[block(n), :], grad_sem.at[n])

    for cp in small[:3]:
        cp.start()
    lat_copy(0).start()
    small[3].start()
    grad_copy(0).start()
    lat_copy(1).start()
    grad_copy(1).start()
    vown = pltpu.make_async_copy(val_h, vg.at[0, x], vown_sem)
    vown.start()
    barrier = pltpu.get_barrier_semaphore()
    near = p_peer + vz_peer + vo_peer + vd_peer + [at(above, c)]
    far = [z_peer, at(above, z_col)]
    for peer in near:
        pl.semaphore_signal(barrier, inc=1, device_id=peer, device_id_type=MESH)

    @pl.when(zh == 0)
    def _():
        for peer in far + [at(below, z_col)]:
            pl.semaphore_signal(barrier, inc=1, device_id=peer, device_id_type=MESH)

    def remote(src, dst, send, recv, peer):
        return pltpu.make_async_remote_copy(
            src_ref=src, dst_ref=dst, send_sem=send, recv_sem=recv,
            device_id=peer, device_id_type=MESH,
        )

    def drain(ref, sem):
        pltpu.make_async_copy(ref, ref, sem).wait()

    def v_begin():
        for k, peer in zip((2, 1, 3), vz_peer):
            remote(val_h, vg.at[4 - k, x], vz_send, vz_recv, peer).start()
        for peer in vo_peer:
            remote(val_h, vg.at[0, x], vo_send, vo_recv, peer).start()
        for k, peer in zip((2, 1, 3), vd_peer):
            remote(val_h, vg.at[4 - k, x], vd_send, vd_recv, peer).start()

    def v_turn():
        drain(vg.at[0, 0:3], vz_recv)
        for peer in vx_peer:
            remote(vg.at[1:4, x], vg.at[1:4, x], vx_send, vx_recv, peer).start()

    gp[...] = jnp.zeros_like(gp)
    side[steps - 1] = jnp.zeros((STEP, PA), BF)
    masked[steps - 1] = jnp.zeros((OWN + PB, STEP), BF)
    for cp in small:
        cp.wait()

    def project(n):
        part = jnp.dot(masked[n], side[n], preferred_element_type=F32)
        gp[0:OWN, :] += part[0:OWN]
        gp[OWN + PB : ROWS, :] += part[OWN:]

    early = jnp.where(x + y < 3, 1, 0)

    def local_step(n, carry):
        lat_copy(n).wait()
        grad_copy(n).wait()

        @pl.when(n < steps - 2)
        def _():
            lat_copy(n + 2).start()
            grad_copy(n + 2).start()

        hidden = nt(lat[block(n), :], down[...]).astype(BF)
        out_side = jnp.dot(grad[block(n), :], sketch[...], preferred_element_type=F32)
        rank_side = lax.dot_general(
            rank[...], hidden, (((0,), (1,)), ((), ())), preferred_element_type=F32
        ).astype(BF).astype(F32)
        project(lax.rem(n + steps - 1, steps))
        ids = seg[n] - first
        for e in range(1, EX_DEV + 1):
            masked[n, (e - 1) * PB : e * PB, :] = jnp.where(ids == e, rank_side, 0.0).astype(BF)
        masked[n, OWN : OWN + PB, :] = jnp.where(ids == 0, rank_side, 0.0).astype(BF)
        side[n] = out_side.astype(BF)

        @pl.when((zh == 1) & (n == early))
        def _():
            pl.semaphore_wait(barrier, len(near) + len(far) + 1)
            v_begin()
            for peer in far:
                pl.semaphore_signal(ready, inc=1, device_id=peer, device_id_type=MESH)

        return carry

    lax.fori_loop(0, steps, local_step, 0)
    project(steps - 1)

    for t in range(ROWS // 128):
        piece = gp[t * 128 : (t + 1) * 128, :].T
        gt[:, :, :, :, t * 128 : (t + 1) * 128] = piece.reshape(2, 4, 2, 8, 128)

    @pl.when(zh == 0)
    def _():
        pl.semaphore_wait(barrier, len(near))

    c0 = [
        remote(gt.at[z, :, 1 - core], r0.at[z], s0_send, sem, core_peer)
        for z, sem in ((1 - zh, s0_far), (zh, s0_near))
    ]
    for cp in c0:
        cp.start()

    @pl.when(zh == 0)
    def _():
        v_begin()

    for n, (z, sem) in enumerate(((1 - zh, s1_far), (zh, s1_near))):
        c0[n].wait_recv()
        a0[z] = gt[z, :, core] + r0[z]
        for k, peer in zip((2, 1, 3), y_peer):
            remote(a0.at[z, (y + k) % 4], r1.at[n, k - 1], s1_send, sem, peer).start()

    @pl.when(zh == 1)
    def _():
        v_turn()

    drain(r1.at[0], s1_far)
    a1[0] = (a0[1 - zh, y] + r1[0, 0]) + (r1[0, 1] + r1[0, 2])

    @pl.when(zh == 0)
    def _():
        pl.semaphore_wait(ready, len(far))

    remote(a1.at[0, :, OWN:ROWS], r3.at[1], s3_send, s3_recv, at(below, z_col)).start()
    c2 = remote(a1.at[0, :, 0:OWN], r2, s2_send, s2_recv, z_peer)
    c2.start()
    drain(r1.at[1], s1_near)
    a1[1] = (a0[zh, y] + r1[1, 0]) + (r1[1, 1] + r1[1, 2])
    remote(a1.at[1, :, OWN:ROWS], r3.at[0], s3_send, s3_recv, at(below, c)).start()

    @pl.when(zh == 0)
    def _():
        v_turn()

    ones = jnp.ones((16, 512), BF)

    def spread():
        c2.wait_recv()
        drain(r3, s3_recv)
        own = a1[1, :, 0:OWN] + r2[...]
        spill = r3[0] + r3[1]
        own = jnp.concatenate([own[:, : OWN - 128], own[:, OWN - 128 :] + spill], axis=1)
        stack = jnp.concatenate([own[:, e * PB : (e + 1) * PB] for e in range(EX_DEV)], axis=0)
        wide = jnp.concatenate([stack, stack], axis=1)
        wide = jnp.concatenate([wide, wide, wide, wide], axis=1)
        row_a = lax.broadcasted_iota(jnp.int32, (EX_DEV * 8, 512), 0) % 8
        lane_a = lax.broadcasted_iota(jnp.int32, (EX_DEV * 8, 512), 1) // PB
        wide = jnp.where(row_a == lane_a, wide, 0.0)
        hi = wide.astype(BF)
        spread_ref[0 : EX_DEV * 8, :] = hi
        spread_ref[EX_DEV * 8 :, :] = (wide - hi.astype(F32)).astype(BF)
        fin[2:3, 256 : 256 + EX_DEV * 8] = nt(ones, (wide * wide).astype(BF))[0:1]

    fin[:, 256:384] = jnp.zeros((8, 128), F32)

    @pl.when(zh == 1)
    def _():
        spread()

    vown.wait()
    drain(vg.at[0, 0:3], vo_recv)
    drain(vg.at[1:4, 0], vd_recv)
    drain(vg.at[1:4, 0:2], vx_recv)
    val = jnp.concatenate([vg[(z - zl + 4) % 4].reshape(64, 512) for z in range(4)], axis=0)
    val_hi = val.astype(BF)
    vb[...] = val_hi
    vsum = nt(ones, (val * val).astype(BF))
    fin[0:1, 256:384] = vsum[0:1, 0:128]
    fin[1:2, 256:384] = vsum[0:1, 128:256]

    @pl.when(zh == 0)
    def _():
        spread()

    dots = nt(spread_ref[...], vb[...])
    dots = dots[0 : EX_DEV * 8] + dots[EX_DEV * 8 :]
    fin[:, 0:256] = jnp.sum(dots.reshape(EX_DEV, 8, 256), axis=1)

    cz = remote(fin, rz, fz_send, fz_recv, z_peer)
    cz.start()
    for ref, sem in (
        (r0, s0_send), (r1, s1_send), (r2, s2_send), (r3, s3_send),
        (vg.at[0, 0:3], vz_send), (vg.at[0, 0:3], vo_send),
        (vg.at[1:4, 0:2], vx_send), (vg.at[1:4, 0], vd_send),
    ):
        drain(ref, sem)
    cz.wait_recv()
    fb[p] = fin[...] + rz[...]
    cb = [
        remote(fb.at[p], fb.at[p], fb_send, fb_recv, p_peer[k]) for k in range(7)
    ]
    for cp in cb:
        cp.start()
    drain(fb.at[0:7], fb_recv)
    total = ((fb[0] + fb[1]) + (fb[2] + fb[3])) + ((fb[4] + fb[5]) + (fb[6] + fb[7]))
    tail = total[:, 256:384]
    lanes = lax.broadcasted_iota(jnp.int32, (EX_DEV, 128), 1) // 8
    slots = lax.broadcasted_iota(jnp.int32, (EX_DEV, 128), 0)
    own_sq = jnp.sum(jnp.where(lanes == slots, tail[2:3], 0.0), axis=1, keepdims=True)
    own_scale = math.sqrt(PA * PB) * lax.rsqrt(own_sq + epsilon)
    val_scale = lax.rsqrt(tail[0:2] + epsilon)
    out_ref[:, 0:128] = total[:, 0:128] * own_scale * val_scale[0:1]
    out_ref[:, 128:256] = total[:, 128:256] * own_scale * val_scale[1:2]
    drain(rz, fz_send)
    drain(fb.at[0:7], fb_send)


def on_device(
    latent,
    adapter_down_matrix,
    output_gradient_rows,
    output_sketch_factor,
    rank_sketch_factor,
    token_example_index,
    validation_sketches,
):
    tokens, columns = output_gradient_rows.shape
    width = latent.shape[1]
    steps = tokens // STEP
    dma = pltpu.SemaphoreType.DMA
    vm = pltpu.VMEM
    return pl.pallas_call(
        kernel,
        out_shape=vm((EX_DEV, 256), F32),
        in_specs=[pl.BlockSpec(memory_space=pl.ANY)] * 7,
        out_specs=pl.BlockSpec(memory_space=pltpu.VMEM),
        scratch_shapes=[
            vm((tokens, width), BF),
            vm((PB, width), BF),
            vm((tokens, columns), BF),
            vm((columns, PA), BF),
            vm((PB, PB), BF),
            vm((steps, 1, STEP), jnp.int32),
            vm((steps, OWN + PB, STEP), BF),
            vm((steps, STEP, PA), BF),
            vm((ROWS, PA), F32),
            vm((2, 4, 2, 8, ROWS), F32),
            vm((2, 4, 8, ROWS), F32),
            vm((2, 4, 8, ROWS), F32),
            vm((2, 3, 8, ROWS), F32),
            vm((2, 8, ROWS), F32),
            vm((8, OWN), F32),
            vm((2, 8, 128), F32),
            vm((4, 4, 16, 512), F32),
            vm((256, 512), BF),
            vm((2 * EX_DEV * 8, 512), BF),
            vm((8, 384), F32),
            vm((8, 384), F32),
            vm((8, 8, 384), F32),
            dma((4,)), dma((steps,)), dma((steps,)), dma,
        ] + [dma] * 10 + [pltpu.SemaphoreType.REGULAR] + [dma] * 12,
        compiler_params=pltpu.CompilerParams(
            collective_id=0, has_side_effects=True, vmem_limit_bytes=60 * 1024 * 1024
        ),
    )(
        latent,
        adapter_down_matrix,
        output_gradient_rows,
        output_sketch_factor,
        rank_sketch_factor,
        token_example_index.reshape(steps, 1, STEP),
        validation_sketches,
    )


def solution(mesh):
    in_specs = (P("dp", None), P(), P("dp", "col"), P("col", None), P(), P("dp"), P("dp", "col"))
    out_specs = P("dp", None)
    return jax.shard_map(
        on_device, mesh=mesh, in_specs=in_specs, out_specs=out_specs, check_vma=False
    )
```

```python
import functools
import math

import jax
import jax.numpy as jnp
from jax import lax
from jax.experimental import pallas as pl
from jax.experimental.pallas import tpu as pltpu
from jax.sharding import PartitionSpec as P

PA = 128
PB = 64
EX_DEV = 8
MESH = pl.DeviceIdType.MESH

epsilon = 1e-06

BF = jnp.bfloat16
F32 = jnp.float32

STEP = 512
OWN = EX_DEV * PB
ROWS = OWN + 2 * PB

FAR_FIRST = ((4, 0), (4, 1), (2, 0), (2, 1), (6, 0), (6, 1), (0, 1))


def nt(x, y):
    return lax.dot_general(x, y, (((1,), (1,)), ((), ())), preferred_element_type=F32)


def kernel(
    lat_h, down_h, grad_h, sketch_h, rank_h, seg_h, val_h, out_ref,
    lat, down, grad, sketch, rank, seg, masked, side, gp, gt,
    r0, a0, r1, a1, r2, r3, vg, vb, spread_ref, fin, rz, fb, local_sem, lat_sem, grad_sem, vown_sem,
    s0_send, s0_far, s0_near, s1_send, s1_far, s1_near, s2_send, s2_recv, s3_send, s3_recv,
    ready, vz_send, vz_recv, vo_send, vo_recv, vx_send, vx_recv, vd_send, vd_recv, fz_send, fz_recv, fb_send, fb_recv,
):
    i = lax.axis_index("dp")
    c = lax.axis_index("col")
    zl, x = i // 4, i % 4
    zh, y, core = c // 8, (c // 2) % 4, c % 2
    p = c % 8
    below, above = (i + 15) % 16, (i + 1) % 16

    def at(dp, col):
        return {"dp": dp, "col": col}

    core_peer = at(i, zh * 8 + y * 2 + (1 - core))
    y_peer = [at(i, zh * 8 + ((y + k) % 4) * 2 + core) for k in (2, 1, 3)]
    z_peer = at(i, (1 - zh) * 8 + p)
    p_peer = [at(i, zh * 8 + (p // 2 * 2 + k) % 8 + (core + j) % 2) for k, j in FAR_FIRST]
    vz_peer = [at(((zl + k) % 4) * 4 + x, c) for k in (2, 1, 3)]
    vd_peer = [at(((zl + k) % 4) * 4 + (x + 2) % 4, c) for k in (2, 1, 3)]
    vo_peer = [at(zl * 4 + (x + k) % 4, c) for k in (2, 1, 3)]
    vx_peer = [at(zl * 4 + (x + k) % 4, c) for k in (1, 3)]
    z_col = (1 - zh) * 8 + p

    tokens = grad.shape[0]
    first = i * EX_DEV - 1

    steps = tokens // STEP
    small = [
        pltpu.make_async_copy(src, dst, local_sem.at[n])
        for n, (src, dst) in enumerate(
            ((down_h, down), (rank_h, rank), (seg_h, seg), (sketch_h, sketch))
        )
    ]

    def block(n):
        return pl.ds(pl.multiple_of(n * STEP, STEP), STEP)

    def lat_copy(n):
        return pltpu.make_async_copy(lat_h.at[block(n), :], lat.at[block(n), :], lat_sem.at[n])

    def grad_copy(n):
        return pltpu.make_async_copy(grad_h.at[block(n), :], grad.at[block(n), :], grad_sem.at[n])

    for cp in small[:3]:
        cp.start()
    lat_copy(0).start()
    small[3].start()
    grad_copy(0).start()
    lat_copy(1).start()
    grad_copy(1).start()
    vown = pltpu.make_async_copy(val_h, vg.at[0, x], vown_sem)
    vown.start()
    barrier = pltpu.get_barrier_semaphore()
    near = p_peer + vz_peer + vo_peer + vd_peer + [at(above, c)]
    far = [z_peer, at(above, z_col)]
    for peer in near:
        pl.semaphore_signal(barrier, inc=1, device_id=peer, device_id_type=MESH)

    @pl.when(zh == 0)
    def _():
        for peer in far + [at(below, z_col)]:
            pl.semaphore_signal(barrier, inc=1, device_id=peer, device_id_type=MESH)

    def remote(src, dst, send, recv, peer):
        return pltpu.make_async_remote_copy(
            src_ref=src, dst_ref=dst, send_sem=send, recv_sem=recv,
            device_id=peer, device_id_type=MESH,
        )

    def drain(ref, sem):
        pltpu.make_async_copy(ref, ref, sem).wait()

    def v_begin():
        for k, peer in zip((2, 1, 3), vz_peer):
            remote(val_h, vg.at[4 - k, x], vz_send, vz_recv, peer).start()
        for peer in vo_peer:
            remote(val_h, vg.at[0, x], vo_send, vo_recv, peer).start()
        for k, peer in zip((2, 1, 3), vd_peer):
            remote(val_h, vg.at[4 - k, x], vd_send, vd_recv, peer).start()

    def v_turn():
        drain(vg.at[0, 0:3], vz_recv)
        for peer in vx_peer:
            remote(vg.at[1:4, x], vg.at[1:4, x], vx_send, vx_recv, peer).start()

    gp[...] = jnp.zeros_like(gp)
    side[steps - 1] = jnp.zeros((STEP, PA), BF)
    masked[steps - 1] = jnp.zeros((OWN + PB, STEP), BF)
    for cp in small:
        cp.wait()

    def project(n):
        part = jnp.dot(masked[n], side[n], preferred_element_type=F32)
        gp[0:OWN, :] += part[0:OWN]
        gp[OWN + PB : ROWS, :] += part[OWN:]

    def local_step(n, carry):
        lat_copy(n).wait()
        grad_copy(n).wait()

        @pl.when(n < steps - 2)
        def _():
            lat_copy(n + 2).start()
            grad_copy(n + 2).start()

        hidden = nt(lat[block(n), :], down[...]).astype(BF)
        out_side = jnp.dot(grad[block(n), :], sketch[...], preferred_element_type=F32)
        rank_side = lax.dot_general(
            rank[...], hidden, (((0,), (1,)), ((), ())), preferred_element_type=F32
        ).astype(BF).astype(F32)
        project(lax.rem(n + steps - 1, steps))
        ids = seg[n] - first
        for e in range(1, EX_DEV + 1):
            masked[n, (e - 1) * PB : e * PB, :] = jnp.where(ids == e, rank_side, 0.0).astype(BF)
        masked[n, OWN : OWN + PB, :] = jnp.where(ids == 0, rank_side, 0.0).astype(BF)
        side[n] = out_side.astype(BF)

        @pl.when((zh == 1) & (n == 0))
        def _():
            pl.semaphore_wait(barrier, len(near) + len(far) + 1)
            v_begin()
            for peer in far:
                pl.semaphore_signal(ready, inc=1, device_id=peer, device_id_type=MESH)

        return carry

    lax.fori_loop(0, steps, local_step, 0)
    part = jnp.dot(masked[steps - 1], side[steps - 1], preferred_element_type=F32)
    for t in range(OWN // 128):
        span = slice(t * 128, (t + 1) * 128)
        gt[:, :, :, :, span] = (gp[span, :] + part[span]).T.reshape(2, 4, 2, 8, 128)
    spill = gp[OWN + PB : ROWS, :] + part[OWN:]
    spill = jnp.concatenate([jnp.zeros((PB, PA), F32), spill], axis=0)
    gt[:, :, :, :, OWN:ROWS] = spill.T.reshape(2, 4, 2, 8, 128)

    @pl.when(zh == 0)
    def _():
        pl.semaphore_wait(barrier, len(near))

    c0 = [
        remote(gt.at[z, :, 1 - core], r0.at[z], s0_send, sem, core_peer)
        for z, sem in ((1 - zh, s0_far), (zh, s0_near))
    ]
    for cp in c0:
        cp.start()

    @pl.when(zh == 0)
    def _():
        v_begin()

    for n, (z, sem) in enumerate(((1 - zh, s1_far), (zh, s1_near))):
        c0[n].wait_recv()
        a0[z] = gt[z, :, core] + r0[z]
        for k, peer in zip((2, 1, 3), y_peer):
            remote(a0.at[z, (y + k) % 4], r1.at[n, k - 1], s1_send, sem, peer).start()

    @pl.when(zh == 1)
    def _():
        v_turn()

    drain(r1.at[0], s1_far)
    a1[0] = (a0[1 - zh, y] + r1[0, 0]) + (r1[0, 1] + r1[0, 2])

    @pl.when(zh == 0)
    def _():
        pl.semaphore_wait(ready, len(far))

    remote(a1.at[0, :, OWN:ROWS], r3.at[1], s3_send, s3_recv, at(below, z_col)).start()
    c2 = remote(a1.at[0, :, 0:OWN], r2, s2_send, s2_recv, z_peer)
    c2.start()
    drain(r1.at[1], s1_near)
    a1[1] = (a0[zh, y] + r1[1, 0]) + (r1[1, 1] + r1[1, 2])
    remote(a1.at[1, :, OWN:ROWS], r3.at[0], s3_send, s3_recv, at(below, c)).start()

    @pl.when(zh == 0)
    def _():
        v_turn()

    ones = jnp.ones((16, 512), BF)

    def spread():
        c2.wait_recv()
        drain(r3, s3_recv)
        own = a1[1, :, 0:OWN] + r2[...]
        spill = r3[0] + r3[1]
        own = jnp.concatenate([own[:, : OWN - 128], own[:, OWN - 128 :] + spill], axis=1)
        stack = jnp.concatenate([own[:, e * PB : (e + 1) * PB] for e in range(EX_DEV)], axis=0)
        wide = jnp.concatenate([stack, stack], axis=1)
        wide = jnp.concatenate([wide, wide, wide, wide], axis=1)
        row_a = lax.broadcasted_iota(jnp.int32, (EX_DEV * 8, 512), 0) % 8
        lane_a = lax.broadcasted_iota(jnp.int32, (EX_DEV * 8, 512), 1) // PB
        wide = jnp.where(row_a == lane_a, wide, 0.0)
        hi = wide.astype(BF)
        spread_ref[0 : EX_DEV * 8, :] = hi
        spread_ref[EX_DEV * 8 :, :] = (wide - hi.astype(F32)).astype(BF)
        fin[2:3, 256 : 256 + EX_DEV * 8] = nt(ones, (wide * wide).astype(BF))[0:1]

    fin[:, 256:384] = jnp.zeros((8, 128), F32)

    @pl.when(zh == 1)
    def _():
        spread()

    vown.wait()
    drain(vg.at[0, 0:3], vo_recv)
    drain(vg.at[1:4, 0], vd_recv)
    drain(vg.at[1:4, 0:2], vx_recv)
    val = jnp.concatenate([vg[(z - zl + 4) % 4].reshape(64, 512) for z in range(4)], axis=0)
    val_hi = val.astype(BF)
    vb[...] = val_hi
    vsum = nt(ones, (val * val).astype(BF))
    fin[0:1, 256:384] = vsum[0:1, 0:128]
    fin[1:2, 256:384] = vsum[0:1, 128:256]

    @pl.when(zh == 0)
    def _():
        spread()

    dots = nt(spread_ref[...], vb[...])
    dots = dots[0 : EX_DEV * 8] + dots[EX_DEV * 8 :]
    fin[:, 0:256] = jnp.sum(dots.reshape(EX_DEV, 8, 256), axis=1)

    cz = remote(fin, rz, fz_send, fz_recv, z_peer)
    cz.start()
    for ref, sem in (
        (r0, s0_send), (r1, s1_send), (r2, s2_send), (r3, s3_send),
        (vg.at[0, 0:3], vz_send), (vg.at[0, 0:3], vo_send),
        (vg.at[1:4, 0:2], vx_send), (vg.at[1:4, 0], vd_send),
    ):
        drain(ref, sem)
    cz.wait_recv()
    fb[p] = fin[...] + rz[...]
    cb = [
        remote(fb.at[p], fb.at[p], fb_send, fb_recv, p_peer[k]) for k in range(7)
    ]
    for cp in cb:
        cp.start()
    drain(fb.at[0:7], fb_recv)
    total = ((fb[0] + fb[1]) + (fb[2] + fb[3])) + ((fb[4] + fb[5]) + (fb[6] + fb[7]))
    tail = total[:, 256:384]
    lanes = lax.broadcasted_iota(jnp.int32, (EX_DEV, 128), 1) // 8
    slots = lax.broadcasted_iota(jnp.int32, (EX_DEV, 128), 0)
    own_sq = jnp.sum(jnp.where(lanes == slots, tail[2:3], 0.0), axis=1, keepdims=True)
    own_scale = math.sqrt(PA * PB) * lax.rsqrt(own_sq + epsilon)
    val_scale = lax.rsqrt(tail[0:2] + epsilon)
    out_ref[:, 0:128] = total[:, 0:128] * own_scale * val_scale[0:1]
    out_ref[:, 128:256] = total[:, 128:256] * own_scale * val_scale[1:2]
    drain(rz, fz_send)
    drain(fb.at[0:7], fb_send)


def on_device(
    latent,
    adapter_down_matrix,
    output_gradient_rows,
    output_sketch_factor,
    rank_sketch_factor,
    token_example_index,
    validation_sketches,
):
    tokens, columns = output_gradient_rows.shape
    width = latent.shape[1]
    steps = tokens // STEP
    dma = pltpu.SemaphoreType.DMA
    vm = pltpu.VMEM
    return pl.pallas_call(
        kernel,
        out_shape=vm((EX_DEV, 256), F32),
        in_specs=[pl.BlockSpec(memory_space=pl.ANY)] * 7,
        out_specs=pl.BlockSpec(memory_space=pltpu.VMEM),
        scratch_shapes=[
            vm((tokens, width), BF),
            vm((PB, width), BF),
            vm((tokens, columns), BF),
            vm((columns, PA), BF),
            vm((PB, PB), BF),
            vm((steps, 1, STEP), jnp.int32),
            vm((steps, OWN + PB, STEP), BF),
            vm((steps, STEP, PA), BF),
            vm((ROWS, PA), F32),
            vm((2, 4, 2, 8, ROWS), F32),
            vm((2, 4, 8, ROWS), F32),
            vm((2, 4, 8, ROWS), F32),
            vm((2, 3, 8, ROWS), F32),
            vm((2, 8, ROWS), F32),
            vm((8, OWN), F32),
            vm((2, 8, 128), F32),
            vm((4, 4, 16, 512), F32),
            vm((256, 512), BF),
            vm((2 * EX_DEV * 8, 512), BF),
            vm((8, 384), F32),
            vm((8, 384), F32),
            vm((8, 8, 384), F32),
            dma((4,)), dma((steps,)), dma((steps,)), dma,
        ] + [dma] * 10 + [pltpu.SemaphoreType.REGULAR] + [dma] * 12,
        compiler_params=pltpu.CompilerParams(
            collective_id=0, has_side_effects=True, vmem_limit_bytes=60 * 1024 * 1024
        ),
    )(
        latent,
        adapter_down_matrix,
        output_gradient_rows,
        output_sketch_factor,
        rank_sketch_factor,
        token_example_index.reshape(steps, 1, STEP),
        validation_sketches,
    )


def solution(mesh):
    in_specs = (P("dp", None), P(), P("dp", "col"), P("col", None), P(), P("dp"), P("dp", "col"))
    out_specs = P("dp", None)
    return jax.shard_map(
        on_device, mesh=mesh, in_specs=in_specs, out_specs=out_specs, check_vma=False
    )
```
